32 devices in a mesh: groups: 2 (over x), row: 16 (over z, y, core).
Axes of the slice: x: 2, y: 2, z: 4, core: 2. Of those that a mesh axis runs over, the one named last changes fastest.
Arguments:
- pair_rep: bfloat16 [128, 64, 128], P(('groups', 'row')), parts along dimension 0, may hold values from -6 to 6
- pair_mask: int32 [128, 64], P(('groups', 'row')), parts along dimension 0, may hold values 0 or 1
- proj_weight: bfloat16 [2, 128, 256], replicated, may hold values from -0.5 to 0.5
- gate_weight: bfloat16 [2, 128, 128], replicated, may hold values from -0.5 to 0.5
- out_weight: bfloat16 [2, 64, 128], replicated, may hold values from -0.75 to 0.75
- norm_gain: float32 [2, 128], replicated, may hold values from 0.1 to 1.9
- mid_gain: float32 [2, 64], replicated, may hold values from 0.1 to 1.9
Outputs:
- pair_out: bfloat16 [128, 64, 128], P(('groups', 'row')), parts along dimension 0
The draws below stay inside these ranges and needn't reach their ends.
There are 2 independent parts, one for each index of `groups`. The reference program is written for one: setup_inputs(seed, part) draws one part's arguments, and reference() takes and returns one part's arrays. A program takes and returns all parts, laid end to end along the dimension named above; an argument that names none is the same for every part. Nothing has to cross between parts.
All inputs are finite; a program needn't handle non-finite values. No bound on the sum of `pair_mask` on one device may be relied on, other than what follows from the above.
Results may differ from the reference program's by a relative error of at most 0.013.
Values may be sent and summed in bfloat16 or wider, within the bound.
No kernel may reach another device: no remote copies, remote signals or barrier semaphores. Data moves between devices by JAX's collectives and lax.ppermute only.
A program may use at most 192 MiB of HBM per device.

```python
import jax
import jax.numpy as jnp
from jax import lax

C = 128
HW = 64
N = 64


def with_ends(values, stream_key, smallest, high):
    longest = values.shape.index(max(values.shape))
    spots = []
    for shift in (0, 1):
        where = [jax.random.randint(jax.random.fold_in(stream_key, axis), (), 0, length) for axis, length in enumerate(values.shape)]
        where[longest] = (where[longest] + shift) % values.shape[longest]
        spots.append(tuple(where))
    return values.at[spots[0]].set(smallest).at[spots[1]].set(high)


def block_levels(key, extent, pieces, smallest, top_value):
    factor_of, own = 1.0, jax.random.fold_in(key, 6)
    for dim, shards_of in pieces:
        heights = jnp.exp(jax.random.uniform(jax.random.fold_in(own, dim), (shards_of,), jnp.float32, smallest / len(pieces), top_value / len(pieces)))
        factor_of = factor_of * jnp.repeat(heights, extent[dim] // shards_of).reshape([-1 if axis == dim else 1 for axis in range(len(extent))])
    return factor_of


def gaussian(rng, shape, scale, limit, split=(), held_as=jnp.bfloat16):
    level = block_levels(rng, shape, split, -0.22, 0.18) if split else 1.0
    values = jax.random.normal(rng, shape, jnp.float32) * scale * level
    return jnp.minimum(jnp.maximum(values, -limit), limit).astype(held_as)


def setup_inputs(seed: int = 0, part: int = 0) -> dict:
    splits = jax.random.split(jax.random.key(seed), 8)
    part_splits = jax.random.split(jax.random.fold_in(splits[7], part), 8)
    return {
        "pair_rep": gaussian(part_splits[0], (N, N, C), 1.0, 6.0, ((0, 16),)),
        "pair_mask": with_ends((jax.random.randint(part_splits[1], (N, N), 0, 8) < 7).astype(jnp.int32), jax.random.fold_in(part_splits[1], 1), 0, 1),
        "proj_weight": gaussian(splits[2], (2, C, 4 * HW), C ** -0.5, 0.5),
        "gate_weight": gaussian(splits[3], (2, C, C), C ** -0.5, 0.5),
        "out_weight": gaussian(splits[4], (2, HW, C), HW ** -0.5, 0.75),
        "norm_gain": jnp.clip(1.0 + 0.18 * jax.random.normal(splits[5], (2, C), jnp.float32), 0.1, 1.9),
        "mid_gain": jnp.clip(1.0 + 0.18 * jax.random.normal(splits[6], (2, HW), jnp.float32), 0.1, 1.9),
    }


small_eps = 1e-05

def layer_norm(values, gain, axis, epsilon):
    average = lax.optimization_barrier(jnp.mean(values, axis=axis, keepdims=True))
    centred = values - average
    variance = lax.optimization_barrier(jnp.mean(centred * centred, axis=axis, keepdims=True))
    return centred * lax.rsqrt(variance + epsilon) * gain

def update_half(pair_now, pair_mask, proj_one, gate_one, out_one, gain_one, mid_one, orient):
    floats = pair_now.astype(jnp.float32)
    normed = layer_norm(floats, gain_one, -1, small_eps).astype(jnp.bfloat16)
    projected = jnp.einsum('ijd,de->eij', normed.astype(jnp.float32), proj_one.astype(jnp.float32))
    weight_mask = pair_mask.astype(jnp.float32)[None]
    factor_left = (weight_mask * jax.nn.sigmoid(projected[HW:2 * HW]) * projected[:HW]).astype(jnp.bfloat16)
    factor_right = (weight_mask * jax.nn.sigmoid(projected[3 * HW:]) * projected[2 * HW:3 * HW]).astype(jnp.bfloat16)
    if orient == 0:
        summed = jnp.einsum('cik,cjk->cij', factor_left.astype(jnp.float32), factor_right.astype(jnp.float32))
    else:
        summed = jnp.einsum('cki,ckj->cij', factor_left.astype(jnp.float32), factor_right.astype(jnp.float32))
    hidden = layer_norm(summed, mid_one[:, None, None], 0, small_eps).astype(jnp.bfloat16)
    gating = jax.nn.sigmoid(jnp.einsum('ijd,de->ije', normed.astype(jnp.float32), gate_one.astype(jnp.float32)))
    update = jnp.einsum('cij,cd->ijd', hidden.astype(jnp.float32), out_one.astype(jnp.float32))
    return (floats + gating * update).astype(jnp.bfloat16)

def reference(pair_rep, pair_mask, proj_weight, gate_weight, out_weight, norm_gain, mid_gain):
    current = pair_rep
    for orient in range(2):
        current = update_half(current, pair_mask, proj_weight[orient], gate_weight[orient], out_weight[orient], norm_gain[orient], mid_gain[orient], orient)
    return current
```

```python
import jax
import jax.numpy as jnp
from jax import lax
from jax.sharding import PartitionSpec as P

EPS = 1e-05


def layer_norm(values, gain, axis):
    average = jnp.mean(values, axis=axis, keepdims=True)
    centred = values - average
    variance = jnp.mean(centred * centred, axis=axis, keepdims=True)
    return centred * lax.rsqrt(variance + EPS) * gain


def factors(normed, mask, proj):
    hw = proj.shape[1] // 4
    projected = jnp.einsum("ijd,de->eij", normed, proj, preferred_element_type=jnp.float32)
    left = mask * jax.nn.sigmoid(projected[hw : 2 * hw]) * projected[:hw]
    right = mask * jax.nn.sigmoid(projected[3 * hw :]) * projected[2 * hw : 3 * hw]
    return left.astype(jnp.bfloat16), right.astype(jnp.bfloat16)


def gather_rows(factor):
    c, rows, k = factor.shape
    half = rows // 2
    packed = jnp.concatenate([factor[:, :half], factor[:, half:]], axis=-1).transpose(1, 0, 2)
    everywhere = lax.all_gather(packed, "row", axis=0, tiled=False)
    n = everywhere.shape[0]
    both = jnp.stack([everywhere[..., :k], everywhere[..., k:]], axis=1)
    return both.reshape(n * rows, c, k).transpose(1, 0, 2)


def finish(floats, normed, summed, gate, out, mid):
    hidden = layer_norm(summed, mid[:, None, None], 0).astype(jnp.bfloat16)
    gating = jax.nn.sigmoid(
        jnp.einsum("ijd,de->ije", normed, gate, preferred_element_type=jnp.float32)
    )
    update = jnp.einsum("cij,cd->ijd", hidden, out, preferred_element_type=jnp.float32)
    return (floats + gating * update).astype(jnp.bfloat16)


def shards(pair_rep, pair_mask, proj_weight, gate_weight, out_weight, norm_gain, mid_gain):
    mask = pair_mask.astype(jnp.float32)[None]
    rows, tokens = pair_mask.shape
    devices = tokens // rows

    floats = pair_rep.astype(jnp.float32)
    normed = layer_norm(floats, norm_gain[0], -1).astype(jnp.bfloat16)
    left, right = factors(normed, mask, proj_weight[0])
    summed = jnp.einsum("cik,cjk->cij", left, gather_rows(right), preferred_element_type=jnp.float32)
    current = finish(floats, normed, summed, gate_weight[0], out_weight[0], mid_gain[0])

    floats = current.astype(jnp.float32)
    normed = layer_norm(floats, norm_gain[1], -1).astype(jnp.bfloat16)
    left, right = factors(normed, mask, proj_weight[1])
    c = left.shape[0]
    blocks = left.reshape(c, rows, devices, rows).transpose(2, 1, 3, 0)
    blocks = blocks.reshape(devices, rows * rows * c // 128, 128)
    columns = lax.all_to_all(blocks, "row", 0, 0, tiled=True)
    columns = columns.reshape(devices * rows, rows, c).transpose(2, 0, 1)
    summed = jnp.einsum(
        "cki,ckj->cij", columns, gather_rows(right), preferred_element_type=jnp.float32
    )
    return finish(floats, normed, summed, gate_weight[1], out_weight[1], mid_gain[1])


def solution(mesh):
    return jax.shard_map(
        shards,
        mesh=mesh,
        in_specs=(P(("groups", "row")), P(("groups", "row")), P(), P(), P(), P(), P()),
        out_specs=P(("groups", "row")),
        check_vma=False,
    )
```

```python
import jax
import jax.numpy as jnp
from jax import lax
from jax.sharding import PartitionSpec as P

EPS = 1e-05


def layer_norm(values, gain, axis):
    average = jnp.mean(values, axis=axis, keepdims=True)
    centred = values - average
    variance = jnp.mean(centred * centred, axis=axis, keepdims=True)
    return centred * lax.rsqrt(variance + EPS) * gain


def by_device(proj, devices):
    d = proj.shape[0]
    grouped = proj.reshape(d, 2, 2, devices, -1).transpose(2, 0, 3, 1, 4)
    return grouped.reshape(2, d, -1)


def triangle(pair, mask, proj, gate, out, gain, mid, orient):
    rows, tokens, _ = pair.shape
    devices = tokens // rows
    hw = out.shape[0]
    floats = pair.astype(jnp.float32)
    normed = layer_norm(floats, gain, -1).astype(jnp.bfloat16)
    flat = normed.reshape(rows * tokens, -1)
    weights = by_device(proj, devices)
    value = jnp.einsum("pd,de->ep", flat, weights[0], preferred_element_type=jnp.float32)
    gates = jnp.einsum("pd,de->ep", flat, weights[1], preferred_element_type=jnp.float32)
    factor = (mask * jax.nn.sigmoid(gates) * value).astype(jnp.bfloat16)
    factor = lax.all_to_all(factor.reshape(devices, -1, rows * tokens), "row", 0, 0, tiled=True)
    c = hw // devices
    factor = factor.reshape(devices, 2, c, rows, tokens).transpose(1, 2, 0, 3, 4)
    left, right = factor.reshape(2, c, tokens, tokens)
    spec = "cik,cjk->cij" if orient == 0 else "cki,ckj->cij"
    summed = jnp.einsum(spec, left, right, preferred_element_type=jnp.float32)
    summed = summed.astype(jnp.bfloat16).reshape(c, devices, rows * tokens).transpose(1, 0, 2)
    summed = lax.all_to_all(summed, "row", 0, 0, tiled=True)
    summed = summed.reshape(hw, rows * tokens).astype(jnp.float32)
    hidden = layer_norm(summed, mid[:, None], 0).astype(jnp.bfloat16)
    gating = jax.nn.sigmoid(jnp.dot(flat, gate, preferred_element_type=jnp.float32))
    update = jnp.einsum("cp,cd->pd", hidden, out, preferred_element_type=jnp.float32)
    return (floats + (gating * update).reshape(pair.shape)).astype(jnp.bfloat16)


def factors(normed, mask, proj):
    hw = proj.shape[1] // 4
    projected = jnp.einsum("ijd,de->eij", normed, proj, preferred_element_type=jnp.float32)
    left = mask * jax.nn.sigmoid(projected[hw : 2 * hw]) * projected[:hw]
    right = mask * jax.nn.sigmoid(projected[3 * hw :]) * projected[2 * hw : 3 * hw]
    return left.astype(jnp.bfloat16), right.astype(jnp.bfloat16)


def triangle_gathered(pair, mask, proj, gate, out, gain, mid, orient):
    rows, tokens, _ = pair.shape
    devices = tokens // rows
    floats = pair.astype(jnp.float32)
    normed = layer_norm(floats, gain, -1).astype(jnp.bfloat16)
    left, right = factors(normed, mask.reshape(1, rows, tokens), proj)
    everywhere = lax.all_gather(right, "row", axis=1, tiled=True)
    if orient == 1:
        c = left.shape[0]
        blocks = left.reshape(c, rows, devices, rows).transpose(2, 1, 3, 0)
        left = lax.all_to_all(blocks, "row", 0, 0, tiled=True)
        left = left.reshape(tokens, rows, c).transpose(2, 0, 1)
    spec = "cik,cjk->cij" if orient == 0 else "cki,ckj->cij"
    summed = jnp.einsum(spec, left, everywhere, preferred_element_type=jnp.float32)
    hidden = layer_norm(summed, mid[:, None, None], 0).astype(jnp.bfloat16)
    gating = jax.nn.sigmoid(
        jnp.einsum("ijd,de->ije", normed, gate, preferred_element_type=jnp.float32)
    )
    update = jnp.einsum("cij,cd->ijd", hidden, out, preferred_element_type=jnp.float32)
    return (floats + gating * update).astype(jnp.bfloat16)


def shards(pair_rep, pair_mask, proj_weight, gate_weight, out_weight, norm_gain, mid_gain):
    mask = pair_mask.astype(jnp.float32).reshape(1, -1)
    current = pair_rep
    devices = pair_rep.shape[1] // pair_rep.shape[0]
    update = triangle if out_weight.shape[1] % devices == 0 else triangle_gathered
    for orient in range(2):
        current = update(
            current, mask, proj_weight[orient], gate_weight[orient], out_weight[orient],
            norm_gain[orient], mid_gain[orient], orient,
        )
    return current


def solution(mesh):
    return jax.shard_map(
        shards,
        mesh=mesh,
        in_specs=(P(("groups", "row")), P(("groups", "row")), P(), P(), P(), P(), P()),
        out_specs=P(("groups", "row")),
        check_vma=False,
    )
```

```python
import functools

import jax
import jax.numpy as jnp
from jax import lax
from jax.experimental import pallas as pl
from jax.experimental.pallas import tpu as pltpu
from jax.sharding import PartitionSpec as P

EPS = 1e-05
F32, BF16 = jnp.float32, jnp.bfloat16
LANES = 128
MASK_ROWS = 16
NT = (((1,), (1,)), ((), ()))


def dot(a, b):
    return jnp.dot(a, b, preferred_element_type=F32)


def dot_nt(a, b):
    return lax.dot_general(a, b, NT, preferred_element_type=F32)


def sigmoid(x):
    return 0.5 * jnp.tanh(0.5 * x) + 0.5


def iota(shape, axis):
    return lax.broadcasted_iota(jnp.int32, shape, axis)


def token_of(t, rows, tokens):
    devices = tokens // rows
    return (t % devices) * rows + t // devices


def column_norm(values, gain):
    average = jnp.mean(values, axis=0, keepdims=True)
    centred = values - average
    variance = jnp.mean(centred * centred, axis=0, keepdims=True)
    return (centred * lax.rsqrt(variance + EPS) * gain).astype(BF16)


def position_permutation(rows, tokens, by_lane):
    size = rows * tokens
    shape = (size, size)
    lane = iota(shape, 0 if by_lane else 1)
    position = iota(shape, 1 if by_lane else 0)
    source = lane // tokens * tokens + token_of(lane % tokens, rows, tokens)
    return (source == position).astype(F32).astype(BF16)


def pack_kernel(rows, tokens, pair_ref, mask_ref, packed_ref):
    channels = pair_ref.shape[-1]
    size = rows * tokens
    permuted = dot(position_permutation(rows, tokens, True), pair_ref[...]).astype(BF16)
    identity = (iota((channels, channels), 0) == iota((channels, channels), 1)).astype(F32)
    packed_ref[:channels, :] = dot_nt(identity.astype(BF16), permuted).astype(BF16)
    lane = iota((tokens, size), 1)
    place = token_of(lane % tokens, rows, tokens) == iota((tokens, size), 0)
    spread = dot(mask_ref[...].astype(F32).astype(BF16), place.astype(F32).astype(BF16))
    own = iota((rows, size), 0) == iota((rows, size), 1) // tokens
    line = jnp.sum(jnp.where(own, spread, 0.0), axis=0, keepdims=True)
    packed_ref[channels:, :] = jnp.broadcast_to(line, (MASK_ROWS, size)).astype(BF16)


def both_kernel(
    rows, tokens, me_ref, packed_ref, proj_ref, gate_ref, out_ref, gain_ref, mid_ref,
    result_ref, left_s, right_s, normed_s, sum_s, now_s, second_left_s, second_right_s,
):
    devices = tokens // rows
    size = rows * tokens
    channels = proj_ref.shape[1]
    hw = out_ref.shape[1]
    tiles = size // LANES
    me = me_ref[0]

    def flipped(weight):
        return weight.astype(F32).T.astype(BF16)

    def column(line, width):
        tall = jnp.broadcast_to(line, (LANES, line.shape[1])).T
        return jnp.concatenate([tall] * (width // LANES), axis=1)

    def factors(projected, mask):
        left = mask * sigmoid(projected[hw : 2 * hw]) * projected[:hw]
        right = mask * sigmoid(projected[3 * hw :]) * projected[2 * hw : 3 * hw]
        return left, right

    gains = [column(gain_ref[o : o + 1, :], size) for o in range(2)]
    mids = [column(mid_ref[o : o + 1, :], size) for o in range(2)]
    proj_t = [flipped(proj_ref[o]) for o in range(2)]
    gate_t = [flipped(gate_ref[o]) for o in range(2)]
    out_t = [flipped(out_ref[o]) for o in range(2)]

    def block_of(b):
        return packed_ref[b, :channels, :].astype(F32)

    def mask_of(b):
        return packed_ref[b, channels : channels + MASK_ROWS, :].astype(F32)[:1]

    def project_first(b, _):
        normed = column_norm(block_of(b), gains[0])
        normed_s[b] = normed
        left, right = factors(dot(proj_t[0], normed), mask_of(b))
        here = pl.ds(pl.multiple_of(b * hw, hw), hw)
        for h in range(tiles):
            left_s[h, here, :] = left[:, h * LANES : (h + 1) * LANES]
            right_s[h, here, :] = right[:, h * LANES : (h + 1) * LANES]
        return 0

    lax.fori_loop(0, devices, project_first, 0, unroll=2)

    low = iota((devices, LANES), 1) < tokens

    def channel_sum(c, _):
        here = pl.ds(c, devices, stride=hw)
        left = jnp.concatenate([left_s[h, here, :] for h in range(tiles)], axis=0)
        halves = [[], []]
        for h in range(tiles):
            right = right_s[h, here, :]
            turned = pltpu.roll(right, tokens, 1)
            for q in range(2):
                straight, other = (right, turned) if q == 0 else (turned, right)
                halves[0].append(jnp.where(low, straight, 0.0))
                halves[1].append(jnp.where(low, 0.0, other))
        against = jnp.concatenate(halves[0] + halves[1], axis=0).astype(BF16)
        here = pl.ds(pl.multiple_of(c * tiles * devices, tiles * devices), tiles * devices)
        sum_s[here, :] = dot_nt(left.astype(BF16), against)
        return 0

    lax.fori_loop(0, hw, channel_sum, 0, unroll=8)

    def second_factors(b, _):
        summed = jnp.concatenate(
            [sum_s[pl.ds(h * devices + b, hw, stride=tiles * devices), :] for h in range(tiles)],
            axis=1,
        )
        update = dot(out_t[0], column_norm(summed, mids[0]))
        gating = sigmoid(dot(gate_t[0], normed_s[b]))
        now = (block_of(b) + gating * update).astype(BF16)
        now_s[b] = now
        normed = column_norm(now.astype(F32), gains[1])
        normed_s[b] = normed
        left, right = factors(dot(proj_t[1], normed), mask_of(b))
        second_left_s[b] = left.astype(BF16)
        second_right_s[b] = right.astype(BF16)
        return 0

    lax.fori_loop(0, devices, second_factors, 0, unroll=2)

    row_group, row_lane = iota((size, size), 0) // tokens, iota((size, size), 0) % tokens
    same = row_group == iota((size, size), 1) // tokens
    sums = []
    for i in range(rows):
        spread = (same & (row_lane == i * devices + me)).astype(F32).astype(BF16)

        def add(b, total):
            return total + dot(second_left_s[b], spread) * second_right_s[b].astype(F32)

        total = lax.fori_loop(0, devices, add, jnp.zeros((hw, size), F32), unroll=4)
        total = sum(total[:, h * LANES : (h + 1) * LANES] for h in range(tiles))
        sums.append(total + pltpu.roll(total, tokens, 1))
    low = iota((hw, LANES), 1) < tokens
    summed = jnp.concatenate(
        [jnp.where(low, sums[2 * h], sums[2 * h + 1]) for h in range(tiles)], axis=1
    )
    update = dot(out_t[1], column_norm(summed, mids[1]))
    gating = sigmoid(dot(gate_t[1], normed_s[me]))
    final = (now_s[me].astype(F32) + gating * update).astype(BF16)
    result_ref[...] = dot_nt(position_permutation(rows, tokens, False), final).astype(BF16)


def small_plan(pair, mask, proj, gate, out, gain, mid):
    rows, tokens, channels = pair.shape
    devices, size, hw = tokens // rows, rows * tokens, out.shape[1]
    packed = pl.pallas_call(
        functools.partial(pack_kernel, rows, tokens),
        out_shape=jax.ShapeDtypeStruct((channels + MASK_ROWS, size), BF16),
        name="pack",
    )(pair.reshape(size, channels), mask)
    everywhere = lax.all_gather(packed, "row", axis=0)
    me = lax.axis_index("row").reshape(1).astype(jnp.int32)
    vmem = pl.BlockSpec(memory_space=pltpu.VMEM)
    result = pl.pallas_call(
        functools.partial(both_kernel, rows, tokens),
        out_shape=jax.ShapeDtypeStruct((size, channels), BF16),
        in_specs=[pl.BlockSpec(memory_space=pltpu.SMEM)] + [vmem] * 6,
        out_specs=vmem,
        scratch_shapes=[
            pltpu.VMEM((size // LANES, devices * hw, LANES), F32),
            pltpu.VMEM((size // LANES, devices * hw, LANES), F32),
            pltpu.VMEM((devices, channels, size), BF16),
            pltpu.VMEM((hw * devices * size // LANES, LANES), F32),
            pltpu.VMEM((devices, channels, size), BF16),
            pltpu.VMEM((devices, hw, size), BF16),
            pltpu.VMEM((devices, hw, size), BF16),
        ],
        compiler_params=pltpu.CompilerParams(vmem_limit_bytes=40 * 1024 * 1024),
        name="both",
    )(me, everywhere, proj, gate, out, gain, mid)
    return result.reshape(pair.shape)


def layer_norm(values, gain, axis):
    average = jnp.mean(values, axis=axis, keepdims=True)
    centred = values - average
    variance = jnp.mean(centred * centred, axis=axis, keepdims=True)
    return centred * lax.rsqrt(variance + EPS) * gain


def factors(normed, mask, proj):
    hw = proj.shape[1] // 4
    projected = jnp.einsum("ijd,de->eij", normed, proj, preferred_element_type=F32)
    left = mask * jax.nn.sigmoid(projected[hw : 2 * hw]) * projected[:hw]
    right = mask * jax.nn.sigmoid(projected[3 * hw :]) * projected[2 * hw : 3 * hw]
    return left.astype(BF16), right.astype(BF16)


def gathered_update(pair, mask, proj, gate, out, gain, mid, orient):
    rows, tokens, _ = pair.shape
    devices = tokens // rows
    floats = pair.astype(F32)
    normed = layer_norm(floats, gain, -1).astype(BF16)
    left, right = factors(normed, mask, proj)
    everywhere = lax.all_gather(right, "row", axis=1, tiled=True)
    if orient == 1:
        c = left.shape[0]
        blocks = left.reshape(c, rows, devices, rows).transpose(2, 1, 3, 0)
        left = lax.all_to_all(blocks, "row", 0, 0, tiled=True)
        left = left.reshape(tokens, rows, c).transpose(2, 0, 1)
    spec = "cik,cjk->cij" if orient == 0 else "cki,ckj->cij"
    summed = jnp.einsum(spec, left, everywhere, preferred_element_type=F32)
    hidden = layer_norm(summed, mid[:, None, None], 0).astype(BF16)
    gating = jax.nn.sigmoid(jnp.einsum("ijd,de->ije", normed, gate, preferred_element_type=F32))
    update = jnp.einsum("cij,cd->ijd", hidden, out, preferred_element_type=F32)
    return (floats + gating * update).astype(BF16)


def shards(pair, pair_mask, proj, gate, out, gain, mid):
    rows, tokens, _ = pair.shape
    if rows == 4 and 2 * tokens == LANES:
        return small_plan(pair, pair_mask, proj, gate, out, gain, mid)
    mask = pair_mask.astype(F32)[None]
    for o in range(2):
        pair = gathered_update(pair, mask, proj[o], gate[o], out[o], gain[o], mid[o], o)
    return pair


def solution(mesh):
    return jax.shard_map(
        shards,
        mesh=mesh,
        in_specs=(P(("groups", "row")), P(("groups", "row")), P(), P(), P(), P(), P()),
        out_specs=P(("groups", "row")),
        check_vma=False,
    )
```

```python
import functools

import jax
import jax.numpy as jnp
from jax import lax
from jax.experimental import pallas as pl
from jax.experimental.pallas import tpu as pltpu
from jax.sharding import PartitionSpec as P

EPS = 1e-05
F32, BF16 = jnp.float32, jnp.bfloat16
LANES = 128
MASK_ROWS = 16
NT = (((1,), (1,)), ((), ()))


def dot(a, b):
    return jnp.dot(a, b, preferred_element_type=F32)


def dot_nt(a, b):
    return lax.dot_general(a, b, NT, preferred_element_type=F32)


def sigmoid(x):
    return 0.5 * jnp.tanh(0.5 * x) + 0.5


def iota(shape, axis):
    return lax.broadcasted_iota(jnp.int32, shape, axis)


def token_of(t, rows, tokens):
    devices = tokens // rows
    return (t % devices) * rows + t // devices


def column_norm(values, gain):
    average = jnp.mean(values, axis=0, keepdims=True)
    centred = values - average
    variance = jnp.mean(centred * centred, axis=0, keepdims=True)
    return (centred * lax.rsqrt(variance + EPS) * gain).astype(BF16)


def position_permutation(rows, tokens, by_lane):
    size = rows * tokens
    shape = (size, size)
    lane = iota(shape, 0 if by_lane else 1)
    position = iota(shape, 1 if by_lane else 0)
    source = lane // tokens * tokens + token_of(lane % tokens, rows, tokens)
    return (source == position).astype(F32).astype(BF16)


def pack_kernel(rows, tokens, pair_ref, mask_ref, packed_ref):
    channels = pair_ref.shape[-1]
    size = rows * tokens
    permuted = dot(position_permutation(rows, tokens, True), pair_ref[...]).astype(BF16)
    identity = (iota((channels, channels), 0) == iota((channels, channels), 1)).astype(F32)
    packed_ref[:channels, :] = dot_nt(identity.astype(BF16), permuted).astype(BF16)
    lane = iota((tokens, size), 1)
    place = token_of(lane % tokens, rows, tokens) == iota((tokens, size), 0)
    spread = dot(mask_ref[...].astype(F32).astype(BF16), place.astype(F32).astype(BF16))
    own = iota((rows, size), 0) == iota((rows, size), 1) // tokens
    line = jnp.sum(jnp.where(own, spread, 0.0), axis=0, keepdims=True)
    packed_ref[channels:, :] = jnp.broadcast_to(line, (MASK_ROWS, size)).astype(BF16)


def prepare_kernel(
    rows, tokens, me_ref, proj_ref, gate_ref, out_ref, gain_ref, mid_ref,
    proj_t_ref, gate_t_ref, out_t_ref, gain_t_ref, mid_t_ref, restore_ref, spread_ref,
):
    size, devices = rows * tokens, tokens // rows

    def flipped(weight):
        return weight.astype(F32).T.astype(BF16)

    def column(line):
        return jnp.broadcast_to(line, (LANES, line.shape[1])).T

    for o in range(2):
        proj_t_ref[o] = flipped(proj_ref[o])
        gate_t_ref[o] = flipped(gate_ref[o])
        out_t_ref[o] = flipped(out_ref[o])
        gain_t_ref[o] = column(gain_ref[o : o + 1, :])
        mid_t_ref[o] = column(mid_ref[o : o + 1, :])
    restore_ref[...] = position_permutation(rows, tokens, False)
    group, lane = iota((size, size), 0) // tokens, iota((size, size), 0) % tokens
    same = group == iota((size, size), 1) // tokens
    for i in range(rows):
        spread_ref[i] = (same & (lane == i * devices + me_ref[0])).astype(F32).astype(BF16)


def both_kernel(
    rows, tokens, me_ref, *refs,
):
    devices = tokens // rows
    packed_refs, refs = refs[:devices], refs[devices:]
    (
        proj_ref, gate_ref, out_ref, gain_ref, mid_ref, restore_ref, spread_ref, result_ref,
        left_s, right_s, normed_s, sum_s, now_s, second_left_s, second_right_s,
    ) = refs
    size = rows * tokens
    channels = gate_ref.shape[1]
    hw = mid_ref.shape[1]
    tiles = size // LANES
    me = me_ref[0]

    def wide(column):
        return jnp.concatenate([column] * tiles, axis=1)

    def factors(projected, mask):
        left = mask * sigmoid(projected[hw : 2 * hw]) * projected[:hw]
        right = mask * sigmoid(projected[3 * hw :]) * projected[2 * hw : 3 * hw]
        return left, right

    def block_of(packed_ref):
        return packed_ref[:channels, :].astype(F32)

    def mask_of(packed_ref):
        return packed_ref[channels:, :].astype(F32)[:1]

    for m, packed_ref in enumerate(packed_refs):
        b = me ^ m
        normed = column_norm(block_of(packed_ref), wide(gain_ref[0]))
        normed_s[m] = normed
        left, right = factors(dot(proj_ref[0], normed), mask_of(packed_ref))
        here = pl.ds(pl.multiple_of(b * hw, hw), hw)
        for h in range(tiles):
            left_s[h, here, :] = left[:, h * LANES : (h + 1) * LANES]
            right_s[h, here, :] = right[:, h * LANES : (h + 1) * LANES]

    low = iota((devices, LANES), 1) < tokens

    def channel_sum(c, _):
        here = pl.ds(c, devices, stride=hw)
        left = jnp.concatenate([left_s[h, here, :] for h in range(tiles)], axis=0)
        halves = [[], []]
        for h in range(tiles):
            right = right_s[h, here, :]
            turned = pltpu.roll(right, tokens, 1)
            for q in range(2):
                straight, other = (right, turned) if q == 0 else (turned, right)
                halves[0].append(jnp.where(low, straight, 0.0))
                halves[1].append(jnp.where(low, 0.0, other))
        against = jnp.concatenate(halves[0] + halves[1], axis=0).astype(BF16)
        here = pl.ds(pl.multiple_of(c * tiles * devices, tiles * devices), tiles * devices)
        sum_s[here, :] = dot_nt(left.astype(BF16), against)
        return 0

    lax.fori_loop(0, hw, channel_sum, 0, unroll=16)

    for m, packed_ref in enumerate(packed_refs):
        b = me ^ m
        summed = jnp.concatenate(
            [sum_s[pl.ds(h * devices + b, hw, stride=tiles * devices), :] for h in range(tiles)],
            axis=1,
        )
        update = dot(out_ref[0], column_norm(summed, wide(mid_ref[0])))
        gating = sigmoid(dot(gate_ref[0], normed_s[m]))
        now = (block_of(packed_ref) + gating * update).astype(BF16)
        normed = column_norm(now.astype(F32), wide(gain_ref[1]))
        if m == 0:
            now_s[...] = now
            normed_s[0] = normed
        left, right = factors(dot(proj_ref[1], normed), mask_of(packed_ref))
        second_left_s[m] = left.astype(BF16)
        second_right_s[m] = right.astype(BF16)

    sums = []
    for i in range(rows):

        def add(m, total):
            return total + dot(second_left_s[m], spread_ref[i]) * second_right_s[m].astype(F32)

        total = lax.fori_loop(0, devices, add, jnp.zeros((hw, size), F32), unroll=4)
        total = sum(total[:, h * LANES : (h + 1) * LANES] for h in range(tiles))
        sums.append(total + pltpu.roll(total, tokens, 1))
    low = iota((hw, LANES), 1) < tokens
    summed = jnp.concatenate(
        [jnp.where(low, sums[2 * h], sums[2 * h + 1]) for h in range(tiles)], axis=1
    )
    update = dot(out_ref[1], column_norm(summed, wide(mid_ref[1])))
    gating = sigmoid(dot(gate_ref[1], normed_s[0]))
    final = (now_s[...].astype(F32) + gating * update).astype(BF16)
    result_ref[...] = dot_nt(restore_ref[...], final).astype(BF16)


def exchange(block, partner_bits, devices):
    pairs = [(d, d ^ partner_bits) for d in range(devices)]
    return lax.ppermute(block, "row", pairs)


def everyone(packed, devices):
    blocks = {0: packed}
    for m in range(4, devices, 4):
        blocks[m] = exchange(packed, m, devices)
    for step in (2, 1):
        for m in sorted(blocks):
            blocks[m ^ step] = exchange(blocks[m], step, devices)
    return [blocks[m] for m in range(devices)]


def small_plan(pair, mask, proj, gate, out, gain, mid):
    rows, tokens, channels = pair.shape
    devices, size, hw = tokens // rows, rows * tokens, out.shape[1]
    packed = pl.pallas_call(
        functools.partial(pack_kernel, rows, tokens),
        out_shape=jax.ShapeDtypeStruct((channels + MASK_ROWS, size), BF16),
        name="pack",
    )(pair.reshape(size, channels), mask)
    me = lax.axis_index("row").reshape(1).astype(jnp.int32)
    whole = pl.BlockSpec()
    index = pl.BlockSpec(memory_space=pltpu.SMEM)
    weights = pl.pallas_call(
        functools.partial(prepare_kernel, rows, tokens),
        in_specs=[index] + [whole] * 5,
        out_shape=(
            jax.ShapeDtypeStruct((2, 4 * hw, channels), BF16),
            jax.ShapeDtypeStruct((2, channels, channels), BF16),
            jax.ShapeDtypeStruct((2, channels, hw), BF16),
            jax.ShapeDtypeStruct((2, channels, LANES), F32),
            jax.ShapeDtypeStruct((2, hw, LANES), F32),
            jax.ShapeDtypeStruct((size, size), BF16),
            jax.ShapeDtypeStruct((rows, size, size), BF16),
        ),
        name="prepare",
    )(me, proj, gate, out, gain, mid)
    blocks = everyone(packed, devices)
    result = pl.pallas_call(
        functools.partial(both_kernel, rows, tokens),
        out_shape=jax.ShapeDtypeStruct((size, channels), BF16),
        in_specs=[index] + [whole] * (devices + len(weights)),
        scratch_shapes=[
            pltpu.VMEM((size // LANES, devices * hw, LANES), F32),
            pltpu.VMEM((size // LANES, devices * hw, LANES), F32),
            pltpu.VMEM((devices, channels, size), BF16),
            pltpu.VMEM((hw * devices * size // LANES, LANES), F32),
            pltpu.VMEM((channels, size), BF16),
            pltpu.VMEM((devices, hw, size), BF16),
            pltpu.VMEM((devices, hw, size), BF16),
        ],
        compiler_params=pltpu.CompilerParams(vmem_limit_bytes=40 * 1024 * 1024),
        name="both",
    )(me, *blocks, *weights)
    return result.reshape(pair.shape)


def layer_norm(values, gain, axis):
    average = jnp.mean(values, axis=axis, keepdims=True)
    centred = values - average
    variance = jnp.mean(centred * centred, axis=axis, keepdims=True)
    return centred * lax.rsqrt(variance + EPS) * gain


def factors(normed, mask, proj):
    hw = proj.shape[1] // 4
    projected = jnp.einsum("ijd,de->eij", normed, proj, preferred_element_type=F32)
    left = mask * jax.nn.sigmoid(projected[hw : 2 * hw]) * projected[:hw]
    right = mask * jax.nn.sigmoid(projected[3 * hw :]) * projected[2 * hw : 3 * hw]
    return left.astype(BF16), right.astype(BF16)


def gathered_update(pair, mask, proj, gate, out, gain, mid, orient):
    rows, tokens, _ = pair.shape
    devices = tokens // rows
    floats = pair.astype(F32)
    normed = layer_norm(floats, gain, -1).astype(BF16)
    left, right = factors(normed, mask, proj)
    everywhere = lax.all_gather(right, "row", axis=1, tiled=True)
    if orient == 1:
        c = left.shape[0]
        blocks = left.reshape(c, rows, devices, rows).transpose(2, 1, 3, 0)
        left = lax.all_to_all(blocks, "row", 0, 0, tiled=True)
        left = left.reshape(tokens, rows, c).transpose(2, 0, 1)
    spec = "cik,cjk->cij" if orient == 0 else "cki,ckj->cij"
    summed = jnp.einsum(spec, left, everywhere, preferred_element_type=F32)
    hidden = layer_norm(summed, mid[:, None, None], 0).astype(BF16)
    gating = jax.nn.sigmoid(jnp.einsum("ijd,de->ije", normed, gate, preferred_element_type=F32))
    update = jnp.einsum("cij,cd->ijd", hidden, out, preferred_element_type=F32)
    return (floats + gating * update).astype(BF16)


def shards(pair, pair_mask, proj, gate, out, gain, mid):
    rows, tokens, _ = pair.shape
    if rows == 4 and 2 * tokens == LANES:
        return small_plan(pair, pair_mask, proj, gate, out, gain, mid)
    mask = pair_mask.astype(F32)[None]
    for o in range(2):
        pair = gathered_update(pair, mask, proj[o], gate[o], out[o], gain[o], mid[o], o)
    return pair


def solution(mesh):
    return jax.shard_map(
        shards,
        mesh=mesh,
        in_specs=(P(("groups", "row")), P(("groups", "row")), P(), P(), P(), P(), P()),
        out_specs=P(("groups", "row")),
        check_vma=False,
    )
```

```python
import functools

import jax
import jax.numpy as jnp
from jax import lax
from jax.experimental import pallas as pl
from jax.experimental.pallas import tpu as pltpu
from jax.sharding import PartitionSpec as P

EPS = 1e-05
F32, BF16 = jnp.float32, jnp.bfloat16
LANES = 128
MASK_ROWS = 16
NT = (((1,), (1,)), ((), ()))


def dot(a, b):
    return jnp.dot(a, b, preferred_element_type=F32)


def dot_nt(a, b):
    return lax.dot_general(a, b, NT, preferred_element_type=F32)


def sigmoid(x):
    return 0.5 * jnp.tanh(0.5 * x) + 0.5


def iota(shape, axis):
    return lax.broadcasted_iota(jnp.int32, shape, axis)


def token_of(t, rows, tokens):
    devices = tokens // rows
    return (t % devices) * rows + t // devices


def column_norm(values, gain):
    average = jnp.mean(values, axis=0, keepdims=True)
    centred = values - average
    variance = jnp.mean(centred * centred, axis=0, keepdims=True)
    return (centred * lax.rsqrt(variance + EPS) * gain).astype(BF16)


def position_permutation(rows, tokens, by_lane):
    size = rows * tokens
    shape = (size, size)
    lane = iota(shape, 0 if by_lane else 1)
    position = iota(shape, 1 if by_lane else 0)
    source = lane // tokens * tokens + token_of(lane % tokens, rows, tokens)
    return (source == position).astype(F32).astype(BF16)


def pack_kernel(rows, tokens, pair_ref, mask_ref, packed_ref):
    channels = pair_ref.shape[-1]
    size = rows * tokens
    permuted = dot(position_permutation(rows, tokens, True), pair_ref[...]).astype(BF16)
    identity = (iota((channels, channels), 0) == iota((channels, channels), 1)).astype(F32)
    packed_ref[:channels, :] = dot_nt(identity.astype(BF16), permuted).astype(BF16)
    lane = iota((tokens, size), 1)
    place = token_of(lane % tokens, rows, tokens) == iota((tokens, size), 0)
    spread = dot(mask_ref[...].astype(F32).astype(BF16), place.astype(F32).astype(BF16))
    own = iota((rows, size), 0) == iota((rows, size), 1) // tokens
    line = jnp.sum(jnp.where(own, spread, 0.0), axis=0, keepdims=True)
    packed_ref[channels:, :] = jnp.broadcast_to(line, (MASK_ROWS, size)).astype(BF16)


def prepare_kernel(
    rows, tokens, me_ref, proj_ref, gate_ref, out_ref, gain_ref, mid_ref,
    proj_t_ref, gate_t_ref, out_t_ref, gain_t_ref, mid_t_ref, restore_ref, spread_ref,
):
    size, devices = rows * tokens, tokens // rows

    def flipped(weight):
        return weight.astype(F32).T.astype(BF16)

    def column(line):
        return jnp.broadcast_to(line, (LANES, line.shape[1])).T

    for o in range(2):
        proj_t_ref[o] = flipped(proj_ref[o])
        gate_t_ref[o] = flipped(gate_ref[o])
        out_t_ref[o] = flipped(out_ref[o])
        gain_t_ref[o] = column(gain_ref[o : o + 1, :])
        mid_t_ref[o] = column(mid_ref[o : o + 1, :])
    restore_ref[...] = position_permutation(rows, tokens, False)
    group, lane = iota((size, size), 0) // tokens, iota((size, size), 0) % tokens
    same = group == iota((size, size), 1) // tokens
    for i in range(rows):
        spread_ref[i] = (same & (lane == i * devices + me_ref[0])).astype(F32).astype(BF16)


def both_kernel(
    rows, tokens, me_ref, *refs,
):
    devices = tokens // rows
    packed_refs, refs = refs[:devices], refs[devices:]
    (
        proj_ref, gate_ref, out_ref, gain_ref, mid_ref, restore_ref, spread_ref, result_ref,
        left_s, right_s, normed_s, sum_s, now_s, second_left_s, second_right_s,
    ) = refs
    size = rows * tokens
    channels = gate_ref.shape[1]
    hw = mid_ref.shape[1]
    tiles = size // LANES
    me = me_ref[0]

    def wide(column):
        return jnp.concatenate([column] * tiles, axis=1)

    def factors(projected, mask):
        left = mask * sigmoid(projected[hw : 2 * hw]) * projected[:hw]
        right = mask * sigmoid(projected[3 * hw :]) * projected[2 * hw : 3 * hw]
        return left, right

    def block_of(packed_ref):
        return packed_ref[:channels, :].astype(F32)

    def mask_of(packed_ref):
        return packed_ref[channels:, :].astype(F32)[:1]

    for m, packed_ref in enumerate(packed_refs):
        b = me ^ m
        normed = column_norm(block_of(packed_ref), wide(gain_ref[0]))
        normed_s[m] = normed
        left, right = factors(dot(proj_ref[0], normed), mask_of(packed_ref))
        here = pl.ds(pl.multiple_of(b * hw, hw), hw)
        for h in range(tiles):
            left_s[h, here, :] = left[:, h * LANES : (h + 1) * LANES]
            right_s[h, here, :] = right[:, h * LANES : (h + 1) * LANES]

    low = iota((devices, LANES), 1) < tokens

    def channel_sum(c, _):
        here = pl.ds(c, devices, stride=hw)
        left = jnp.concatenate([left_s[h, here, :] for h in range(tiles)], axis=0)
        halves = [[], []]
        for h in range(tiles):
            right = right_s[h, here, :]
            turned = pltpu.roll(right, tokens, 1)
            for q in range(2):
                straight, other = (right, turned) if q == 0 else (turned, right)
                halves[0].append(jnp.where(low, straight, 0.0))
                halves[1].append(jnp.where(low, 0.0, other))
        against = jnp.concatenate(halves[0] + halves[1], axis=0).astype(BF16)
        here = pl.ds(pl.multiple_of(c * tiles * devices, tiles * devices), tiles * devices)
        sum_s[here, :] = dot_nt(left.astype(BF16), against)
        return 0

    lax.fori_loop(0, hw, channel_sum, 0, unroll=16)

    for m, packed_ref in enumerate(packed_refs):
        b = me ^ m
        summed = jnp.concatenate(
            [sum_s[pl.ds(h * devices + b, hw, stride=tiles * devices), :] for h in range(tiles)],
            axis=1,
        )
        update = dot(out_ref[0], column_norm(summed, wide(mid_ref[0])))
        gating = sigmoid(dot(gate_ref[0], normed_s[m]))
        now = (block_of(packed_ref) + gating * update).astype(BF16)
        normed = column_norm(now.astype(F32), wide(gain_ref[1]))
        if m == 0:
            now_s[...] = now
            normed_s[0] = normed
        left, right = factors(dot(proj_ref[1], normed), mask_of(packed_ref))
        second_left_s[m] = left.astype(BF16)
        second_right_s[m] = right.astype(BF16)

    sums = []
    for i in range(rows):

        def add(m, total):
            return total + dot(second_left_s[m], spread_ref[i]) * second_right_s[m].astype(F32)

        total = lax.fori_loop(0, devices, add, jnp.zeros((hw, size), F32), unroll=4)
        total = sum(total[:, h * LANES : (h + 1) * LANES] for h in range(tiles))
        sums.append(total + pltpu.roll(total, tokens, 1))
    low = iota((hw, LANES), 1) < tokens
    summed = jnp.concatenate(
        [jnp.where(low, sums[2 * h], sums[2 * h + 1]) for h in range(tiles)], axis=1
    )
    update = dot(out_ref[1], column_norm(summed, wide(mid_ref[1])))
    gating = sigmoid(dot(gate_ref[1], normed_s[0]))
    final = (now_s[...].astype(F32) + gating * update).astype(BF16)
    result_ref[...] = dot_nt(restore_ref[...], final).astype(BF16)


def exchange(block, partner_bits, devices):
    pairs = [(d, d ^ partner_bits) for d in range(devices)]
    return lax.ppermute(block, "row", pairs)


def everyone(packed, devices):
    blocks = {0: packed}
    for m in range(devices - 4, 0, -4):
        blocks[m] = exchange(packed, m, devices)
    for step in (2, 1):
        for m in sorted(blocks, reverse=True):
            blocks[m ^ step] = exchange(blocks[m], step, devices)
    return [blocks[m] for m in range(devices)]


def small_plan(pair, mask, proj, gate, out, gain, mid):
    rows, tokens, channels = pair.shape
    devices, size, hw = tokens // rows, rows * tokens, out.shape[1]
    index = pl.BlockSpec(memory_space=pltpu.SMEM)
    vmem = pl.BlockSpec(memory_space=pltpu.VMEM)
    packed = pl.pallas_call(
        functools.partial(pack_kernel, rows, tokens),
        out_shape=jax.ShapeDtypeStruct((channels + MASK_ROWS, size), BF16),
        out_specs=vmem,
        name="pack",
    )(pair.reshape(size, channels), mask)
    me = lax.axis_index("row").reshape(1).astype(jnp.int32)
    weights = pl.pallas_call(
        functools.partial(prepare_kernel, rows, tokens),
        in_specs=[index] + [pl.BlockSpec()] * 5,
        out_specs=(vmem,) * 7,
        out_shape=(
            jax.ShapeDtypeStruct((2, 4 * hw, channels), BF16),
            jax.ShapeDtypeStruct((2, channels, channels), BF16),
            jax.ShapeDtypeStruct((2, channels, hw), BF16),
            jax.ShapeDtypeStruct((2, channels, LANES), F32),
            jax.ShapeDtypeStruct((2, hw, LANES), F32),
            jax.ShapeDtypeStruct((size, size), BF16),
            jax.ShapeDtypeStruct((rows, size, size), BF16),
        ),
        name="prepare",
    )(me, proj, gate, out, gain, mid)
    blocks = everyone(packed, devices)
    result = pl.pallas_call(
        functools.partial(both_kernel, rows, tokens),
        out_shape=jax.ShapeDtypeStruct((size, channels), BF16),
        in_specs=[index] + [vmem] * (devices + len(weights)),
        scratch_shapes=[
            pltpu.VMEM((size // LANES, devices * hw, LANES), F32),
            pltpu.VMEM((size // LANES, devices * hw, LANES), F32),
            pltpu.VMEM((devices, channels, size), BF16),
            pltpu.VMEM((hw * devices * size // LANES, LANES), F32),
            pltpu.VMEM((channels, size), BF16),
            pltpu.VMEM((devices, hw, size), BF16),
            pltpu.VMEM((devices, hw, size), BF16),
        ],
        compiler_params=pltpu.CompilerParams(vmem_limit_bytes=40 * 1024 * 1024),
        name="both",
    )(me, *blocks, *weights)
    return result.reshape(pair.shape)


def layer_norm(values, gain, axis):
    average = jnp.mean(values, axis=axis, keepdims=True)
    centred = values - average
    variance = jnp.mean(centred * centred, axis=axis, keepdims=True)
    return centred * lax.rsqrt(variance + EPS) * gain


def factors(normed, mask, proj):
    hw = proj.shape[1] // 4
    projected = jnp.einsum("ijd,de->eij", normed, proj, preferred_element_type=F32)
    left = mask * jax.nn.sigmoid(projected[hw : 2 * hw]) * projected[:hw]
    right = mask * jax.nn.sigmoid(projected[3 * hw :]) * projected[2 * hw : 3 * hw]
    return left.astype(BF16), right.astype(BF16)


def gathered_update(pair, mask, proj, gate, out, gain, mid, orient):
    rows, tokens, _ = pair.shape
    devices = tokens // rows
    floats = pair.astype(F32)
    normed = layer_norm(floats, gain, -1).astype(BF16)
    left, right = factors(normed, mask, proj)
    everywhere = lax.all_gather(right, "row", axis=1, tiled=True)
    if orient == 1:
        c = left.shape[0]
        blocks = left.reshape(c, rows, devices, rows).transpose(2, 1, 3, 0)
        left = lax.all_to_all(blocks, "row", 0, 0, tiled=True)
        left = left.reshape(tokens, rows, c).transpose(2, 0, 1)
    spec = "cik,cjk->cij" if orient == 0 else "cki,ckj->cij"
    summed = jnp.einsum(spec, left, everywhere, preferred_element_type=F32)
    hidden = layer_norm(summed, mid[:, None, None], 0).astype(BF16)
    gating = jax.nn.sigmoid(jnp.einsum("ijd,de->ije", normed, gate, preferred_element_type=F32))
    update = jnp.einsum("cij,cd->ijd", hidden, out, preferred_element_type=F32)
    return (floats + gating * update).astype(BF16)


def shards(pair, pair_mask, proj, gate, out, gain, mid):
    rows, tokens, _ = pair.shape
    if rows == 4 and 2 * tokens == LANES:
        return small_plan(pair, pair_mask, proj, gate, out, gain, mid)
    mask = pair_mask.astype(F32)[None]
    for o in range(2):
        pair = gathered_update(pair, mask, proj[o], gate[o], out[o], gain[o], mid[o], o)
    return pair


def solution(mesh):
    return jax.shard_map(
        shards,
        mesh=mesh,
        in_specs=(P(("groups", "row")), P(("groups", "row")), P(), P(), P(), P(), P()),
        out_specs=P(("groups", "row")),
        check_vma=False,
    )
```

```python
import functools

import jax
import jax.numpy as jnp
from jax import lax
from jax.experimental import pallas as pl
from jax.experimental.pallas import tpu as pltpu
from jax.sharding import PartitionSpec as P

EPS = 1e-05
F32, BF16 = jnp.float32, jnp.bfloat16
LANES = 128
MASK_ROWS = 16
NT = (((1,), (1,)), ((), ()))


def dot(a, b):
    return jnp.dot(a, b, preferred_element_type=F32)


def dot_nt(a, b):
    return lax.dot_general(a, b, NT, preferred_element_type=F32)


def sigmoid(x):
    return 0.5 * jnp.tanh(0.5 * x) + 0.5


def iota(shape, axis):
    return lax.broadcasted_iota(jnp.int32, shape, axis)


def token_of(t, rows, tokens):
    devices = tokens // rows
    return (t % devices) * rows + t // devices


def column_norm(values, gain):
    average = jnp.mean(values, axis=0, keepdims=True)
    centred = values - average
    variance = jnp.mean(centred * centred, axis=0, keepdims=True)
    return (centred * lax.rsqrt(variance + EPS) * gain).astype(BF16)


def position_permutation(rows, tokens, by_lane):
    size = rows * tokens
    shape = (size, size)
    lane = iota(shape, 0 if by_lane else 1)
    position = iota(shape, 1 if by_lane else 0)
    source = lane // tokens * tokens + token_of(lane % tokens, rows, tokens)
    return (source == position).astype(F32).astype(BF16)


def pack_kernel(rows, tokens, pair_ref, mask_ref, packed_ref):
    channels = pair_ref.shape[-1]
    size = rows * tokens
    permuted = dot(position_permutation(rows, tokens, True), pair_ref[...]).astype(BF16)
    identity = (iota((channels, channels), 0) == iota((channels, channels), 1)).astype(F32)
    packed_ref[0, :channels, :] = dot_nt(identity.astype(BF16), permuted).astype(BF16)
    lane = iota((tokens, size), 1)
    place = token_of(lane % tokens, rows, tokens) == iota((tokens, size), 0)
    spread = dot(mask_ref[...].astype(F32).astype(BF16), place.astype(F32).astype(BF16))
    own = iota((rows, size), 0) == iota((rows, size), 1) // tokens
    line = jnp.sum(jnp.where(own, spread, 0.0), axis=0, keepdims=True)
    packed_ref[0, channels:, :] = jnp.broadcast_to(line, (MASK_ROWS, size)).astype(BF16)


def prepare_kernel(
    rows, tokens, me_ref, proj_ref, gate_ref, out_ref, gain_ref, mid_ref,
    proj_t_ref, gate_t_ref, out_t_ref, gain_t_ref, mid_t_ref, restore_ref, spread_ref,
):
    devices = tokens // rows

    def flipped(weight):
        return weight.astype(F32).T.astype(BF16)

    def column(line):
        return jnp.broadcast_to(line, (LANES, line.shape[1])).T

    for o in range(2):
        proj_t_ref[o] = flipped(proj_ref[o])
        gate_t_ref[o] = flipped(gate_ref[o])
        out_t_ref[o] = flipped(out_ref[o])
        gain_t_ref[o] = column(gain_ref[o : o + 1, :])
        mid_t_ref[o] = column(mid_ref[o : o + 1, :])
    restore_ref[...] = position_permutation(rows, tokens, False)
    shape = (LANES, LANES)
    group, lane = iota(shape, 0) // tokens, iota(shape, 0) % tokens
    same = group == iota(shape, 1) // tokens
    for i in range(rows):
        spread_ref[i] = (same & (lane == i * devices + me_ref[0])).astype(F32).astype(BF16)


def both_kernel(rows, tokens, sources, me_ref, *refs):
    devices = tokens // rows
    block_refs, refs = refs[: len(sources)], refs[len(sources) :]
    weight_refs, result_ref, refs = refs[:7], refs[7], refs[8:]
    weights, refs = refs[:7], refs[7:]
    (
        packed_s, left_s, right_s, normed_s, sum_s, now_s, second_left_s, second_right_s,
        block_sem, weight_sem,
    ) = refs
    proj_ref, gate_ref, out_ref, gain_ref, mid_ref, restore_ref, spread_ref = weights
    channels = gate_ref.shape[1]
    hw = mid_ref.shape[1]
    tiles = rows * tokens // LANES
    me = me_ref[0]

    weight_copies = [
        pltpu.make_async_copy(weight_refs[n], weights[n], weight_sem.at[n]) for n in range(7)
    ]
    block_copies = {}
    for block_ref, held in zip(block_refs, sources):
        for k, m in enumerate(held):
            block_copies[m] = pltpu.make_async_copy(
                block_ref.at[k], packed_s.at[me ^ m], block_sem.at[m]
            )
    for n in (0, 3):
        weight_copies[n].start()
    for m in range(devices):
        block_copies[m].start()
    for n in (1, 2, 4, 5, 6):
        weight_copies[n].start()
    for n in range(7):
        weight_copies[n].wait()
    for m in range(devices):
        block_copies[m].wait()

    def factors(projected, mask):
        left = mask * sigmoid(projected[hw : 2 * hw]) * projected[:hw]
        right = mask * sigmoid(projected[3 * hw :]) * projected[2 * hw : 3 * hw]
        return left, right

    def block_of(b, h):
        return packed_s[b, :channels, h * LANES : (h + 1) * LANES].astype(F32)

    def mask_of(b, h):
        rows_of_mask = packed_s[b, channels:, h * LANES : (h + 1) * LANES]
        return rows_of_mask.astype(F32)[:1]

    def project_first(b, _):
        for h in range(tiles):
            normed = column_norm(block_of(b, h), gain_ref[0])
            normed_s[b * tiles + h] = normed
            left, right = factors(dot(proj_ref[0], normed), mask_of(b, h))
            here = pl.ds(pl.multiple_of(b * hw, hw), hw)
            left_s[h, here, :] = left
            right_s[h, here, :] = right
        return 0

    lax.fori_loop(0, devices, project_first, 0, unroll=2)

    low = iota((devices, LANES), 1) < tokens

    def channel_sum(c, _):
        here = pl.ds(c, devices, stride=hw)
        left = jnp.concatenate([left_s[h, here, :] for h in range(tiles)], axis=0)
        halves = [[], []]
        for h in range(tiles):
            right = right_s[h, here, :]
            turned = pltpu.roll(right, tokens, 1)
            for q in range(2):
                straight, other = (right, turned) if q == 0 else (turned, right)
                halves[0].append(jnp.where(low, straight, 0.0))
                halves[1].append(jnp.where(low, 0.0, other))
        against = jnp.concatenate(halves[0] + halves[1], axis=0).astype(BF16)
        here = pl.ds(pl.multiple_of(c * tiles * devices, tiles * devices), tiles * devices)
        sum_s[here, :] = dot_nt(left.astype(BF16), against)
        return 0

    lax.fori_loop(0, hw, channel_sum, 0, unroll=8)

    def second_factors(b, _):
        for h in range(tiles):
            summed = sum_s[pl.ds(h * devices + b, hw, stride=tiles * devices), :]
            update = dot(out_ref[0], column_norm(summed, mid_ref[0]))
            gating = sigmoid(dot(gate_ref[0], normed_s[b * tiles + h]))
            now = (block_of(b, h) + gating * update).astype(BF16)
            now_s[b * tiles + h] = now
            normed = column_norm(now.astype(F32), gain_ref[1])
            normed_s[b * tiles + h] = normed
            left, right = factors(dot(proj_ref[1], normed), mask_of(b, h))
            here = pl.ds(pl.multiple_of((b * tiles + h) * hw, hw), hw)
            second_left_s[here, :] = left.astype(BF16)
            second_right_s[here, :] = right.astype(BF16)
        return 0

    lax.fori_loop(0, devices, second_factors, 0, unroll=2)

    depth = 4 * hw
    sums = []
    for i in range(rows):

        def add(n, total):
            here = pl.ds(pl.multiple_of(n * depth, depth), depth)
            terms = dot(second_left_s[here, :], spread_ref[i]) * second_right_s[here, :].astype(F32)
            return total + sum(terms[k * hw : (k + 1) * hw] for k in range(4))

        total = lax.fori_loop(
            0, devices * tiles // 4, add, jnp.zeros((hw, LANES), F32), unroll=2
        )
        sums.append(total + pltpu.roll(total, tokens, 1))
    low = iota((hw, LANES), 1) < tokens
    final = []
    for h in range(tiles):
        summed = jnp.where(low, sums[2 * h], sums[2 * h + 1])
        update = dot(out_ref[1], column_norm(summed, mid_ref[1]))
        gating = sigmoid(dot(gate_ref[1], normed_s[me * tiles + h]))
        final.append((now_s[me * tiles + h].astype(F32) + gating * update).astype(BF16))
    final = jnp.concatenate(final, axis=1)
    result_ref[...] = dot_nt(restore_ref[...], final).astype(BF16)


def exchange(block, partner_bits, devices):
    pairs = [(d, d ^ partner_bits) for d in range(devices)]
    return lax.ppermute(block, "row", pairs)


def everyone(packed, ready, devices):
    far = {m: exchange(packed, m, devices) for m in range(4, devices, 4)}
    beside = exchange(packed, 2, devices)
    far[12], ready = lax.optimization_barrier((far[12], ready))
    near = exchange(far[4], 2, devices)
    rest = exchange(jnp.concatenate([far[8], far[12]]), 2, devices)
    first = jnp.concatenate([packed, beside] + [far[m] for m in sorted(far)])
    second = jnp.concatenate([near, rest])
    arrays = [packed, beside, far[4], far[8], far[12], near, rest]
    sources = [(0,), (2,), (4,), (8,), (12,), (6,), (10, 14)]
    arrays += [exchange(first, 1, devices), exchange(second, 1, devices)]
    sources += [(1, 3, 5, 9, 13), (7, 11, 15)]
    return arrays, sources, ready


def small_plan(pair, mask, proj, gate, out, gain, mid):
    rows, tokens, channels = pair.shape
    devices, size, hw = tokens // rows, rows * tokens, out.shape[1]
    index = pl.BlockSpec(memory_space=pltpu.SMEM)
    anywhere = pl.BlockSpec(memory_space=pl.ANY)
    packed = pl.pallas_call(
        functools.partial(pack_kernel, rows, tokens),
        out_shape=jax.ShapeDtypeStruct((1, channels + MASK_ROWS, size), BF16),
        name="pack",
    )(pair.reshape(size, channels), mask)
    me = lax.axis_index("row").reshape(1).astype(jnp.int32)
    weights = pl.pallas_call(
        functools.partial(prepare_kernel, rows, tokens),
        in_specs=[index] + [pl.BlockSpec()] * 5,
        out_shape=(
            jax.ShapeDtypeStruct((2, 4 * hw, channels), BF16),
            jax.ShapeDtypeStruct((2, channels, channels), BF16),
            jax.ShapeDtypeStruct((2, channels, hw), BF16),
            jax.ShapeDtypeStruct((2, channels, LANES), F32),
            jax.ShapeDtypeStruct((2, hw, LANES), F32),
            jax.ShapeDtypeStruct((size, size), BF16),
            jax.ShapeDtypeStruct((rows, LANES, LANES), BF16),
        ),
        name="prepare",
    )(me, proj, gate, out, gain, mid)
    arrays, sources, weights = everyone(packed, weights, devices)
    chunks = devices * size // LANES
    result = pl.pallas_call(
        functools.partial(both_kernel, rows, tokens, sources),
        out_shape=jax.ShapeDtypeStruct((size, channels), BF16),
        in_specs=[index] + [anywhere] * (len(arrays) + len(weights)),
        scratch_shapes=[pltpu.VMEM(w.shape, w.dtype) for w in weights]
        + [
            pltpu.VMEM((devices,) + packed.shape[1:], BF16),
            pltpu.VMEM((size // LANES, devices * hw, LANES), F32),
            pltpu.VMEM((size // LANES, devices * hw, LANES), F32),
            pltpu.VMEM((chunks, channels, LANES), BF16),
            pltpu.VMEM((hw * chunks, LANES), F32),
            pltpu.VMEM((chunks, channels, LANES), BF16),
            pltpu.VMEM((chunks * hw, LANES), BF16),
            pltpu.VMEM((chunks * hw, LANES), BF16),
            pltpu.SemaphoreType.DMA((devices,)),
            pltpu.SemaphoreType.DMA((len(weights),)),
        ],
        compiler_params=pltpu.CompilerParams(vmem_limit_bytes=40 * 1024 * 1024),
        name="both",
    )(me, *arrays, *weights)
    return result.reshape(pair.shape)


def layer_norm(values, gain, axis):
    average = jnp.mean(values, axis=axis, keepdims=True)
    centred = values - average
    variance = jnp.mean(centred * centred, axis=axis, keepdims=True)
    return centred * lax.rsqrt(variance + EPS) * gain


def factors(normed, mask, proj):
    hw = proj.shape[1] // 4
    projected = jnp.einsum("ijd,de->eij", normed, proj, preferred_element_type=F32)
    left = mask * jax.nn.sigmoid(projected[hw : 2 * hw]) * projected[:hw]
    right = mask * jax.nn.sigmoid(projected[3 * hw :]) * projected[2 * hw : 3 * hw]
    return left.astype(BF16), right.astype(BF16)


def gathered_update(pair, mask, proj, gate, out, gain, mid, orient):
    rows, tokens, _ = pair.shape
    devices = tokens // rows
    floats = pair.astype(F32)
    normed = layer_norm(floats, gain, -1).astype(BF16)
    left, right = factors(normed, mask, proj)
    everywhere = lax.all_gather(right, "row", axis=1, tiled=True)
    if orient == 1:
        c = left.shape[0]
        blocks = left.reshape(c, rows, devices, rows).transpose(2, 1, 3, 0)
        left = lax.all_to_all(blocks, "row", 0, 0, tiled=True)
        left = left.reshape(tokens, rows, c).transpose(2, 0, 1)
    spec = "cik,cjk->cij" if orient == 0 else "cki,ckj->cij"
    summed = jnp.einsum(spec, left, everywhere, preferred_element_type=F32)
    hidden = layer_norm(summed, mid[:, None, None], 0).astype(BF16)
    gating = jax.nn.sigmoid(jnp.einsum("ijd,de->ije", normed, gate, preferred_element_type=F32))
    update = jnp.einsum("cij,cd->ijd", hidden, out, preferred_element_type=F32)
    return (floats + gating * update).astype(BF16)


def shards(pair, pair_mask, proj, gate, out, gain, mid):
    rows, tokens, _ = pair.shape
    if rows == 4 and 2 * tokens == LANES:
        return small_plan(pair, pair_mask, proj, gate, out, gain, mid)
    mask = pair_mask.astype(F32)[None]
    for o in range(2):
        pair = gathered_update(pair, mask, proj[o], gate[o], out[o], gain[o], mid[o], o)
    return pair


def solution(mesh):
    return jax.shard_map(
        shards,
        mesh=mesh,
        in_specs=(P(("groups", "row")), P(("groups", "row")), P(), P(), P(), P(), P()),
        out_specs=P(("groups", "row")),
        check_vma=False,
    )
```

```python
import functools

import jax
import jax.numpy as jnp
from jax import lax
from jax.experimental import pallas as pl
from jax.experimental.pallas import tpu as pltpu
from jax.sharding import PartitionSpec as P

EPS = 1e-05
F32, BF16 = jnp.float32, jnp.bfloat16
LANES = 128
MASK_ROWS = 16
NT = (((1,), (1,)), ((), ()))


def dot(a, b):
    return jnp.dot(a, b, preferred_element_type=F32)


def dot_nt(a, b):
    return lax.dot_general(a, b, NT, preferred_element_type=F32)


def sigmoid(x):
    return 0.5 * jnp.tanh(0.5 * x) + 0.5


def iota(shape, axis):
    return lax.broadcasted_iota(jnp.int32, shape, axis)


def token_of(t, rows, tokens):
    devices = tokens // rows
    return (t % devices) * rows + t // devices


def column_norm(values, gain):
    average = jnp.mean(values, axis=0, keepdims=True)
    centred = values - average
    variance = jnp.mean(centred * centred, axis=0, keepdims=True)
    return (centred * lax.rsqrt(variance + EPS) * gain).astype(BF16)


def position_permutation(rows, tokens, by_lane):
    size = rows * tokens
    shape = (size, size)
    lane = iota(shape, 0 if by_lane else 1)
    position = iota(shape, 1 if by_lane else 0)
    source = lane // tokens * tokens + token_of(lane % tokens, rows, tokens)
    return (source == position).astype(F32).astype(BF16)


def pack_kernel(rows, tokens, pair_ref, mask_ref, packed_ref):
    channels = pair_ref.shape[-1]
    size = rows * tokens
    permuted = dot(position_permutation(rows, tokens, True), pair_ref[...]).astype(BF16)
    identity = (iota((channels, channels), 0) == iota((channels, channels), 1)).astype(F32)
    packed_ref[0, :channels, :] = dot_nt(identity.astype(BF16), permuted).astype(BF16)
    lane = iota((tokens, size), 1)
    place = token_of(lane % tokens, rows, tokens) == iota((tokens, size), 0)
    spread = dot(mask_ref[...].astype(F32).astype(BF16), place.astype(F32).astype(BF16))
    own = iota((rows, size), 0) == iota((rows, size), 1) // tokens
    line = jnp.sum(jnp.where(own, spread, 0.0), axis=0, keepdims=True)
    packed_ref[0, channels:, :] = jnp.broadcast_to(line, (MASK_ROWS, size)).astype(BF16)


def prepare_kernel(
    rows, tokens, me_ref, proj_ref, gate_ref, out_ref, gain_ref, mid_ref,
    proj_t_ref, gate_t_ref, out_t_ref, gain_t_ref, mid_t_ref, restore_ref, spread_ref,
):
    devices = tokens // rows

    def flipped(weight):
        return weight.astype(F32).T.astype(BF16)

    def column(line):
        return jnp.broadcast_to(line, (LANES, line.shape[1])).T

    for o in range(2):
        proj_t_ref[o] = flipped(proj_ref[o])
        gate_t_ref[o] = flipped(gate_ref[o])
        out_t_ref[o] = flipped(out_ref[o])
        gain_t_ref[o] = column(gain_ref[o : o + 1, :])
        mid_t_ref[o] = column(mid_ref[o : o + 1, :])
    restore_ref[...] = position_permutation(rows, tokens, False)
    shape = (LANES, LANES)
    group, lane = iota(shape, 0) // tokens, iota(shape, 0) % tokens
    same = group == iota(shape, 1) // tokens
    for i in range(rows):
        spread_ref[i] = (same & (lane == i * devices + me_ref[0])).astype(F32).astype(BF16)


def both_kernel(rows, tokens, sources, me_ref, *refs):
    devices = tokens // rows
    block_refs, refs = refs[: len(sources)], refs[len(sources) :]
    weight_refs, result_ref, refs = refs[:7], refs[7], refs[8:]
    weights, refs = refs[:7], refs[7:]
    (
        packed_s, left_s, right_s, normed_s, sum_s, now_s, second_left_s, second_right_s,
        block_sem, weight_sem,
    ) = refs
    proj_ref, gate_ref, out_ref, gain_ref, mid_ref, restore_ref, spread_ref = weights
    channels = gate_ref.shape[1]
    hw = mid_ref.shape[1]
    tiles = rows * tokens // LANES
    me = me_ref[0]

    weight_copies = [
        pltpu.make_async_copy(weight_refs[n], weights[n], weight_sem.at[n]) for n in range(7)
    ]
    block_copies = {}
    for block_ref, held in zip(block_refs, sources):
        for k, m in enumerate(held):
            block_copies[m] = pltpu.make_async_copy(
                block_ref.at[k], packed_s.at[me ^ m], block_sem.at[m]
            )
    for n in (0, 3):
        weight_copies[n].start()
    for m in range(devices):
        block_copies[m].start()
    for n in (1, 2, 4, 5, 6):
        weight_copies[n].start()
    for n in range(7):
        weight_copies[n].wait()
    for m in range(devices):
        block_copies[m].wait()

    def factors(projected, mask):
        left = mask * sigmoid(projected[hw : 2 * hw]) * projected[:hw]
        right = mask * sigmoid(projected[3 * hw :]) * projected[2 * hw : 3 * hw]
        return left, right

    def block_of(b, h):
        return packed_s[b, :channels, h * LANES : (h + 1) * LANES].astype(F32)

    def mask_of(b, h):
        rows_of_mask = packed_s[b, channels:, h * LANES : (h + 1) * LANES]
        return rows_of_mask.astype(F32)[:1]

    def project_first(b, _):
        for h in range(tiles):
            normed = column_norm(block_of(b, h), gain_ref[0])
            normed_s[b * tiles + h] = normed
            left, right = factors(dot(proj_ref[0], normed), mask_of(b, h))
            here = pl.ds(b * hw, hw)
            left_s[h, here, :] = left
            right_s[h, here, :] = right
        return 0

    for b in range(devices):
        project_first(b, 0)

    low = iota((devices, LANES), 1) < tokens

    def channel_sum(c, _):
        here = pl.ds(c, devices, stride=hw)
        left = jnp.concatenate([left_s[h, here, :] for h in range(tiles)], axis=0)
        halves = [[], []]
        for h in range(tiles):
            right = right_s[h, here, :]
            turned = pltpu.roll(right, tokens, 1)
            for q in range(2):
                straight, other = (right, turned) if q == 0 else (turned, right)
                halves[0].append(jnp.where(low, straight, 0.0))
                halves[1].append(jnp.where(low, 0.0, other))
        against = jnp.concatenate(halves[0] + halves[1], axis=0).astype(BF16)
        here = pl.ds(pl.multiple_of(c * tiles * devices, tiles * devices), tiles * devices)
        sum_s[here, :] = dot_nt(left.astype(BF16), against)
        return 0

    lax.fori_loop(0, hw, channel_sum, 0, unroll=16)

    def second_factors(b, _):
        for h in range(tiles):
            summed = sum_s[pl.ds(h * devices + b, hw, stride=tiles * devices), :]
            update = dot(out_ref[0], column_norm(summed, mid_ref[0]))
            gating = sigmoid(dot(gate_ref[0], normed_s[b * tiles + h]))
            now = (block_of(b, h) + gating * update).astype(BF16)
            now_s[b * tiles + h] = now
            normed = column_norm(now.astype(F32), gain_ref[1])
            normed_s[b * tiles + h] = normed
            left, right = factors(dot(proj_ref[1], normed), mask_of(b, h))
            here = pl.ds((b * tiles + h) * hw, hw)
            second_left_s[here, :] = left.astype(BF16)
            second_right_s[here, :] = right.astype(BF16)
        return 0

    for b in range(devices):
        second_factors(b, 0)

    depth = 4 * hw
    sums = []
    for i in range(rows):

        def add(n, total):
            here = pl.ds(n * depth, depth)
            terms = dot(second_left_s[here, :], spread_ref[i]) * second_right_s[here, :].astype(F32)
            return total + sum(terms[k * hw : (k + 1) * hw] for k in range(4))

        total = lax.fori_loop(
            0, devices * tiles // 4, add, jnp.zeros((hw, LANES), F32), unroll=True
        )
        sums.append(total + pltpu.roll(total, tokens, 1))
    low = iota((hw, LANES), 1) < tokens
    final = []
    for h in range(tiles):
        summed = jnp.where(low, sums[2 * h], sums[2 * h + 1])
        update = dot(out_ref[1], column_norm(summed, mid_ref[1]))
        gating = sigmoid(dot(gate_ref[1], normed_s[me * tiles + h]))
        final.append((now_s[me * tiles + h].astype(F32) + gating * update).astype(BF16))
    final = jnp.concatenate(final, axis=1)
    result_ref[...] = dot_nt(restore_ref[...], final).astype(BF16)


def exchange(block, partner_bits, devices):
    pairs = [(d, d ^ partner_bits) for d in range(devices)]
    return lax.ppermute(block, "row", pairs)


def everyone(packed, ready, devices):
    held = {0: packed}
    for m in (4, 2, 8, 12):
        held[m] = exchange(packed, m, devices)
    held[4], held[2] = lax.optimization_barrier((held[4], held[2]))
    held[6] = exchange(held[4], 2, devices)
    held[8], held[4], ready = lax.optimization_barrier((held[8], held[4], ready))
    held[10] = exchange(held[8], 2, devices)
    held[12], held[6] = lax.optimization_barrier((held[12], held[6]))
    held[14] = exchange(held[12], 2, devices)
    arrays = [held[m] for m in sorted(held)]
    sources = [(m,) for m in sorted(held)]
    for group in ((0, 2, 4), (6, 8), (10, 12, 14)):
        arrays.append(exchange(jnp.concatenate([held[m] for m in group]), 1, devices))
        sources.append(tuple(m ^ 1 for m in group))
    return arrays, sources, ready


def small_plan(pair, mask, proj, gate, out, gain, mid):
    rows, tokens, channels = pair.shape
    devices, size, hw = tokens // rows, rows * tokens, out.shape[1]
    index = pl.BlockSpec(memory_space=pltpu.SMEM)
    anywhere = pl.BlockSpec(memory_space=pl.ANY)
    packed = pl.pallas_call(
        functools.partial(pack_kernel, rows, tokens),
        out_shape=jax.ShapeDtypeStruct((1, channels + MASK_ROWS, size), BF16),
        name="pack",
    )(pair.reshape(size, channels), mask)
    me = lax.axis_index("row").reshape(1).astype(jnp.int32)
    weights = pl.pallas_call(
        functools.partial(prepare_kernel, rows, tokens),
        in_specs=[index] + [pl.BlockSpec()] * 5,
        out_shape=(
            jax.ShapeDtypeStruct((2, 4 * hw, channels), BF16),
            jax.ShapeDtypeStruct((2, channels, channels), BF16),
            jax.ShapeDtypeStruct((2, channels, hw), BF16),
            jax.ShapeDtypeStruct((2, channels, LANES), F32),
            jax.ShapeDtypeStruct((2, hw, LANES), F32),
            jax.ShapeDtypeStruct((size, size), BF16),
            jax.ShapeDtypeStruct((rows, LANES, LANES), BF16),
        ),
        name="prepare",
    )(me, proj, gate, out, gain, mid)
    arrays, sources, weights = everyone(packed, weights, devices)
    chunks = devices * size // LANES
    result = pl.pallas_call(
        functools.partial(both_kernel, rows, tokens, sources),
        out_shape=jax.ShapeDtypeStruct((size, channels), BF16),
        in_specs=[index] + [anywhere] * (len(arrays) + len(weights)),
        scratch_shapes=[pltpu.VMEM(w.shape, w.dtype) for w in weights]
        + [
            pltpu.VMEM((devices,) + packed.shape[1:], BF16),
            pltpu.VMEM((size // LANES, devices * hw, LANES), F32),
            pltpu.VMEM((size // LANES, devices * hw, LANES), F32),
            pltpu.VMEM((chunks, channels, LANES), BF16),
            pltpu.VMEM((hw * chunks, LANES), F32),
            pltpu.VMEM((chunks, channels, LANES), BF16),
            pltpu.VMEM((chunks * hw, LANES), BF16),
            pltpu.VMEM((chunks * hw, LANES), BF16),
            pltpu.SemaphoreType.DMA((devices,)),
            pltpu.SemaphoreType.DMA((len(weights),)),
        ],
        compiler_params=pltpu.CompilerParams(vmem_limit_bytes=40 * 1024 * 1024),
        name="both",
    )(me, *arrays, *weights)
    return result.reshape(pair.shape)


def layer_norm(values, gain, axis):
    average = jnp.mean(values, axis=axis, keepdims=True)
    centred = values - average
    variance = jnp.mean(centred * centred, axis=axis, keepdims=True)
    return centred * lax.rsqrt(variance + EPS) * gain


def factors(normed, mask, proj):
    hw = proj.shape[1] // 4
    projected = jnp.einsum("ijd,de->eij", normed, proj, preferred_element_type=F32)
    left = mask * jax.nn.sigmoid(projected[hw : 2 * hw]) * projected[:hw]
    right = mask * jax.nn.sigmoid(projected[3 * hw :]) * projected[2 * hw : 3 * hw]
    return left.astype(BF16), right.astype(BF16)


def gathered_update(pair, mask, proj, gate, out, gain, mid, orient):
    rows, tokens, _ = pair.shape
    devices = tokens // rows
    floats = pair.astype(F32)
    normed = layer_norm(floats, gain, -1).astype(BF16)
    left, right = factors(normed, mask, proj)
    everywhere = lax.all_gather(right, "row", axis=1, tiled=True)
    if orient == 1:
        c = left.shape[0]
        blocks = left.reshape(c, rows, devices, rows).transpose(2, 1, 3, 0)
        left = lax.all_to_all(blocks, "row", 0, 0, tiled=True)
        left = left.reshape(tokens, rows, c).transpose(2, 0, 1)
    spec = "cik,cjk->cij" if orient == 0 else "cki,ckj->cij"
    summed = jnp.einsum(spec, left, everywhere, preferred_element_type=F32)
    hidden = layer_norm(summed, mid[:, None, None], 0).astype(BF16)
    gating = jax.nn.sigmoid(jnp.einsum("ijd,de->ije", normed, gate, preferred_element_type=F32))
    update = jnp.einsum("cij,cd->ijd", hidden, out, preferred_element_type=F32)
    return (floats + gating * update).astype(BF16)


def shards(pair, pair_mask, proj, gate, out, gain, mid):
    rows, tokens, _ = pair.shape
    if rows == 4 and 2 * tokens == LANES:
        return small_plan(pair, pair_mask, proj, gate, out, gain, mid)
    mask = pair_mask.astype(F32)[None]
    for o in range(2):
        pair = gathered_update(pair, mask, proj[o], gate[o], out[o], gain[o], mid[o], o)
    return pair


def solution(mesh):
    return jax.shard_map(
        shards,
        mesh=mesh,
        in_specs=(P(("groups", "row")), P(("groups", "row")), P(), P(), P(), P(), P()),
        out_specs=P(("groups", "row")),
        check_vma=False,
    )
```

```python
import functools

import jax
import jax.numpy as jnp
from jax import lax
from jax.experimental import pallas as pl
from jax.experimental.pallas import tpu as pltpu
from jax.sharding import PartitionSpec as P

EPS = 1e-05
F32, BF16 = jnp.float32, jnp.bfloat16
LANES = 128
MASK_ROWS = 16
NT = (((1,), (1,)), ((), ()))
VMEM = pltpu.VMEM
IN_VMEM = pl.BlockSpec(memory_space=pltpu.VMEM)
IN_SMEM = pl.BlockSpec(memory_space=pltpu.SMEM)


def dot(a, b):
    return jnp.dot(a, b, preferred_element_type=F32)


def dot_nt(a, b):
    return lax.dot_general(a, b, NT, preferred_element_type=F32)


def sigmoid(x):
    return 0.5 * jnp.tanh(0.5 * x) + 0.5


def iota(shape, axis):
    return lax.broadcasted_iota(jnp.int32, shape, axis)


def one_hot(condition):
    return condition.astype(F32).astype(BF16)


def token_of(t, rows, tokens):
    devices = tokens // rows
    return (t % devices) * rows + t // devices


def column_norm(values, gain):
    average = jnp.mean(values, axis=0, keepdims=True)
    centred = values - average
    variance = jnp.mean(centred * centred, axis=0, keepdims=True)
    return (centred * lax.rsqrt(variance + EPS) * gain).astype(BF16)


def factors(projected, mask):
    hw = projected.shape[0] // 4
    left = mask * sigmoid(projected[hw : 2 * hw]) * projected[:hw]
    right = mask * sigmoid(projected[3 * hw :]) * projected[2 * hw : 3 * hw]
    return left, right


def pack_kernel(rows, tokens, pair_ref, mask_ref, packed_ref):
    channels = pair_ref.shape[-1]
    square = (tokens, tokens)
    by_lane = one_hot(token_of(iota(square, 0), rows, tokens) == iota(square, 1))
    by_token = one_hot(token_of(iota(square, 1), rows, tokens) == iota(square, 0))
    identity = one_hot(iota((channels, channels), 0) == iota((channels, channels), 1))
    masks = dot(one_hot(mask_ref[...] != 0), by_token)
    tiles = rows * tokens // LANES
    for h in range(tiles):
        pair = [dot(by_lane, pair_ref[i]).astype(BF16) for i in (2 * h, 2 * h + 1)]
        chunk = dot_nt(identity, jnp.concatenate(pair, axis=0))
        packed_ref[0, h * channels : (h + 1) * channels, :] = chunk.astype(BF16)
    lines = [
        jnp.concatenate([masks[2 * h : 2 * h + 1], masks[2 * h + 1 : 2 * h + 2]], axis=1)
        for h in range(tiles)
    ]
    shape = (MASK_ROWS, LANES)
    block = jnp.where(iota(shape, 0) < MASK_ROWS // 2, lines[0], lines[1])
    packed_ref[0, tiles * channels :, :] = block.astype(BF16)


def chunk_of(ref, channels, k, h):
    return ref[k, h * channels : (h + 1) * channels, :].astype(F32)


def mask_of(ref, channels, k, h):
    lines = ref[k, -MASK_ROWS:, :].astype(F32)
    return lines[h * MASK_ROWS // 2 : h * MASK_ROWS // 2 + 1]


def prepare_kernel(
    rows, tokens, me_ref, proj_ref, gate_ref, out_ref, gain_ref, mid_ref,
    proj_t_ref, gate_t_ref, out_t_ref, gain_t_ref, mid_t_ref, restore_ref, spread_ref,
):
    devices = tokens // rows

    def flipped(weight):
        return weight.astype(F32).T.astype(BF16)

    def column(line):
        return jnp.broadcast_to(line, (LANES, line.shape[1])).T

    for o in range(2):
        proj_t_ref[o] = flipped(proj_ref[o])
        gate_t_ref[o] = flipped(gate_ref[o])
        out_t_ref[o] = flipped(out_ref[o])
        gain_t_ref[o] = column(gain_ref[o : o + 1, :])
        mid_t_ref[o] = column(mid_ref[o : o + 1, :])
    shape = (LANES, LANES)
    lane = iota(shape, 1)
    source = lane // tokens * tokens + token_of(lane % tokens, rows, tokens)
    restore_ref[...] = one_hot(source == iota(shape, 0))
    group, lane = iota(shape, 0) // tokens, iota(shape, 0) % tokens
    same = group == iota(shape, 1) // tokens
    for i in range(rows):
        spread_ref[i] = one_hot(same & (lane == i * devices + me_ref[0]))


def early_kernel(counts, *refs):
    block_refs, (proj_ref, gain_ref, left_ref, right_ref, normed_ref) = refs[:-5], refs[-5:]
    channels, tiles = normed_ref.shape[2], normed_ref.shape[1]
    place = 0
    for block_ref, count in zip(block_refs, counts):
        for k in range(count):
            for h in range(tiles):
                normed = column_norm(chunk_of(block_ref, channels, k, h), gain_ref[0])
                normed_ref[place, h] = normed
                left, right = factors(dot(proj_ref[0], normed), mask_of(block_ref, channels, k, h))
                left_ref[place, h] = left
                right_ref[place, h] = right
            place += 1


def both_kernel(rows, tokens, sources, early, me_ref, *refs):
    devices = tokens // rows
    block_refs, refs = refs[: len(sources)], refs[len(sources) :]
    (
        proj_ref, gate_ref, out_ref, gain_ref, mid_ref, restore_ref, spread_ref,
        early_left_ref, early_right_ref, early_normed_ref, result_ref,
        left_s, right_s, normed_s, sum_s, now_s, second_left_s, second_right_s,
    ) = refs
    channels = gate_ref.shape[1]
    hw = mid_ref.shape[1]
    tiles = rows * tokens // LANES
    me = me_ref[0]

    where = {m: (ref, k) for ref, held in zip(block_refs, sources) for k, m in enumerate(held)}
    later = [m for m in range(devices) if m not in early]

    def place(m, h, left, right):
        here = pl.ds(pl.multiple_of((me ^ m) * hw, hw), hw)
        left_s[h, here, :] = left
        right_s[h, here, :] = right

    for m in later:
        for h in range(tiles):
            ref, k = where[m]
            normed = column_norm(chunk_of(ref, channels, k, h), gain_ref[0])
            normed_s[later.index(m), h] = normed
            place(m, h, *factors(dot(proj_ref[0], normed), mask_of(ref, channels, k, h)))
    for n, m in enumerate(early):
        for h in range(tiles):
            place(m, h, early_left_ref[n, h], early_right_ref[n, h])

    low = iota((devices, LANES), 1) < tokens

    def channel_sum(c, _):
        here = pl.ds(c, devices, stride=hw)
        left = jnp.concatenate([left_s[h, here, :] for h in range(tiles)], axis=0)
        halves = [[], []]
        for h in range(tiles):
            right = right_s[h, here, :]
            turned = pltpu.roll(right, tokens, 1)
            for q in range(2):
                straight, other = (right, turned) if q == 0 else (turned, right)
                halves[0].append(jnp.where(low, straight, 0.0))
                halves[1].append(jnp.where(low, 0.0, other))
        against = jnp.concatenate(halves[0] + halves[1], axis=0).astype(BF16)
        here = pl.ds(pl.multiple_of(c * tiles * devices, tiles * devices), tiles * devices)
        sum_s[here, :] = dot_nt(left.astype(BF16), against)
        return 0

    lax.fori_loop(0, hw, channel_sum, 0, unroll=16)

    for m in range(devices):
        for h in range(tiles):
            ref, k = where[m]
            first = early_normed_ref[early.index(m), h] if m in early else normed_s[later.index(m), h]
            summed = sum_s[pl.ds(h * devices + (me ^ m), hw, stride=tiles * devices), :]
            update = dot(out_ref[0], column_norm(summed, mid_ref[0]))
            gating = sigmoid(dot(gate_ref[0], first))
            now = (chunk_of(ref, channels, k, h) + gating * update).astype(BF16)
            normed = column_norm(now.astype(F32), gain_ref[1])
            if m == 0:
                now_s[h] = now
                now_s[tiles + h] = normed
            left, right = factors(dot(proj_ref[1], normed), mask_of(ref, channels, k, h))
            here = pl.ds((m * tiles + h) * hw, hw)
            second_left_s[here, :] = left.astype(BF16)
            second_right_s[here, :] = right.astype(BF16)

    depth = 4 * hw
    sums = []
    for i in range(rows):
        total = jnp.zeros((hw, LANES), F32)
        for n in range(devices * tiles // 4):
            here = pl.ds(n * depth, depth)
            terms = dot(second_left_s[here, :], spread_ref[i]) * second_right_s[here, :].astype(F32)
            total = total + sum(terms[k * hw : (k + 1) * hw] for k in range(4))
        sums.append(total + pltpu.roll(total, tokens, 1))
    low = iota((hw, LANES), 1) < tokens
    for h in range(tiles):
        summed = jnp.where(low, sums[2 * h], sums[2 * h + 1])
        update = dot(out_ref[1], column_norm(summed, mid_ref[1]))
        gating = sigmoid(dot(gate_ref[1], now_s[tiles + h]))
        final = (now_s[h].astype(F32) + gating * update).astype(BF16)
        result_ref[h * LANES : (h + 1) * LANES, :] = dot_nt(restore_ref[...], final).astype(BF16)


def exchange(block, partner_bits, devices):
    pairs = [(d, d ^ partner_bits) for d in range(devices)]
    return lax.ppermute(block, "row", pairs)


def small_plan(pair, mask, proj, gate, out, gain, mid):
    rows, tokens, channels = pair.shape
    devices, size, hw = tokens // rows, rows * tokens, out.shape[1]
    tiles = size // LANES
    packed = pl.pallas_call(
        functools.partial(pack_kernel, rows, tokens),
        out_shape=VMEM((1, tiles * channels + MASK_ROWS, LANES), BF16),
        out_specs=IN_VMEM,
        name="pack",
    )(pair, mask)
    me = lax.axis_index("row").reshape(1).astype(jnp.int32)
    weights = pl.pallas_call(
        functools.partial(prepare_kernel, rows, tokens),
        in_specs=[IN_SMEM] + [pl.BlockSpec()] * 5,
        out_shape=(
            VMEM((2, 4 * hw, channels), BF16),
            VMEM((2, channels, channels), BF16),
            VMEM((2, channels, hw), BF16),
            VMEM((2, channels, LANES), F32),
            VMEM((2, hw, LANES), F32),
            VMEM((LANES, LANES), BF16),
            VMEM((rows, LANES, LANES), BF16),
        ),
        out_specs=(IN_VMEM,) * 7,
        name="prepare",
    )(me, proj, gate, out, gain, mid)

    def swapped(group):
        return exchange(jnp.concatenate([held[m] for m in group]), 1, devices)

    held = {0: packed}
    for m in (12, 8, 4, 2):
        held[m] = exchange(packed, m, devices)
    first = (0, 2, 4)
    held[2], weights = lax.optimization_barrier((held[2], weights))
    held[6] = exchange(held[2], 4, devices)
    swaps = [swapped(first)]
    held[8], held[12] = lax.optimization_barrier((held[8], held[12]))
    held[10] = exchange(held[8], 2, devices)
    held[14] = exchange(held[12], 2, devices)

    early = (0, 2, 4, 8, 12) + tuple(m ^ 1 for m in first)
    count = len(early)
    ahead = pl.pallas_call(
        functools.partial(early_kernel, (1,) * 5 + (len(first),)),
        in_specs=[IN_VMEM] * 8,
        out_shape=(
            VMEM((count, tiles, hw, LANES), F32),
            VMEM((count, tiles, hw, LANES), F32),
            VMEM((count, tiles, channels, LANES), BF16),
        ),
        out_specs=(IN_VMEM,) * 3,
        name="early",
    )(*[held[m] for m in (0, 2, 4, 8, 12)], swaps[0], weights[0], weights[3])
    held[10], ahead = lax.optimization_barrier((held[10], ahead))
    second = (6, 8, 10, 12, 14)
    swaps.append(swapped(second))

    arrays = [held[m] for m in sorted(held)] + swaps
    sources = [(m,) for m in sorted(held)]
    sources += [tuple(m ^ 1 for m in group) for group in (first, second)]
    result = pl.pallas_call(
        functools.partial(both_kernel, rows, tokens, sources, early),
        out_shape=jax.ShapeDtypeStruct((size, channels), BF16),
        in_specs=[IN_SMEM] + [IN_VMEM] * (len(arrays) + 10),
        scratch_shapes=[
            pltpu.VMEM((tiles, devices * hw, LANES), F32),
            pltpu.VMEM((tiles, devices * hw, LANES), F32),
            pltpu.VMEM((devices - count, tiles, channels, LANES), BF16),
            pltpu.VMEM((hw * devices * tiles, LANES), F32),
            pltpu.VMEM((2 * tiles, channels, LANES), BF16),
            pltpu.VMEM((devices * tiles * hw, LANES), BF16),
            pltpu.VMEM((devices * tiles * hw, LANES), BF16),
        ],
        compiler_params=pltpu.CompilerParams(vmem_limit_bytes=24 * 1024 * 1024),
        name="both",
    )(me, *arrays, *weights, *ahead)
    return result.reshape(pair.shape)


def layer_norm(values, gain, axis):
    average = jnp.mean(values, axis=axis, keepdims=True)
    centred = values - average
    variance = jnp.mean(centred * centred, axis=axis, keepdims=True)
    return centred * lax.rsqrt(variance + EPS) * gain


def wide_factors(normed, mask, proj):
    hw = proj.shape[1] // 4
    projected = jnp.einsum("ijd,de->eij", normed, proj, preferred_element_type=F32)
    left = mask * jax.nn.sigmoid(projected[hw : 2 * hw]) * projected[:hw]
    right = mask * jax.nn.sigmoid(projected[3 * hw :]) * projected[2 * hw : 3 * hw]
    return left.astype(BF16), right.astype(BF16)


def gathered_update(pair, mask, proj, gate, out, gain, mid, orient):
    rows, tokens, _ = pair.shape
    devices = tokens // rows
    floats = pair.astype(F32)
    normed = layer_norm(floats, gain, -1).astype(BF16)
    left, right = wide_factors(normed, mask, proj)
    everywhere = lax.all_gather(right, "row", axis=1, tiled=True)
    if orient == 1:
        c = left.shape[0]
        blocks = left.reshape(c, rows, devices, rows).transpose(2, 1, 3, 0)
        left = lax.all_to_all(blocks, "row", 0, 0, tiled=True)
        left = left.reshape(tokens, rows, c).transpose(2, 0, 1)
    spec = "cik,cjk->cij" if orient == 0 else "cki,ckj->cij"
    summed = jnp.einsum(spec, left, everywhere, preferred_element_type=F32)
    hidden = layer_norm(summed, mid[:, None, None], 0).astype(BF16)
    gating = jax.nn.sigmoid(jnp.einsum("ijd,de->ije", normed, gate, preferred_element_type=F32))
    update = jnp.einsum("cij,cd->ijd", hidden, out, preferred_element_type=F32)
    return (floats + gating * update).astype(BF16)


def shards(pair, pair_mask, proj, gate, out, gain, mid):
    rows, tokens, _ = pair.shape
    if rows == 4 and 2 * tokens == LANES:
        return small_plan(pair, pair_mask, proj, gate, out, gain, mid)
    mask = pair_mask.astype(F32)[None]
    for o in range(2):
        pair = gathered_update(pair, mask, proj[o], gate[o], out[o], gain[o], mid[o], o)
    return pair


def solution(mesh):
    return jax.shard_map(
        shards,
        mesh=mesh,
        in_specs=(P(("groups", "row")), P(("groups", "row")), P(), P(), P(), P(), P()),
        out_specs=P(("groups", "row")),
        check_vma=False,
    )
```

```python
import functools

import jax
import jax.numpy as jnp
from jax import lax
from jax.experimental import pallas as pl
from jax.experimental.pallas import tpu as pltpu
from jax.sharding import PartitionSpec as P

EPS = 1e-05
F32, BF16 = jnp.float32, jnp.bfloat16
LANES = 128
MASK_ROWS = 16
NT = (((1,), (1,)), ((), ()))
VMEM = pltpu.VMEM
IN_VMEM = pl.BlockSpec(memory_space=pltpu.VMEM)
IN_SMEM = pl.BlockSpec(memory_space=pltpu.SMEM)
SMALL = pltpu.CompilerParams(vmem_limit_bytes=8 * 1024 * 1024)


def dot(a, b):
    return jnp.dot(a, b, preferred_element_type=F32)


def dot_nt(a, b):
    return lax.dot_general(a, b, NT, preferred_element_type=F32)


def sigmoid(x):
    return 0.5 * jnp.tanh(0.5 * x) + 0.5


def iota(shape, axis):
    return lax.broadcasted_iota(jnp.int32, shape, axis)


def one_hot(condition):
    return condition.astype(F32).astype(BF16)


def token_of(t, rows, tokens):
    devices = tokens // rows
    return (t % devices) * rows + t // devices


def column_norm(values, gain):
    average = jnp.mean(values, axis=0, keepdims=True)
    centred = values - average
    variance = jnp.mean(centred * centred, axis=0, keepdims=True)
    return (centred * lax.rsqrt(variance + EPS) * gain).astype(BF16)


def factors(projected, mask):
    hw = projected.shape[0] // 4
    left = mask * sigmoid(projected[hw : 2 * hw]) * projected[:hw]
    right = mask * sigmoid(projected[3 * hw :]) * projected[2 * hw : 3 * hw]
    return left, right


def side_by_side(chunks):
    return jnp.concatenate(chunks, axis=1)


def tile(values, h):
    return values[:, h * LANES : (h + 1) * LANES]


def pack_kernel(rows, tokens, pair_ref, mask_ref, packed_ref):
    channels = pair_ref.shape[-1]
    square = (tokens, tokens)
    by_lane = one_hot(token_of(iota(square, 0), rows, tokens) == iota(square, 1))
    by_token = one_hot(token_of(iota(square, 1), rows, tokens) == iota(square, 0))
    identity = one_hot(iota((channels, channels), 0) == iota((channels, channels), 1))
    masks = dot(one_hot(mask_ref[...] != 0), by_token)
    tiles = rows * tokens // LANES
    for h in range(tiles):
        pair = [dot(by_lane, pair_ref[i]).astype(BF16) for i in (2 * h, 2 * h + 1)]
        chunk = dot_nt(identity, jnp.concatenate(pair, axis=0))
        packed_ref[0, h * channels : (h + 1) * channels, :] = chunk.astype(BF16)
    lines = [
        jnp.concatenate([masks[2 * h : 2 * h + 1], masks[2 * h + 1 : 2 * h + 2]], axis=1)
        for h in range(tiles)
    ]
    shape = (MASK_ROWS, LANES)
    block = jnp.where(iota(shape, 0) < MASK_ROWS // 2, lines[0], lines[1])
    packed_ref[0, tiles * channels :, :] = block.astype(BF16)


def chunk_of(ref, channels, k, h):
    return ref[k, h * channels : (h + 1) * channels, :].astype(F32)


def mask_of(ref, channels, k, h):
    lines = ref[k, -MASK_ROWS:, :].astype(F32)
    return lines[h * MASK_ROWS // 2 : h * MASK_ROWS // 2 + 1]


def prepare_kernel(
    rows, tokens, me_ref, proj_ref, gate_ref, out_ref, gain_ref, mid_ref,
    proj_t_ref, gate_t_ref, out_t_ref, gain_t_ref, mid_t_ref, restore_ref, spread_ref,
):
    devices = tokens // rows

    def flipped(weight):
        return weight.astype(F32).T.astype(BF16)

    def column(line):
        return jnp.broadcast_to(line, (LANES, line.shape[1])).T

    for o in range(2):
        proj_t_ref[o] = flipped(proj_ref[o])
        gate_t_ref[o] = flipped(gate_ref[o])
        out_t_ref[o] = flipped(out_ref[o])
        gain_t_ref[o] = column(gain_ref[o : o + 1, :])
        mid_t_ref[o] = column(mid_ref[o : o + 1, :])
    shape = (LANES, LANES)
    lane = iota(shape, 1)
    source = lane // tokens * tokens + token_of(lane % tokens, rows, tokens)
    restore_ref[...] = one_hot(source == iota(shape, 0))
    group, lane = iota(shape, 0) // tokens, iota(shape, 0) % tokens
    same = group == iota(shape, 1) // tokens
    for i in range(rows):
        spread_ref[i] = one_hot(same & (lane == i * devices + me_ref[0]))


def early_kernel(counts, *refs):
    block_refs, (proj_ref, gain_ref, left_ref, right_ref, normed_ref) = refs[:-5], refs[-5:]
    channels, tiles = normed_ref.shape[2], normed_ref.shape[1]
    place = 0
    for block_ref, count in zip(block_refs, counts):
        for k in range(count):
            normed = [
                column_norm(chunk_of(block_ref, channels, k, h), gain_ref[0]) for h in range(tiles)
            ]
            projected = dot(proj_ref[0], side_by_side(normed))
            for h in range(tiles):
                normed_ref[place, h] = normed[h]
                left, right = factors(tile(projected, h), mask_of(block_ref, channels, k, h))
                left_ref[place, h] = left
                right_ref[place, h] = right
            place += 1


def both_kernel(rows, tokens, sources, early, me_ref, *refs):
    devices = tokens // rows
    block_refs, refs = refs[: len(sources)], refs[len(sources) :]
    (
        proj_ref, gate_ref, out_ref, gain_ref, mid_ref, restore_ref, spread_ref,
        early_left_ref, early_right_ref, early_normed_ref, result_ref,
        left_s, right_s, normed_s, sum_s, now_s, second_left_s, second_right_s,
    ) = refs
    channels = gate_ref.shape[1]
    hw = mid_ref.shape[1]
    tiles = rows * tokens // LANES
    me = me_ref[0]

    where = {m: (ref, k) for ref, held in zip(block_refs, sources) for k, m in enumerate(held)}
    later = [m for m in range(devices) if m not in early]

    def place(m, h, left, right):
        here = pl.ds(pl.multiple_of((me ^ m) * hw, hw), hw)
        left_s[h, here, :] = left
        right_s[h, here, :] = right

    for m in later:
        ref, k = where[m]
        normed = [column_norm(chunk_of(ref, channels, k, h), gain_ref[0]) for h in range(tiles)]
        projected = dot(proj_ref[0], side_by_side(normed))
        for h in range(tiles):
            normed_s[later.index(m), h] = normed[h]
            place(m, h, *factors(tile(projected, h), mask_of(ref, channels, k, h)))
    for n, m in enumerate(early):
        for h in range(tiles):
            place(m, h, early_left_ref[n, h], early_right_ref[n, h])

    low = iota((devices, LANES), 1) < tokens

    def channel_sum(c, _):
        here = pl.ds(c, devices, stride=hw)
        left = jnp.concatenate([left_s[h, here, :] for h in range(tiles)], axis=0)
        halves = [[], []]
        for h in range(tiles):
            right = right_s[h, here, :]
            turned = pltpu.roll(right, tokens, 1)
            for q in range(2):
                straight, other = (right, turned) if q == 0 else (turned, right)
                halves[0].append(jnp.where(low, straight, 0.0))
                halves[1].append(jnp.where(low, 0.0, other))
        against = jnp.concatenate(halves[0] + halves[1], axis=0).astype(BF16)
        here = pl.ds(pl.multiple_of(c * tiles * devices, tiles * devices), tiles * devices)
        sum_s[here, :] = dot_nt(left.astype(BF16), against)
        return 0

    lax.fori_loop(0, hw, channel_sum, 0, unroll=16)

    for m in range(devices):
        ref, k = where[m]
        hidden, first = [], []
        for h in range(tiles):
            summed = sum_s[pl.ds(h * devices + (me ^ m), hw, stride=tiles * devices), :]
            hidden.append(column_norm(summed, mid_ref[0]))
            first.append(early_normed_ref[early.index(m), h] if m in early else normed_s[later.index(m), h])
        update = dot(out_ref[0], side_by_side(hidden))
        logits = dot(gate_ref[0], side_by_side(first))
        normed = []
        for h in range(tiles):
            gated = sigmoid(tile(logits, h)) * tile(update, h)
            now = (chunk_of(ref, channels, k, h) + gated).astype(BF16)
            normed.append(column_norm(now.astype(F32), gain_ref[1]))
            if m == 0:
                now_s[h] = now
                now_s[tiles + h] = normed[h]
        projected = dot(proj_ref[1], side_by_side(normed))
        for h in range(tiles):
            left, right = factors(tile(projected, h), mask_of(ref, channels, k, h))
            here = pl.ds((m * tiles + h) * hw, hw)
            second_left_s[here, :] = left.astype(BF16)
            second_right_s[here, :] = right.astype(BF16)

    depth = 2 * hw
    sums = []
    for i in range(0, rows, 2):
        pair = side_by_side([spread_ref[i], spread_ref[i + 1]])
        totals = [jnp.zeros((hw, LANES), F32)] * 2
        for n in range(devices * tiles // 2):
            here = pl.ds(n * depth, depth)
            spread = dot(second_left_s[here, :], pair)
            right = second_right_s[here, :].astype(F32)
            for o in range(2):
                terms = tile(spread, o) * right
                totals[o] = totals[o] + (terms[:hw] + terms[hw:])
        sums += [total + pltpu.roll(total, tokens, 1) for total in totals]
    low = iota((hw, LANES), 1) < tokens
    for h in range(tiles):
        summed = jnp.where(low, sums[2 * h], sums[2 * h + 1])
        update = dot(out_ref[1], column_norm(summed, mid_ref[1]))
        gating = sigmoid(dot(gate_ref[1], now_s[tiles + h]))
        final = (now_s[h].astype(F32) + gating * update).astype(BF16)
        result_ref[h * LANES : (h + 1) * LANES, :] = dot_nt(restore_ref[...], final).astype(BF16)


def exchange(block, partner_bits, devices):
    pairs = [(d, d ^ partner_bits) for d in range(devices)]
    return lax.ppermute(block, "row", pairs)


def small_plan(pair, mask, proj, gate, out, gain, mid):
    rows, tokens, channels = pair.shape
    devices, size, hw = tokens // rows, rows * tokens, out.shape[1]
    tiles = size // LANES
    packed = pl.pallas_call(
        functools.partial(pack_kernel, rows, tokens),
        out_shape=VMEM((1, tiles * channels + MASK_ROWS, LANES), BF16),
        out_specs=IN_VMEM,
        compiler_params=SMALL,
        name="pack",
    )(pair, mask)
    me = lax.axis_index("row").reshape(1).astype(jnp.int32)
    weights = pl.pallas_call(
        functools.partial(prepare_kernel, rows, tokens),
        in_specs=[IN_SMEM] + [pl.BlockSpec()] * 5,
        out_shape=(
            VMEM((2, 4 * hw, channels), BF16),
            VMEM((2, channels, channels), BF16),
            VMEM((2, channels, hw), BF16),
            VMEM((2, channels, LANES), F32),
            VMEM((2, hw, LANES), F32),
            VMEM((LANES, LANES), BF16),
            VMEM((rows, LANES, LANES), BF16),
        ),
        out_specs=(IN_VMEM,) * 7,
        compiler_params=SMALL,
        name="prepare",
    )(me, proj, gate, out, gain, mid)

    def swapped(group):
        return exchange(jnp.concatenate([held[m] for m in group]), 1, devices)

    held = {0: packed}
    for m in (12, 8, 4, 2):
        held[m] = exchange(packed, m, devices)
    held[2], held[4], held[8], held[12], weights = lax.optimization_barrier(
        (held[2], held[4], held[8], held[12], weights)
    )
    held[14] = exchange(held[12], 2, devices)
    held[10] = exchange(held[8], 2, devices)
    held[6] = exchange(held[2], 4, devices)
    early = (0, 2, 4, 8, 12)
    count = len(early)
    ahead = pl.pallas_call(
        functools.partial(early_kernel, (1,) * 5),
        in_specs=[IN_VMEM] * 7,
        out_shape=(
            VMEM((count, tiles, hw, LANES), F32),
            VMEM((count, tiles, hw, LANES), F32),
            VMEM((count, tiles, channels, LANES), BF16),
        ),
        out_specs=(IN_VMEM,) * 3,
        compiler_params=SMALL,
        name="early",
    )(*[held[m] for m in (0, 2, 4, 8, 12)], weights[0], weights[3])
    held[14], held[10], held[6], ahead = lax.optimization_barrier(
        (held[14], held[10], held[6], ahead)
    )
    group = (0, 12, 8, 4, 2, 14, 10, 6)
    arrays = [held[m] for m in group] + [swapped(group)]
    sources = [(m,) for m in group] + [tuple(m ^ 1 for m in group)]
    result = pl.pallas_call(
        functools.partial(both_kernel, rows, tokens, sources, early),
        out_shape=jax.ShapeDtypeStruct((size, channels), BF16),
        in_specs=[IN_SMEM] + [IN_VMEM] * (len(arrays) + 10),
        scratch_shapes=[
            pltpu.VMEM((tiles, devices * hw, LANES), F32),
            pltpu.VMEM((tiles, devices * hw, LANES), F32),
            pltpu.VMEM((devices - count, tiles, channels, LANES), BF16),
            pltpu.VMEM((hw * devices * tiles, LANES), F32),
            pltpu.VMEM((2 * tiles, channels, LANES), BF16),
            pltpu.VMEM((devices * tiles * hw, LANES), BF16),
            pltpu.VMEM((devices * tiles * hw, LANES), BF16),
        ],
        compiler_params=pltpu.CompilerParams(vmem_limit_bytes=24 * 1024 * 1024),
        name="both",
    )(me, *arrays, *weights, *ahead)
    return result.reshape(pair.shape)


def layer_norm(values, gain, axis):
    average = jnp.mean(values, axis=axis, keepdims=True)
    centred = values - average
    variance = jnp.mean(centred * centred, axis=axis, keepdims=True)
    return centred * lax.rsqrt(variance + EPS) * gain


def wide_factors(normed, mask, proj):
    hw = proj.shape[1] // 4
    projected = jnp.einsum("ijd,de->eij", normed, proj, preferred_element_type=F32)
    left = mask * jax.nn.sigmoid(projected[hw : 2 * hw]) * projected[:hw]
    right = mask * jax.nn.sigmoid(projected[3 * hw :]) * projected[2 * hw : 3 * hw]
    return left.astype(BF16), right.astype(BF16)


def gathered_update(pair, mask, proj, gate, out, gain, mid, orient):
    rows, tokens, _ = pair.shape
    devices = tokens // rows
    floats = pair.astype(F32)
    normed = layer_norm(floats, gain, -1).astype(BF16)
    left, right = wide_factors(normed, mask, proj)
    everywhere = lax.all_gather(right, "row", axis=1, tiled=True)
    if orient == 1:
        c = left.shape[0]
        blocks = left.reshape(c, rows, devices, rows).transpose(2, 1, 3, 0)
        left = lax.all_to_all(blocks, "row", 0, 0, tiled=True)
        left = left.reshape(tokens, rows, c).transpose(2, 0, 1)
    spec = "cik,cjk->cij" if orient == 0 else "cki,ckj->cij"
    summed = jnp.einsum(spec, left, everywhere, preferred_element_type=F32)
    hidden = layer_norm(summed, mid[:, None, None], 0).astype(BF16)
    gating = jax.nn.sigmoid(jnp.einsum("ijd,de->ije", normed, gate, preferred_element_type=F32))
    update = jnp.einsum("cij,cd->ijd", hidden, out, preferred_element_type=F32)
    return (floats + gating * update).astype(BF16)


def shards(pair, pair_mask, proj, gate, out, gain, mid):
    rows, tokens, _ = pair.shape
    if rows == 4 and 2 * tokens == LANES:
        return small_plan(pair, pair_mask, proj, gate, out, gain, mid)
    mask = pair_mask.astype(F32)[None]
    for o in range(2):
        pair = gathered_update(pair, mask, proj[o], gate[o], out[o], gain[o], mid[o], o)
    return pair


def solution(mesh):
    return jax.shard_map(
        shards,
        mesh=mesh,
        in_specs=(P(("groups", "row")), P(("groups", "row")), P(), P(), P(), P(), P()),
        out_specs=P(("groups", "row")),
        check_vma=False,
    )
```

```python
import functools

import jax
import jax.numpy as jnp
from jax import lax
from jax.experimental import pallas as pl
from jax.experimental.pallas import tpu as pltpu
from jax.sharding import PartitionSpec as P

EPS = 1e-05
F32, BF16 = jnp.float32, jnp.bfloat16
LANES = 128
MASK_ROWS = 16
NT = (((1,), (1,)), ((), ()))
VMEM = pltpu.VMEM
IN_VMEM = pl.BlockSpec(memory_space=pltpu.VMEM)
IN_SMEM = pl.BlockSpec(memory_space=pltpu.SMEM)
SMALL = pltpu.CompilerParams(vmem_limit_bytes=8 * 1024 * 1024)


def dot(a, b):
    return jnp.dot(a, b, preferred_element_type=F32)


def dot_nt(a, b):
    return lax.dot_general(a, b, NT, preferred_element_type=F32)


def twice_sigmoid(half):
    return jnp.tanh(half) + 1.0


def iota(shape, axis):
    return lax.broadcasted_iota(jnp.int32, shape, axis)


def one_hot(condition):
    return condition.astype(F32).astype(BF16)


def token_of(t, rows, tokens):
    devices = tokens // rows
    return (t % devices) * rows + t // devices


def column_norm(values, gain):
    average = jnp.mean(values, axis=0, keepdims=True)
    centred = values - average
    variance = jnp.mean(centred * centred, axis=0, keepdims=True)
    return (centred * lax.rsqrt(variance + EPS) * gain).astype(BF16)


def factors(projected, half_mask):
    hw = projected.shape[0] // 4
    left = half_mask * twice_sigmoid(projected[hw : 2 * hw]) * projected[:hw]
    right = half_mask * twice_sigmoid(projected[3 * hw :]) * projected[2 * hw : 3 * hw]
    return left, right


def side_by_side(chunks):
    return jnp.concatenate(chunks, axis=1)


def tile(values, h):
    return values[:, h * LANES : (h + 1) * LANES]


def pack_kernel(rows, tokens, pair_ref, mask_ref, packed_ref):
    channels = pair_ref.shape[-1]
    square = (tokens, tokens)
    by_lane = one_hot(token_of(iota(square, 0), rows, tokens) == iota(square, 1))
    by_token = one_hot(token_of(iota(square, 1), rows, tokens) == iota(square, 0))
    identity = one_hot(iota((channels, channels), 0) == iota((channels, channels), 1))
    masks = 0.5 * dot(one_hot(mask_ref[...] != 0), by_token)
    tiles = rows * tokens // LANES
    for h in range(tiles):
        pair = [dot(by_lane, pair_ref[i]).astype(BF16) for i in (2 * h, 2 * h + 1)]
        chunk = dot_nt(identity, jnp.concatenate(pair, axis=0))
        packed_ref[0, h * channels : (h + 1) * channels, :] = chunk.astype(BF16)
    lines = [
        jnp.concatenate([masks[2 * h : 2 * h + 1], masks[2 * h + 1 : 2 * h + 2]], axis=1)
        for h in range(tiles)
    ]
    shape = (MASK_ROWS, LANES)
    block = jnp.where(iota(shape, 0) < MASK_ROWS // 2, lines[0], lines[1])
    packed_ref[0, tiles * channels :, :] = block.astype(BF16)


def chunk_of(ref, channels, k, h):
    return ref[k, h * channels : (h + 1) * channels, :].astype(F32)


def mask_of(ref, channels, k, h):
    lines = ref[k, -MASK_ROWS:, :].astype(F32)
    return lines[h * MASK_ROWS // 2 : h * MASK_ROWS // 2 + 1]


def prepare_kernel(
    rows, tokens, me_ref, proj_ref, gate_ref, out_ref, gain_ref, mid_ref,
    proj_t_ref, gate_t_ref, out_t_ref, gain_t_ref, mid_t_ref, restore_ref, spread_ref,
):
    devices = tokens // rows

    def flipped(weight):
        return weight.astype(F32).T

    def column(line):
        return jnp.broadcast_to(line, (LANES, line.shape[1])).T

    hw = mid_ref.shape[1]
    is_gate = iota((4 * hw, proj_ref.shape[1]), 0) // hw % 2 == 1
    for o in range(2):
        proj = flipped(proj_ref[o])
        proj_t_ref[o] = jnp.where(is_gate, 0.5 * proj, proj).astype(BF16)
        gate_t_ref[o] = (0.5 * flipped(gate_ref[o])).astype(BF16)
        out_t_ref[o] = (0.5 * flipped(out_ref[o])).astype(BF16)
        gain_t_ref[o] = column(gain_ref[o : o + 1, :])
        mid_t_ref[o] = column(mid_ref[o : o + 1, :])
    shape = (LANES, LANES)
    lane = iota(shape, 1)
    source = lane // tokens * tokens + token_of(lane % tokens, rows, tokens)
    restore_ref[...] = one_hot(source == iota(shape, 0))
    group, lane = iota(shape, 0) // tokens, iota(shape, 0) % tokens
    same = group == iota(shape, 1) // tokens
    for i in range(rows):
        spread_ref[i] = one_hot(same & (lane == i * devices + me_ref[0]))


def early_kernel(counts, *refs):
    block_refs, (proj_ref, gain_ref, left_ref, right_ref, normed_ref) = refs[:-5], refs[-5:]
    channels, tiles = normed_ref.shape[2], normed_ref.shape[1]
    place = 0
    for block_ref, count in zip(block_refs, counts):
        for k in range(count):
            normed = [
                column_norm(chunk_of(block_ref, channels, k, h), gain_ref[0]) for h in range(tiles)
            ]
            projected = dot(proj_ref[0], side_by_side(normed))
            for h in range(tiles):
                normed_ref[place, h] = normed[h]
                left, right = factors(tile(projected, h), mask_of(block_ref, channels, k, h))
                left_ref[place, h] = left
                right_ref[place, h] = right
            place += 1


def both_kernel(rows, tokens, sources, early_groups, me_ref, *refs):
    devices = tokens // rows
    block_refs, refs = refs[: len(sources)], refs[len(sources) :]
    weight_refs, refs = refs[:7], refs[7:]
    proj_ref, gate_ref, out_ref, gain_ref, mid_ref, restore_ref, spread_ref = weight_refs
    ahead = {}
    for group in early_groups:
        for n, m in enumerate(group):
            ahead[m] = refs[:3] + (n,)
        refs = refs[3:]
    (
        result_ref, left_s, right_s, normed_s, sum_s, now_s, second_left_s, second_right_s,
    ) = refs
    channels = gate_ref.shape[1]
    hw = mid_ref.shape[1]
    tiles = rows * tokens // LANES
    me = me_ref[0]

    where = {m: (ref, k) for ref, held in zip(block_refs, sources) for k, m in enumerate(held)}
    later = [m for m in range(devices) if m not in ahead]

    def place(m, h, left, right):
        here = pl.ds(pl.multiple_of((me ^ m) * hw, hw), hw)
        left_s[h, here, :] = left
        right_s[h, here, :] = right

    for m in later:
        ref, k = where[m]
        normed = [column_norm(chunk_of(ref, channels, k, h), gain_ref[0]) for h in range(tiles)]
        projected = dot(proj_ref[0], side_by_side(normed))
        for h in range(tiles):
            normed_s[later.index(m), h] = normed[h]
            place(m, h, *factors(tile(projected, h), mask_of(ref, channels, k, h)))
    for m, (left_ref, right_ref, _, n) in ahead.items():
        for h in range(tiles):
            place(m, h, left_ref[n, h], right_ref[n, h])

    def normed_of(m, h):
        if m in ahead:
            return ahead[m][2][ahead[m][3], h]
        return normed_s[later.index(m), h]

    low = iota((devices, LANES), 1) < tokens

    def channel_sum(c):
        here = pl.ds(c, devices, stride=hw)
        left = jnp.concatenate([left_s[h, here, :] for h in range(tiles)], axis=0)
        halves = [[], []]
        for h in range(tiles):
            right = right_s[h, here, :]
            turned = pltpu.roll(right, tokens, 1)
            for q in range(2):
                straight, other = (right, turned) if q == 0 else (turned, right)
                halves[0].append(jnp.where(low, straight, 0.0))
                halves[1].append(jnp.where(low, 0.0, other))
        against = jnp.concatenate(halves[0] + halves[1], axis=0).astype(BF16)
        here = pl.ds(c * tiles * devices, tiles * devices)
        sum_s[here, :] = dot_nt(left.astype(BF16), against)

    for c in range(hw):
        channel_sum(c)

    for m in range(devices):
        ref, k = where[m]
        hidden, first = [], []
        for h in range(tiles):
            summed = sum_s[pl.ds(h * devices + (me ^ m), hw, stride=tiles * devices), :]
            hidden.append(column_norm(summed, mid_ref[0]))
            first.append(normed_of(m, h))
        update = dot(out_ref[0], side_by_side(hidden))
        logits = dot(gate_ref[0], side_by_side(first))
        normed = []
        for h in range(tiles):
            gated = twice_sigmoid(tile(logits, h)) * tile(update, h)
            now = (chunk_of(ref, channels, k, h) + gated).astype(BF16)
            normed.append(column_norm(now.astype(F32), gain_ref[1]))
            if m == 0:
                now_s[h] = now
                now_s[tiles + h] = normed[h]
        projected = dot(proj_ref[1], side_by_side(normed))
        for h in range(tiles):
            left, right = factors(tile(projected, h), mask_of(ref, channels, k, h))
            here = pl.ds((m * tiles + h) * hw, hw)
            second_left_s[here, :] = left.astype(BF16)
            second_right_s[here, :] = right.astype(BF16)

    depth = 2 * hw
    sums = []
    for i in range(0, rows, 2):
        pair = side_by_side([spread_ref[i], spread_ref[i + 1]])
        totals = [jnp.zeros((hw, LANES), F32)] * 2
        for n in range(devices * tiles // 2):
            here = pl.ds(n * depth, depth)
            spread = dot(second_left_s[here, :], pair)
            right = second_right_s[here, :].astype(F32)
            for o in range(2):
                terms = tile(spread, o) * right
                totals[o] = totals[o] + (terms[:hw] + terms[hw:])
        sums += [total + pltpu.roll(total, tokens, 1) for total in totals]
    low = iota((hw, LANES), 1) < tokens
    for h in range(tiles):
        summed = jnp.where(low, sums[2 * h], sums[2 * h + 1])
        update = dot(out_ref[1], column_norm(summed, mid_ref[1]))
        gating = twice_sigmoid(dot(gate_ref[1], now_s[tiles + h]))
        final = (now_s[h].astype(F32) + gating * update).astype(BF16)
        result_ref[h * LANES : (h + 1) * LANES, :] = dot_nt(restore_ref[...], final).astype(BF16)


def exchange(block, partner_bits, devices):
    pairs = [(d, d ^ partner_bits) for d in range(devices)]
    return lax.ppermute(block, "row", pairs)


def small_plan(pair, mask, proj, gate, out, gain, mid):
    rows, tokens, channels = pair.shape
    devices, size, hw = tokens // rows, rows * tokens, out.shape[1]
    tiles = size // LANES
    packed = pl.pallas_call(
        functools.partial(pack_kernel, rows, tokens),
        out_shape=VMEM((1, tiles * channels + MASK_ROWS, LANES), BF16),
        out_specs=IN_VMEM,
        name="pack",
    )(pair, mask)
    me = lax.axis_index("row").reshape(1).astype(jnp.int32)
    weights = pl.pallas_call(
        functools.partial(prepare_kernel, rows, tokens),
        in_specs=[IN_SMEM] + [pl.BlockSpec()] * 5,
        out_shape=(
            VMEM((2, 4 * hw, channels), BF16),
            VMEM((2, channels, channels), BF16),
            VMEM((2, channels, hw), BF16),
            VMEM((2, channels, LANES), F32),
            VMEM((2, hw, LANES), F32),
            VMEM((LANES, LANES), BF16),
            VMEM((rows, LANES, LANES), BF16),
        ),
        out_specs=(IN_VMEM,) * 7,
        name="prepare",
    )(me, proj, gate, out, gain, mid)

    def swapped(group):
        return exchange(jnp.concatenate([held[m] for m in group]), 1, devices)

    def project_early(blocks):
        count = sum(block.shape[0] for block in blocks)
        return pl.pallas_call(
            functools.partial(early_kernel, [block.shape[0] for block in blocks]),
            in_specs=[IN_VMEM] * (len(blocks) + 2),
            out_shape=(
                VMEM((count, tiles, hw, LANES), F32),
                VMEM((count, tiles, hw, LANES), F32),
                VMEM((count, tiles, channels, LANES), BF16),
            ),
            out_specs=(IN_VMEM,) * 3,
            compiler_params=SMALL,
            name="early",
        )(*blocks, weights[0], weights[3])

    held = {0: packed}
    for m in (12, 8, 6, 4, 2):
        held[m] = exchange(packed, m, devices)
    near = (2, 4, 6, 8, 12)
    *blocks, weights = lax.optimization_barrier([held[m] for m in near] + [weights])
    held.update(zip(near, blocks))
    for m in (12, 8):
        held[m ^ 2] = exchange(held[m], 2, devices)
    first = (0, 12, 8, 4, 2, 6)
    last = (14, 10)
    swaps = [swapped(first)]
    ahead = project_early([held[m] for m in first])
    swaps[0], ahead = lax.optimization_barrier((swaps[0], ahead))
    again = project_early(swaps)
    held[14], held[10], ahead, again = lax.optimization_barrier(
        (held[14], held[10], ahead, again)
    )
    swaps.append(swapped(last))
    arrays = [held[m] for m in first + last] + swaps
    sources = [(m,) for m in first + last]
    sources += [tuple(m ^ 1 for m in group) for group in (first, last)]
    early_groups = (first, sources[-2])
    result = pl.pallas_call(
        functools.partial(both_kernel, rows, tokens, sources, early_groups),
        out_shape=jax.ShapeDtypeStruct((size, channels), BF16),
        in_specs=[IN_SMEM] + [IN_VMEM] * (len(arrays) + len(weights) + len(ahead) + len(again)),
        scratch_shapes=[
            pltpu.VMEM((tiles, devices * hw, LANES), F32),
            pltpu.VMEM((tiles, devices * hw, LANES), F32),
            pltpu.VMEM((2 * len(last), tiles, channels, LANES), BF16),
            pltpu.VMEM((hw * devices * tiles, LANES), F32),
            pltpu.VMEM((2 * tiles, channels, LANES), BF16),
            pltpu.VMEM((devices * tiles * hw, LANES), BF16),
            pltpu.VMEM((devices * tiles * hw, LANES), BF16),
        ],
        compiler_params=pltpu.CompilerParams(vmem_limit_bytes=24 * 1024 * 1024),
        name="both",
    )(me, *arrays, *weights, *ahead, *again)
    return result.reshape(pair.shape)


def layer_norm(values, gain, axis):
    average = jnp.mean(values, axis=axis, keepdims=True)
    centred = values - average
    variance = jnp.mean(centred * centred, axis=axis, keepdims=True)
    return centred * lax.rsqrt(variance + EPS) * gain


def wide_factors(normed, mask, proj):
    hw = proj.shape[1] // 4
    projected = jnp.einsum("ijd,de->eij", normed, proj, preferred_element_type=F32)
    left = mask * jax.nn.sigmoid(projected[hw : 2 * hw]) * projected[:hw]
    right = mask * jax.nn.sigmoid(projected[3 * hw :]) * projected[2 * hw : 3 * hw]
    return left.astype(BF16), right.astype(BF16)


def gathered_update(pair, mask, proj, gate, out, gain, mid, orient):
    rows, tokens, _ = pair.shape
    devices = tokens // rows
    floats = pair.astype(F32)
    normed = layer_norm(floats, gain, -1).astype(BF16)
    left, right = wide_factors(normed, mask, proj)
    everywhere = lax.all_gather(right, "row", axis=1, tiled=True)
    if orient == 1:
        c = left.shape[0]
        blocks = left.reshape(c, rows, devices, rows).transpose(2, 1, 3, 0)
        left = lax.all_to_all(blocks, "row", 0, 0, tiled=True)
        left = left.reshape(tokens, rows, c).transpose(2, 0, 1)
    spec = "cik,cjk->cij" if orient == 0 else "cki,ckj->cij"
    summed = jnp.einsum(spec, left, everywhere, preferred_element_type=F32)
    hidden = layer_norm(summed, mid[:, None, None], 0).astype(BF16)
    gating = jax.nn.sigmoid(jnp.einsum("ijd,de->ije", normed, gate, preferred_element_type=F32))
    update = jnp.einsum("cij,cd->ijd", hidden, out, preferred_element_type=F32)
    return (floats + gating * update).astype(BF16)


def shards(pair, pair_mask, proj, gate, out, gain, mid):
    rows, tokens, _ = pair.shape
    if rows == 4 and 2 * tokens == LANES:
        return small_plan(pair, pair_mask, proj, gate, out, gain, mid)
    mask = pair_mask.astype(F32)[None]
    for o in range(2):
        pair = gathered_update(pair, mask, proj[o], gate[o], out[o], gain[o], mid[o], o)
    return pair


def solution(mesh):
    return jax.shard_map(
        shards,
        mesh=mesh,
        in_specs=(P(("groups", "row")), P(("groups", "row")), P(), P(), P(), P(), P()),
        out_specs=P(("groups", "row")),
        check_vma=False,
    )
```

```python
import functools

import jax
import jax.numpy as jnp
from jax import lax
from jax.experimental import pallas as pl
from jax.experimental.pallas import tpu as pltpu
from jax.sharding import PartitionSpec as P

EPS = 1e-05
F32, BF16 = jnp.float32, jnp.bfloat16
LANES = 128
MASK_ROWS = 16
NT = (((1,), (1,)), ((), ()))
VMEM = pltpu.VMEM
IN_VMEM = pl.BlockSpec(memory_space=pltpu.VMEM)
IN_SMEM = pl.BlockSpec(memory_space=pltpu.SMEM)
SMALL = pltpu.CompilerParams(vmem_limit_bytes=8 * 1024 * 1024)


def dot(a, b):
    return jnp.dot(a, b, preferred_element_type=F32)


def dot_nt(a, b):
    return lax.dot_general(a, b, NT, preferred_element_type=F32)


def twice_sigmoid(half):
    return jnp.tanh(half) + 1.0


def iota(shape, axis):
    return lax.broadcasted_iota(jnp.int32, shape, axis)


def one_hot(condition):
    return condition.astype(F32).astype(BF16)


def token_of(t, rows, tokens):
    devices = tokens // rows
    return (t % devices) * rows + t // devices


def column_norm(values, gain):
    average = jnp.mean(values, axis=0, keepdims=True)
    centred = values - average
    variance = jnp.mean(centred * centred, axis=0, keepdims=True)
    return (centred * lax.rsqrt(variance + EPS) * gain).astype(BF16)


def factors(projected, half_mask):
    hw = projected.shape[0] // 4
    left = half_mask * twice_sigmoid(projected[hw : 2 * hw]) * projected[:hw]
    right = half_mask * twice_sigmoid(projected[3 * hw :]) * projected[2 * hw : 3 * hw]
    return left, right


def side_by_side(chunks):
    return jnp.concatenate(chunks, axis=1)


def tile(values, h):
    return values[:, h * LANES : (h + 1) * LANES]


def pack_kernel(rows, tokens, pair_ref, mask_ref, packed_ref):
    channels = pair_ref.shape[-1]
    square = (tokens, tokens)
    by_lane = one_hot(token_of(iota(square, 0), rows, tokens) == iota(square, 1))
    by_token = one_hot(token_of(iota(square, 1), rows, tokens) == iota(square, 0))
    identity = one_hot(iota((channels, channels), 0) == iota((channels, channels), 1))
    masks = 0.5 * dot(one_hot(mask_ref[...] != 0), by_token)
    tiles = rows * tokens // LANES
    for h in range(tiles):
        pair = [dot(by_lane, pair_ref[i]).astype(BF16) for i in (2 * h, 2 * h + 1)]
        chunk = dot_nt(identity, jnp.concatenate(pair, axis=0))
        packed_ref[0, h * channels : (h + 1) * channels, :] = chunk.astype(BF16)
    lines = [
        jnp.concatenate([masks[2 * h : 2 * h + 1], masks[2 * h + 1 : 2 * h + 2]], axis=1)
        for h in range(tiles)
    ]
    shape = (MASK_ROWS, LANES)
    block = jnp.where(iota(shape, 0) < MASK_ROWS // 2, lines[0], lines[1])
    packed_ref[0, tiles * channels :, :] = block.astype(BF16)


def chunk_of(ref, channels, k, h):
    return ref[k, h * channels : (h + 1) * channels, :].astype(F32)


def mask_of(ref, channels, k, h):
    lines = ref[k, -MASK_ROWS:, :].astype(F32)
    return lines[h * MASK_ROWS // 2 : h * MASK_ROWS // 2 + 1]


def prepare_kernel(
    rows, tokens, me_ref, proj_ref, gate_ref, out_ref, gain_ref, mid_ref,
    proj_t_ref, gate_t_ref, out_t_ref, gain_t_ref, mid_t_ref, restore_ref, spread_ref,
):
    devices = tokens // rows

    def flipped(weight):
        return weight.astype(F32).T

    def column(line):
        return jnp.broadcast_to(line, (LANES, line.shape[1])).T

    hw = mid_ref.shape[1]
    is_gate = iota((4 * hw, proj_ref.shape[1]), 0) // hw % 2 == 1
    for o in range(2):
        proj = flipped(proj_ref[o])
        proj_t_ref[o] = jnp.where(is_gate, 0.5 * proj, proj).astype(BF16)
        gate_t_ref[o] = (0.5 * flipped(gate_ref[o])).astype(BF16)
        out_t_ref[o] = (0.5 * flipped(out_ref[o])).astype(BF16)
        gain_t_ref[o] = column(gain_ref[o : o + 1, :])
        mid_t_ref[o] = column(mid_ref[o : o + 1, :])
    shape = (LANES, LANES)
    lane = iota(shape, 1)
    source = lane // tokens * tokens + token_of(lane % tokens, rows, tokens)
    restore_ref[...] = one_hot(source == iota(shape, 0))
    group, lane = iota(shape, 0) // tokens, iota(shape, 0) % tokens
    same = group == iota(shape, 1) // tokens
    for i in range(rows):
        spread_ref[i] = one_hot(same & (lane == i * devices + me_ref[0]))


def early_kernel(counts, *refs):
    block_refs, (proj_ref, gain_ref, left_ref, right_ref, normed_ref) = refs[:-5], refs[-5:]
    channels, tiles = normed_ref.shape[2], normed_ref.shape[1]
    place = 0
    for block_ref, count in zip(block_refs, counts):
        for k in range(count):
            normed = [
                column_norm(chunk_of(block_ref, channels, k, h), gain_ref[0]) for h in range(tiles)
            ]
            projected = dot(proj_ref[0], side_by_side(normed))
            for h in range(tiles):
                normed_ref[place, h] = normed[h]
                left, right = factors(tile(projected, h), mask_of(block_ref, channels, k, h))
                left_ref[place, h] = left
                right_ref[place, h] = right
            place += 1


def both_kernel(rows, tokens, sources, early_groups, me_ref, *refs):
    devices = tokens // rows
    block_refs, refs = refs[: len(sources)], refs[len(sources) :]
    weight_refs, refs = refs[:7], refs[7:]
    proj_ref, gate_ref, out_ref, gain_ref, mid_ref, restore_ref, spread_ref = weight_refs
    ahead = {}
    for group in early_groups:
        for n, m in enumerate(group):
            ahead[m] = refs[:3] + (n,)
        refs = refs[3:]
    (
        result_ref, left_s, right_s, normed_s, sum_s, now_s, second_left_s, second_right_s,
    ) = refs
    channels = gate_ref.shape[1]
    hw = mid_ref.shape[1]
    tiles = rows * tokens // LANES
    me = me_ref[0]

    where = {m: (ref, k) for ref, held in zip(block_refs, sources) for k, m in enumerate(held)}
    later = [m for m in range(devices) if m not in ahead]

    def place(m, h, left, right):
        here = pl.ds(pl.multiple_of((me ^ m) * hw, hw), hw)
        left_s[h, here, :] = left
        right_s[h, here, :] = right

    for m in later:
        ref, k = where[m]
        normed = [column_norm(chunk_of(ref, channels, k, h), gain_ref[0]) for h in range(tiles)]
        projected = dot(proj_ref[0], side_by_side(normed))
        for h in range(tiles):
            normed_s[later.index(m), h] = normed[h]
            place(m, h, *factors(tile(projected, h), mask_of(ref, channels, k, h)))
    for m, (left_ref, right_ref, _, n) in ahead.items():
        for h in range(tiles):
            place(m, h, left_ref[n, h], right_ref[n, h])

    def normed_of(m, h):
        if m in ahead:
            return ahead[m][2][ahead[m][3], h]
        return normed_s[later.index(m), h]

    low = iota((devices, LANES), 1) < tokens

    def channel_sum(c):
        here = pl.ds(c, devices, stride=hw)
        left = jnp.concatenate([left_s[h, here, :] for h in range(tiles)], axis=0)
        halves = [[], []]
        for h in range(tiles):
            right = right_s[h, here, :]
            turned = pltpu.roll(right, tokens, 1)
            for q in range(2):
                straight, other = (right, turned) if q == 0 else (turned, right)
                halves[0].append(jnp.where(low, straight, 0.0))
                halves[1].append(jnp.where(low, 0.0, other))
        against = jnp.concatenate(halves[0] + halves[1], axis=0).astype(BF16)
        here = pl.ds(c * tiles * devices, tiles * devices)
        sum_s[here, :] = dot_nt(left.astype(BF16), against)

    for c in range(hw):
        channel_sum(c)

    for m in range(devices):
        ref, k = where[m]
        hidden, first = [], []
        for h in range(tiles):
            summed = sum_s[pl.ds(h * devices + (me ^ m), hw, stride=tiles * devices), :]
            hidden.append(column_norm(summed, mid_ref[0]))
            first.append(normed_of(m, h))
        update = dot(out_ref[0], side_by_side(hidden))
        logits = dot(gate_ref[0], side_by_side(first))
        normed = []
        for h in range(tiles):
            gated = twice_sigmoid(tile(logits, h)) * tile(update, h)
            now = (chunk_of(ref, channels, k, h) + gated).astype(BF16)
            normed.append(column_norm(now.astype(F32), gain_ref[1]))
            if m == 0:
                now_s[h] = now
                now_s[tiles + h] = normed[h]
        projected = dot(proj_ref[1], side_by_side(normed))
        for h in range(tiles):
            left, right = factors(tile(projected, h), mask_of(ref, channels, k, h))
            here = pl.ds((m * tiles + h) * hw, hw)
            second_left_s[here, :] = left.astype(BF16)
            second_right_s[here, :] = right.astype(BF16)

    depth = 2 * hw
    sums = []
    for i in range(0, rows, 2):
        pair = side_by_side([spread_ref[i], spread_ref[i + 1]])
        totals = [jnp.zeros((hw, LANES), F32)] * 2
        for n in range(devices * tiles // 2):
            here = pl.ds(n * depth, depth)
            spread = dot(second_left_s[here, :], pair)
            right = second_right_s[here, :].astype(F32)
            for o in range(2):
                terms = tile(spread, o) * right
                totals[o] = totals[o] + (terms[:hw] + terms[hw:])
        sums += [total + pltpu.roll(total, tokens, 1) for total in totals]
    low = iota((hw, LANES), 1) < tokens
    for h in range(tiles):
        summed = jnp.where(low, sums[2 * h], sums[2 * h + 1])
        update = dot(out_ref[1], column_norm(summed, mid_ref[1]))
        gating = twice_sigmoid(dot(gate_ref[1], now_s[tiles + h]))
        final = (now_s[h].astype(F32) + gating * update).astype(BF16)
        result_ref[h * LANES : (h + 1) * LANES, :] = dot_nt(restore_ref[...], final).astype(BF16)


def exchange(block, partner_bits, devices):
    pairs = [(d, d ^ partner_bits) for d in range(devices)]
    return lax.ppermute(block, "row", pairs)


def small_plan(pair, mask, proj, gate, out, gain, mid):
    rows, tokens, channels = pair.shape
    devices, size, hw = tokens // rows, rows * tokens, out.shape[1]
    tiles = size // LANES
    packed = pl.pallas_call(
        functools.partial(pack_kernel, rows, tokens),
        out_shape=VMEM((1, tiles * channels + MASK_ROWS, LANES), BF16),
        out_specs=IN_VMEM,
        name="pack",
    )(pair, mask)
    me = lax.axis_index("row").reshape(1).astype(jnp.int32)
    weights = pl.pallas_call(
        functools.partial(prepare_kernel, rows, tokens),
        in_specs=[IN_SMEM] + [pl.BlockSpec()] * 5,
        out_shape=(
            VMEM((2, 4 * hw, channels), BF16),
            VMEM((2, channels, channels), BF16),
            VMEM((2, channels, hw), BF16),
            VMEM((2, channels, LANES), F32),
            VMEM((2, hw, LANES), F32),
            VMEM((LANES, LANES), BF16),
            VMEM((rows, LANES, LANES), BF16),
        ),
        out_specs=(IN_VMEM,) * 7,
        name="prepare",
    )(me, proj, gate, out, gain, mid)

    def swapped(group):
        return exchange(jnp.concatenate([held[m] for m in group]), 1, devices)

    def project_early(blocks):
        count = sum(block.shape[0] for block in blocks)
        return pl.pallas_call(
            functools.partial(early_kernel, [block.shape[0] for block in blocks]),
            in_specs=[IN_VMEM] * (len(blocks) + 2),
            out_shape=(
                VMEM((count, tiles, hw, LANES), F32),
                VMEM((count, tiles, hw, LANES), F32),
                VMEM((count, tiles, channels, LANES), BF16),
            ),
            out_specs=(IN_VMEM,) * 3,
            compiler_params=SMALL,
            name="early",
        )(*blocks, weights[0], weights[3])

    held = {0: packed}
    for m in (12, 8, 4, 2):
        held[m] = exchange(packed, m, devices)
    held[12], weights = lax.optimization_barrier((held[12], weights))
    held[14] = exchange(held[12], 2, devices)
    held[6] = exchange(held[2], 4, devices)
    held[10] = exchange(held[8], 2, devices)
    first = (0, 4, 2, 8, 12)
    last = (14, 6, 10)
    swaps = [swapped(first), swapped(last)]
    ahead = project_early([held[m] for m in first + last] + swaps[:1])
    arrays = [held[m] for m in first + last] + swaps
    sources = [(m,) for m in first + last]
    sources += [tuple(m ^ 1 for m in group) for group in (first, last)]
    early_groups = (first + last + sources[-2],)
    result = pl.pallas_call(
        functools.partial(both_kernel, rows, tokens, sources, early_groups),
        out_shape=jax.ShapeDtypeStruct((size, channels), BF16),
        in_specs=[IN_SMEM] + [IN_VMEM] * (len(arrays) + len(weights) + len(ahead)),
        scratch_shapes=[
            pltpu.VMEM((tiles, devices * hw, LANES), F32),
            pltpu.VMEM((tiles, devices * hw, LANES), F32),
            pltpu.VMEM((len(last), tiles, channels, LANES), BF16),
            pltpu.VMEM((hw * devices * tiles, LANES), F32),
            pltpu.VMEM((2 * tiles, channels, LANES), BF16),
            pltpu.VMEM((devices * tiles * hw, LANES), BF16),
            pltpu.VMEM((devices * tiles * hw, LANES), BF16),
        ],
        compiler_params=pltpu.CompilerParams(vmem_limit_bytes=24 * 1024 * 1024),
        name="both",
    )(me, *arrays, *weights, *ahead)
    return result.reshape(pair.shape)


def layer_norm(values, gain, axis):
    average = jnp.mean(values, axis=axis, keepdims=True)
    centred = values - average
    variance = jnp.mean(centred * centred, axis=axis, keepdims=True)
    return centred * lax.rsqrt(variance + EPS) * gain


def wide_factors(normed, mask, proj):
    hw = proj.shape[1] // 4
    projected = jnp.einsum("ijd,de->eij", normed, proj, preferred_element_type=F32)
    left = mask * jax.nn.sigmoid(projected[hw : 2 * hw]) * projected[:hw]
    right = mask * jax.nn.sigmoid(projected[3 * hw :]) * projected[2 * hw : 3 * hw]
    return left.astype(BF16), right.astype(BF16)


def gathered_update(pair, mask, proj, gate, out, gain, mid, orient):
    rows, tokens, _ = pair.shape
    devices = tokens // rows
    floats = pair.astype(F32)
    normed = layer_norm(floats, gain, -1).astype(BF16)
    left, right = wide_factors(normed, mask, proj)
    everywhere = lax.all_gather(right, "row", axis=1, tiled=True)
    if orient == 1:
        c = left.shape[0]
        blocks = left.reshape(c, rows, devices, rows).transpose(2, 1, 3, 0)
        left = lax.all_to_all(blocks, "row", 0, 0, tiled=True)
        left = left.reshape(tokens, rows, c).transpose(2, 0, 1)
    spec = "cik,cjk->cij" if orient == 0 else "cki,ckj->cij"
    summed = jnp.einsum(spec, left, everywhere, preferred_element_type=F32)
    hidden = layer_norm(summed, mid[:, None, None], 0).astype(BF16)
    gating = jax.nn.sigmoid(jnp.einsum("ijd,de->ije", normed, gate, preferred_element_type=F32))
    update = jnp.einsum("cij,cd->ijd", hidden, out, preferred_element_type=F32)
    return (floats + gating * update).astype(BF16)


def shards(pair, pair_mask, proj, gate, out, gain, mid):
    rows, tokens, _ = pair.shape
    if rows == 4 and 2 * tokens == LANES:
        return small_plan(pair, pair_mask, proj, gate, out, gain, mid)
    mask = pair_mask.astype(F32)[None]
    for o in range(2):
        pair = gathered_update(pair, mask, proj[o], gate[o], out[o], gain[o], mid[o], o)
    return pair


def solution(mesh):
    return jax.shard_map(
        shards,
        mesh=mesh,
        in_specs=(P(("groups", "row")), P(("groups", "row")), P(), P(), P(), P(), P()),
        out_specs=P(("groups", "row")),
        check_vma=False,
    )
```

```python
import functools

import jax
import jax.numpy as jnp
from jax import lax
from jax.experimental import pallas as pl
from jax.experimental.pallas import tpu as pltpu
from jax.sharding import PartitionSpec as P

EPS = 1e-05
F32, BF16 = jnp.float32, jnp.bfloat16
LANES = 128
MASK_ROWS = 16
BLOCKS_AT_ONCE = 4
CHANNELS_AT_ONCE = 8
NT = (((1,), (1,)), ((), ()))
VMEM = pltpu.VMEM
IN_VMEM = pl.BlockSpec(memory_space=pltpu.VMEM)
IN_SMEM = pl.BlockSpec(memory_space=pltpu.SMEM)
SMALL = pltpu.CompilerParams(vmem_limit_bytes=8 * 1024 * 1024)


def dot(a, b):
    return jnp.dot(a, b, preferred_element_type=F32)


def dot_nt(a, b):
    return lax.dot_general(a, b, NT, preferred_element_type=F32)


def twice_sigmoid(half):
    return jnp.tanh(half) + 1.0


def iota(shape, axis):
    return lax.broadcasted_iota(jnp.int32, shape, axis)


def one_hot(condition):
    return condition.astype(F32).astype(BF16)


def token_of(t, rows, tokens):
    devices = tokens // rows
    return (t % devices) * rows + t // devices


def column_norm(values, gain):
    average = jnp.mean(values, axis=0, keepdims=True)
    centred = values - average
    variance = jnp.mean(centred * centred, axis=0, keepdims=True)
    return (centred * lax.rsqrt(variance + EPS) * gain).astype(BF16)


def factors(projected, half_mask):
    hw = projected.shape[0] // 4
    left = half_mask * twice_sigmoid(projected[hw : 2 * hw]) * projected[:hw]
    right = half_mask * twice_sigmoid(projected[3 * hw :]) * projected[2 * hw : 3 * hw]
    return left, right


def side_by_side(chunks):
    return jnp.concatenate(chunks, axis=1)


def tile(values, h):
    return values[:, h * LANES : (h + 1) * LANES]


def pack_kernel(rows, tokens, pair_ref, mask_ref, packed_ref):
    channels = pair_ref.shape[-1]
    square = (tokens, tokens)
    by_lane = one_hot(token_of(iota(square, 0), rows, tokens) == iota(square, 1))
    by_token = one_hot(token_of(iota(square, 1), rows, tokens) == iota(square, 0))
    identity = one_hot(iota((channels, channels), 0) == iota((channels, channels), 1))
    masks = 0.5 * dot(one_hot(mask_ref[...] != 0), by_token)
    tiles = rows * tokens // LANES
    for h in range(tiles):
        pair = [dot(by_lane, pair_ref[i]).astype(BF16) for i in (2 * h, 2 * h + 1)]
        chunk = dot_nt(identity, jnp.concatenate(pair, axis=0))
        packed_ref[0, h * channels : (h + 1) * channels, :] = chunk.astype(BF16)
    lines = [
        jnp.concatenate([masks[2 * h : 2 * h + 1], masks[2 * h + 1 : 2 * h + 2]], axis=1)
        for h in range(tiles)
    ]
    shape = (MASK_ROWS, LANES)
    block = jnp.where(iota(shape, 0) < MASK_ROWS // 2, lines[0], lines[1])
    packed_ref[0, tiles * channels :, :] = block.astype(BF16)


def chunk_of(ref, channels, k, h):
    return ref[k, h * channels : (h + 1) * channels, :].astype(F32)


def mask_of(ref, channels, k, h):
    lines = ref[k, -MASK_ROWS:, :].astype(F32)
    return lines[h * MASK_ROWS // 2 : h * MASK_ROWS // 2 + 1]


def prepare_kernel(
    rows, tokens, me_ref, proj_ref, gate_ref, out_ref, gain_ref, mid_ref,
    proj_t_ref, gate_t_ref, out_t_ref, gain_t_ref, mid_t_ref, restore_ref, spread_ref,
):
    devices = tokens // rows

    def flipped(weight):
        return weight.astype(F32).T

    def column(line):
        return jnp.broadcast_to(line, (LANES, line.shape[1])).T

    hw = mid_ref.shape[1]
    is_gate = iota((4 * hw, proj_ref.shape[1]), 0) // hw % 2 == 1
    for o in range(2):
        proj = flipped(proj_ref[o])
        proj_t_ref[o] = jnp.where(is_gate, 0.5 * proj, proj).astype(BF16)
        gate_t_ref[o] = (0.5 * flipped(gate_ref[o])).astype(BF16)
        out_t_ref[o] = (0.5 * flipped(out_ref[o])).astype(BF16)
        gain_t_ref[o] = column(gain_ref[o : o + 1, :])
        mid_t_ref[o] = column(mid_ref[o : o + 1, :])
    shape = (LANES, LANES)
    lane = iota(shape, 1)
    source = lane // tokens * tokens + token_of(lane % tokens, rows, tokens)
    restore_ref[...] = one_hot(source == iota(shape, 0))
    group, lane = iota(shape, 0) // tokens, iota(shape, 0) % tokens
    same = group == iota(shape, 1) // tokens
    for i in range(rows):
        spread_ref[i] = one_hot(same & (lane == i * devices + me_ref[0]))


def early_kernel(counts, *refs):
    block_refs, (proj_ref, gain_ref, left_ref, right_ref, normed_ref) = refs[:-5], refs[-5:]
    channels, tiles = normed_ref.shape[2], normed_ref.shape[1]
    place = 0
    for block_ref, count in zip(block_refs, counts):
        for k in range(count):
            normed = [
                column_norm(chunk_of(block_ref, channels, k, h), gain_ref[0]) for h in range(tiles)
            ]
            projected = dot(proj_ref[0], side_by_side(normed))
            for h in range(tiles):
                normed_ref[place, h] = normed[h]
                left, right = factors(tile(projected, h), mask_of(block_ref, channels, k, h))
                left_ref[place, h] = left
                right_ref[place, h] = right
            place += 1


def both_kernel(rows, tokens, sources, early_groups, me_ref, *refs):
    devices = tokens // rows
    block_refs, refs = refs[: len(sources)], refs[len(sources) :]
    weight_refs, refs = refs[:7], refs[7:]
    proj_ref, gate_ref, out_ref, gain_ref, mid_ref, restore_ref, spread_ref = weight_refs
    ahead = {}
    for group in early_groups:
        for n, m in enumerate(group):
            ahead[m] = refs[:3] + (n,)
        refs = refs[3:]
    (
        result_ref, left_s, right_s, normed_s, sum_s, now_s, second_left_s, second_right_s,
    ) = refs
    channels = gate_ref.shape[1]
    hw = mid_ref.shape[1]
    tiles = rows * tokens // LANES
    me = me_ref[0]

    where = {m: (ref, k) for ref, held in zip(block_refs, sources) for k, m in enumerate(held)}
    later = [m for m in range(devices) if m not in ahead]

    def place(m, h, left, right):
        here = pl.ds(pl.multiple_of((me ^ m) * hw, hw), hw)
        left_s[h, here, :] = left
        right_s[h, here, :] = right

    for m in later:
        ref, k = where[m]
        normed = [column_norm(chunk_of(ref, channels, k, h), gain_ref[0]) for h in range(tiles)]
        projected = dot(proj_ref[0], side_by_side(normed))
        for h in range(tiles):
            normed_s[later.index(m), h] = normed[h]
            place(m, h, *factors(tile(projected, h), mask_of(ref, channels, k, h)))
    for m, (left_ref, right_ref, _, n) in ahead.items():
        for h in range(tiles):
            place(m, h, left_ref[n, h], right_ref[n, h])

    def normed_of(m, h):
        if m in ahead:
            return ahead[m][2][ahead[m][3], h]
        return normed_s[later.index(m), h]

    low = iota((devices, LANES), 1) < tokens

    def operands(c):
        here = pl.ds(c, devices, stride=hw)
        left = jnp.concatenate([left_s[h, here, :] for h in range(tiles)], axis=0)
        halves = [[], []]
        for h in range(tiles):
            right = right_s[h, here, :]
            turned = pltpu.roll(right, tokens, 1)
            for q in range(2):
                straight, other = (right, turned) if q == 0 else (turned, right)
                halves[0].append(jnp.where(low, straight, 0.0))
                halves[1].append(jnp.where(low, 0.0, other))
        against = jnp.concatenate(halves[0] + halves[1], axis=0)
        return left.astype(BF16), against.astype(BF16)

    for c in range(0, hw, CHANNELS_AT_ONCE):
        group = [operands(c + n) for n in range(CHANNELS_AT_ONCE)]
        for n, (left, against) in enumerate(group):
            here = pl.ds((c + n) * tiles * devices, tiles * devices)
            sum_s[here, :] = dot_nt(left, against)

    both_tiles = range(tiles)
    for start in range(0, devices, BLOCKS_AT_ONCE):
        group = range(start, start + BLOCKS_AT_ONCE)
        hidden, updates, logits, normed, projected = {}, {}, {}, {}, {}
        for m in group:
            rows_of = [pl.ds(h * devices + (me ^ m), hw, stride=tiles * devices) for h in both_tiles]
            hidden[m] = [column_norm(sum_s[here, :], mid_ref[0]) for here in rows_of]
        for m in group:
            updates[m] = dot(out_ref[0], side_by_side(hidden[m]))
            logits[m] = dot(gate_ref[0], side_by_side([normed_of(m, h) for h in both_tiles]))
        for m in group:
            ref, k = where[m]
            normed[m] = []
            for h in both_tiles:
                gated = twice_sigmoid(tile(logits[m], h)) * tile(updates[m], h)
                now = (chunk_of(ref, channels, k, h) + gated).astype(BF16)
                normed[m].append(column_norm(now.astype(F32), gain_ref[1]))
                if m == 0:
                    now_s[h] = now
                    now_s[tiles + h] = normed[m][h]
        for m in group:
            projected[m] = dot(proj_ref[1], side_by_side(normed[m]))
        for m in group:
            ref, k = where[m]
            for h in both_tiles:
                left, right = factors(tile(projected[m], h), mask_of(ref, channels, k, h))
                here = pl.ds((m * tiles + h) * hw, hw)
                second_left_s[here, :] = left.astype(BF16)
                second_right_s[here, :] = right.astype(BF16)

    depth = 2 * hw
    sums = []
    for i in range(0, rows, 2):
        pair = side_by_side([spread_ref[i], spread_ref[i + 1]])
        totals = [jnp.zeros((hw, LANES), F32)] * 2
        for n in range(devices * tiles // 2):
            here = pl.ds(n * depth, depth)
            spread = dot(second_left_s[here, :], pair)
            right = second_right_s[here, :].astype(F32)
            for o in range(2):
                terms = tile(spread, o) * right
                totals[o] = totals[o] + (terms[:hw] + terms[hw:])
        sums += [total + pltpu.roll(total, tokens, 1) for total in totals]
    low = iota((hw, LANES), 1) < tokens
    for h in range(tiles):
        summed = jnp.where(low, sums[2 * h], sums[2 * h + 1])
        update = dot(out_ref[1], column_norm(summed, mid_ref[1]))
        gating = twice_sigmoid(dot(gate_ref[1], now_s[tiles + h]))
        final = (now_s[h].astype(F32) + gating * update).astype(BF16)
        result_ref[h * LANES : (h + 1) * LANES, :] = dot_nt(restore_ref[...], final).astype(BF16)


def exchange(block, partner_bits, devices):
    pairs = [(d, d ^ partner_bits) for d in range(devices)]
    return lax.ppermute(block, "row", pairs)


def small_plan(pair, mask, proj, gate, out, gain, mid):
    rows, tokens, channels = pair.shape
    devices, size, hw = tokens // rows, rows * tokens, out.shape[1]
    tiles = size // LANES
    packed = pl.pallas_call(
        functools.partial(pack_kernel, rows, tokens),
        out_shape=VMEM((1, tiles * channels + MASK_ROWS, LANES), BF16),
        out_specs=IN_VMEM,
        name="pack",
    )(pair, mask)
    me = lax.axis_index("row").reshape(1).astype(jnp.int32)
    weights = pl.pallas_call(
        functools.partial(prepare_kernel, rows, tokens),
        in_specs=[IN_SMEM] + [pl.BlockSpec()] * 5,
        out_shape=(
            VMEM((2, 4 * hw, channels), BF16),
            VMEM((2, channels, channels), BF16),
            VMEM((2, channels, hw), BF16),
            VMEM((2, channels, LANES), F32),
            VMEM((2, hw, LANES), F32),
            VMEM((LANES, LANES), BF16),
            VMEM((rows, LANES, LANES), BF16),
        ),
        out_specs=(IN_VMEM,) * 7,
        name="prepare",
    )(me, proj, gate, out, gain, mid)

    def swapped(group):
        return exchange(jnp.concatenate([held[m] for m in group]), 1, devices)

    def project_early(blocks):
        count = sum(block.shape[0] for block in blocks)
        return pl.pallas_call(
            functools.partial(early_kernel, [block.shape[0] for block in blocks]),
            in_specs=[IN_VMEM] * (len(blocks) + 2),
            out_shape=(
                VMEM((count, tiles, hw, LANES), F32),
                VMEM((count, tiles, hw, LANES), F32),
                VMEM((count, tiles, channels, LANES), BF16),
            ),
            out_specs=(IN_VMEM,) * 3,
            compiler_params=SMALL,
            name="early",
        )(*blocks, weights[0], weights[3])

    held = {0: packed}
    for m in (12, 8, 4, 2):
        held[m] = exchange(packed, m, devices)
    held[12], weights = lax.optimization_barrier((held[12], weights))
    held[14] = exchange(held[12], 2, devices)
    held[6] = exchange(held[2], 4, devices)
    held[10] = exchange(held[8], 2, devices)
    first = (0, 4, 2, 8, 12)
    last = (14, 6, 10)
    swaps = [swapped(first), swapped(last)]
    ahead = project_early([held[m] for m in first + last] + swaps[:1])
    arrays = [held[m] for m in first + last] + swaps
    sources = [(m,) for m in first + last]
    sources += [tuple(m ^ 1 for m in group) for group in (first, last)]
    early_groups = (first + last + sources[-2],)
    result = pl.pallas_call(
        functools.partial(both_kernel, rows, tokens, sources, early_groups),
        out_shape=jax.ShapeDtypeStruct((size, channels), BF16),
        in_specs=[IN_SMEM] + [IN_VMEM] * (len(arrays) + len(weights) + len(ahead)),
        scratch_shapes=[
            pltpu.VMEM((tiles, devices * hw, LANES), F32),
            pltpu.VMEM((tiles, devices * hw, LANES), F32),
            pltpu.VMEM((len(last), tiles, channels, LANES), BF16),
            pltpu.VMEM((hw * devices * tiles, LANES), F32),
            pltpu.VMEM((2 * tiles, channels, LANES), BF16),
            pltpu.VMEM((devices * tiles * hw, LANES), BF16),
            pltpu.VMEM((devices * tiles * hw, LANES), BF16),
        ],
        compiler_params=pltpu.CompilerParams(vmem_limit_bytes=24 * 1024 * 1024),
        name="both",
    )(me, *arrays, *weights, *ahead)
    return result.reshape(pair.shape)


def layer_norm(values, gain, axis):
    average = jnp.mean(values, axis=axis, keepdims=True)
    centred = values - average
    variance = jnp.mean(centred * centred, axis=axis, keepdims=True)
    return centred * lax.rsqrt(variance + EPS) * gain


def wide_factors(normed, mask, proj):
    hw = proj.shape[1] // 4
    projected = jnp.einsum("ijd,de->eij", normed, proj, preferred_element_type=F32)
    left = mask * jax.nn.sigmoid(projected[hw : 2 * hw]) * projected[:hw]
    right = mask * jax.nn.sigmoid(projected[3 * hw :]) * projected[2 * hw : 3 * hw]
    return left.astype(BF16), right.astype(BF16)


def gathered_update(pair, mask, proj, gate, out, gain, mid, orient):
    rows, tokens, _ = pair.shape
    devices = tokens // rows
    floats = pair.astype(F32)
    normed = layer_norm(floats, gain, -1).astype(BF16)
    left, right = wide_factors(normed, mask, proj)
    everywhere = lax.all_gather(right, "row", axis=1, tiled=True)
    if orient == 1:
        c = left.shape[0]
        blocks = left.reshape(c, rows, devices, rows).transpose(2, 1, 3, 0)
        left = lax.all_to_all(blocks, "row", 0, 0, tiled=True)
        left = left.reshape(tokens, rows, c).transpose(2, 0, 1)
    spec = "cik,cjk->cij" if orient == 0 else "cki,ckj->cij"
    summed = jnp.einsum(spec, left, everywhere, preferred_element_type=F32)
    hidden = layer_norm(summed, mid[:, None, None], 0).astype(BF16)
    gating = jax.nn.sigmoid(jnp.einsum("ijd,de->ije", normed, gate, preferred_element_type=F32))
    update = jnp.einsum("cij,cd->ijd", hidden, out, preferred_element_type=F32)
    return (floats + gating * update).astype(BF16)


def shards(pair, pair_mask, proj, gate, out, gain, mid):
    rows, tokens, _ = pair.shape
    if rows == 4 and 2 * tokens == LANES:
        return small_plan(pair, pair_mask, proj, gate, out, gain, mid)
    mask = pair_mask.astype(F32)[None]
    for o in range(2):
        pair = gathered_update(pair, mask, proj[o], gate[o], out[o], gain[o], mid[o], o)
    return pair


def solution(mesh):
    return jax.shard_map(
        shards,
        mesh=mesh,
        in_specs=(P(("groups", "row")), P(("groups", "row")), P(), P(), P(), P(), P()),
        out_specs=P(("groups", "row")),
        check_vma=False,
    )
```

```python
import functools

import jax
import jax.numpy as jnp
from jax import lax
from jax.experimental import pallas as pl
from jax.experimental.pallas import tpu as pltpu
from jax.sharding import PartitionSpec as P

EPS = 1e-05
F32, BF16 = jnp.float32, jnp.bfloat16
LANES = 128
MASK_ROWS = 16
NT = (((1,), (1,)), ((), ()))
VMEM = pltpu.VMEM
IN_VMEM = pl.BlockSpec(memory_space=pltpu.VMEM)
IN_SMEM = pl.BlockSpec(memory_space=pltpu.SMEM)
SMALL = pltpu.CompilerParams(vmem_limit_bytes=8 * 1024 * 1024)


def dot(a, b):
    return jnp.dot(a, b, preferred_element_type=F32)


def dot_nt(a, b):
    return lax.dot_general(a, b, NT, preferred_element_type=F32)


def twice_sigmoid(half):
    return jnp.tanh(half) + 1.0


def iota(shape, axis):
    return lax.broadcasted_iota(jnp.int32, shape, axis)


def one_hot(condition):
    return condition.astype(F32).astype(BF16)


def token_of(t, rows, tokens):
    devices = tokens // rows
    return (t % devices) * rows + t // devices


def column_norm(values, gain):
    average = jnp.mean(values, axis=0, keepdims=True)
    centred = values - average
    variance = jnp.mean(centred * centred, axis=0, keepdims=True)
    return (centred * lax.rsqrt(variance + EPS) * gain).astype(BF16)


def factors(projected, half_mask):
    hw = projected.shape[0] // 4
    left = half_mask * twice_sigmoid(projected[hw : 2 * hw]) * projected[:hw]
    right = half_mask * twice_sigmoid(projected[3 * hw :]) * projected[2 * hw : 3 * hw]
    return left, right


def side_by_side(chunks):
    return jnp.concatenate(chunks, axis=1)


def tile(values, h):
    return values[:, h * LANES : (h + 1) * LANES]


def pack_kernel(rows, tokens, pair_ref, mask_ref, packed_ref):
    channels = pair_ref.shape[-1]
    square = (tokens, tokens)
    by_lane = one_hot(token_of(iota(square, 0), rows, tokens) == iota(square, 1))
    by_token = one_hot(token_of(iota(square, 1), rows, tokens) == iota(square, 0))
    identity = one_hot(iota((channels, channels), 0) == iota((channels, channels), 1))
    masks = 0.5 * dot(one_hot(mask_ref[...] != 0), by_token)
    tiles = rows * tokens // LANES
    for h in range(tiles):
        pair = [dot(by_lane, pair_ref[i]).astype(BF16) for i in (2 * h, 2 * h + 1)]
        chunk = dot_nt(identity, jnp.concatenate(pair, axis=0))
        packed_ref[0, h * channels : (h + 1) * channels, :] = chunk.astype(BF16)
    lines = [
        jnp.concatenate([masks[2 * h : 2 * h + 1], masks[2 * h + 1 : 2 * h + 2]], axis=1)
        for h in range(tiles)
    ]
    shape = (MASK_ROWS, LANES)
    block = jnp.where(iota(shape, 0) < MASK_ROWS // 2, lines[0], lines[1])
    packed_ref[0, tiles * channels :, :] = block.astype(BF16)


def chunk_of(ref, channels, k, h):
    return ref[k, h * channels : (h + 1) * channels, :].astype(F32)


def mask_of(ref, channels, k, h):
    lines = ref[k, -MASK_ROWS:, :].astype(F32)
    return lines[h * MASK_ROWS // 2 : h * MASK_ROWS // 2 + 1]


def prepare_kernel(
    rows, tokens, me_ref, proj_ref, gate_ref, out_ref, gain_ref, mid_ref,
    proj_t_ref, gate_t_ref, out_t_ref, gain_t_ref, mid_t_ref, restore_ref, spread_ref,
):
    devices = tokens // rows

    def flipped(weight):
        return weight.astype(F32).T

    def column(line):
        return jnp.broadcast_to(line, (LANES, line.shape[1])).T

    hw = mid_ref.shape[1]
    is_gate = iota((4 * hw, proj_ref.shape[1]), 0) // hw % 2 == 1
    for o in range(2):
        proj = flipped(proj_ref[o])
        proj_t_ref[o] = jnp.where(is_gate, 0.5 * proj, proj).astype(BF16)
        gate_t_ref[o] = (0.5 * flipped(gate_ref[o])).astype(BF16)
        out_t_ref[o] = (0.5 * flipped(out_ref[o])).astype(BF16)
        gain_t_ref[o] = column(gain_ref[o : o + 1, :])
        mid_t_ref[o] = column(mid_ref[o : o + 1, :])
    shape = (LANES, LANES)
    lane = iota(shape, 1)
    source = lane // tokens * tokens + token_of(lane % tokens, rows, tokens)
    restore_ref[...] = one_hot(source == iota(shape, 0))
    group, lane = iota(shape, 0) // tokens, iota(shape, 0) % tokens
    same = group == iota(shape, 1) // tokens
    for i in range(rows):
        spread_ref[i] = one_hot(same & (lane == i * devices + me_ref[0]))


def early_kernel(counts, *refs):
    block_refs, (proj_ref, gain_ref, left_ref, right_ref, normed_ref) = refs[:-5], refs[-5:]
    channels, tiles = normed_ref.shape[2], normed_ref.shape[1]
    place = 0
    for block_ref, count in zip(block_refs, counts):
        for k in range(count):
            normed = [
                column_norm(chunk_of(block_ref, channels, k, h), gain_ref[0]) for h in range(tiles)
            ]
            projected = dot(proj_ref[0], side_by_side(normed))
            for h in range(tiles):
                normed_ref[place, h] = normed[h]
                left, right = factors(tile(projected, h), mask_of(block_ref, channels, k, h))
                left_ref[place, h] = left
                right_ref[place, h] = right
            place += 1


def both_kernel(rows, tokens, sources, early_groups, me_ref, *refs):
    devices = tokens // rows
    block_refs, refs = refs[: len(sources)], refs[len(sources) :]
    weight_refs, refs = refs[:7], refs[7:]
    proj_ref, gate_ref, out_ref, gain_ref, mid_ref, restore_ref, spread_ref = weight_refs
    ahead = {}
    for group in early_groups:
        for n, m in enumerate(group):
            ahead[m] = refs[:3] + (n,)
        refs = refs[3:]
    (
        result_ref, left_s, right_s, normed_s, sum_s, now_s, second_left_s, second_right_s,
    ) = refs
    channels = gate_ref.shape[1]
    hw = mid_ref.shape[1]
    tiles = rows * tokens // LANES
    me = me_ref[0]

    where = {m: (ref, k) for ref, held in zip(block_refs, sources) for k, m in enumerate(held)}
    later = [m for m in range(devices) if m not in ahead]

    def place(m, h, left, right):
        here = pl.ds((me ^ m) * (hw + 1), hw)
        left_s[h, here, :] = left
        right_s[h, here, :] = right

    for m in later:
        ref, k = where[m]
        normed = [column_norm(chunk_of(ref, channels, k, h), gain_ref[0]) for h in range(tiles)]
        projected = dot(proj_ref[0], side_by_side(normed))
        for h in range(tiles):
            normed_s[later.index(m), h] = normed[h]
            place(m, h, *factors(tile(projected, h), mask_of(ref, channels, k, h)))
    for m, (left_ref, right_ref, _, n) in ahead.items():
        for h in range(tiles):
            place(m, h, left_ref[n, h], right_ref[n, h])

    def normed_of(m, h):
        if m in ahead:
            return ahead[m][2][ahead[m][3], h]
        return normed_s[later.index(m), h]

    low = iota((devices, LANES), 1) < tokens

    def channel_sum(c):
        here = pl.ds(c, devices, stride=hw + 1)
        left = jnp.concatenate([left_s[h, here, :] for h in range(tiles)], axis=0)
        halves = [[], []]
        for h in range(tiles):
            right = right_s[h, here, :]
            turned = pltpu.roll(right, tokens, 1)
            for q in range(2):
                straight, other = (right, turned) if q == 0 else (turned, right)
                halves[0].append(jnp.where(low, straight, 0.0))
                halves[1].append(jnp.where(low, 0.0, other))
        against = jnp.concatenate(halves[0] + halves[1], axis=0).astype(BF16)
        here = pl.ds(c * (tiles * devices + 1), tiles * devices)
        sum_s[here, :] = dot_nt(left.astype(BF16), against)

    for c in range(hw):
        channel_sum(c)

    for m in range(devices):
        ref, k = where[m]
        hidden, first = [], []
        for h in range(tiles):
            summed = sum_s[pl.ds(h * devices + (me ^ m), hw, stride=tiles * devices + 1), :]
            hidden.append(column_norm(summed, mid_ref[0]))
            first.append(normed_of(m, h))
        update = dot(out_ref[0], side_by_side(hidden))
        logits = dot(gate_ref[0], side_by_side(first))
        normed = []
        for h in range(tiles):
            gated = twice_sigmoid(tile(logits, h)) * tile(update, h)
            now = (chunk_of(ref, channels, k, h) + gated).astype(BF16)
            normed.append(column_norm(now.astype(F32), gain_ref[1]))
            if m == 0:
                now_s[h] = now
                now_s[tiles + h] = normed[h]
        projected = dot(proj_ref[1], side_by_side(normed))
        for h in range(tiles):
            left, right = factors(tile(projected, h), mask_of(ref, channels, k, h))
            here = pl.ds((m * tiles + h) * hw, hw)
            second_left_s[here, :] = left.astype(BF16)
            second_right_s[here, :] = right.astype(BF16)

    depth = 2 * hw
    sums = []
    for i in range(0, rows, 2):
        pair = side_by_side([spread_ref[i], spread_ref[i + 1]])
        totals = [jnp.zeros((hw, LANES), F32)] * 2
        for n in range(devices * tiles // 2):
            here = pl.ds(n * depth, depth)
            spread = dot(second_left_s[here, :], pair)
            right = second_right_s[here, :].astype(F32)
            for o in range(2):
                terms = tile(spread, o) * right
                totals[o] = totals[o] + (terms[:hw] + terms[hw:])
        sums += [total + pltpu.roll(total, tokens, 1) for total in totals]
    low = iota((hw, LANES), 1) < tokens
    for h in range(tiles):
        summed = jnp.where(low, sums[2 * h], sums[2 * h + 1])
        update = dot(out_ref[1], column_norm(summed, mid_ref[1]))
        gating = twice_sigmoid(dot(gate_ref[1], now_s[tiles + h]))
        final = (now_s[h].astype(F32) + gating * update).astype(BF16)
        result_ref[h * LANES : (h + 1) * LANES, :] = dot_nt(restore_ref[...], final).astype(BF16)


def exchange(block, partner_bits, devices):
    pairs = [(d, d ^ partner_bits) for d in range(devices)]
    return lax.ppermute(block, "row", pairs)


def small_plan(pair, mask, proj, gate, out, gain, mid):
    rows, tokens, channels = pair.shape
    devices, size, hw = tokens // rows, rows * tokens, out.shape[1]
    tiles = size // LANES
    packed = pl.pallas_call(
        functools.partial(pack_kernel, rows, tokens),
        out_shape=VMEM((1, tiles * channels + MASK_ROWS, LANES), BF16),
        out_specs=IN_VMEM,
        name="pack",
    )(pair, mask)
    me = lax.axis_index("row").reshape(1).astype(jnp.int32)
    weights = pl.pallas_call(
        functools.partial(prepare_kernel, rows, tokens),
        in_specs=[IN_SMEM] + [pl.BlockSpec()] * 5,
        out_shape=(
            VMEM((2, 4 * hw, channels), BF16),
            VMEM((2, channels, channels), BF16),
            VMEM((2, channels, hw), BF16),
            VMEM((2, channels, LANES), F32),
            VMEM((2, hw, LANES), F32),
            VMEM((LANES, LANES), BF16),
            VMEM((rows, LANES, LANES), BF16),
        ),
        out_specs=(IN_VMEM,) * 7,
        name="prepare",
    )(me, proj, gate, out, gain, mid)

    def swapped(group):
        return exchange(jnp.concatenate([held[m] for m in group]), 1, devices)

    def project_early(blocks):
        count = sum(block.shape[0] for block in blocks)
        return pl.pallas_call(
            functools.partial(early_kernel, [block.shape[0] for block in blocks]),
            in_specs=[IN_VMEM] * (len(blocks) + 2),
            out_shape=(
                VMEM((count, tiles, hw, LANES), F32),
                VMEM((count, tiles, hw, LANES), F32),
                VMEM((count, tiles, channels, LANES), BF16),
            ),
            out_specs=(IN_VMEM,) * 3,
            compiler_params=SMALL,
            name="early",
        )(*blocks, weights[0], weights[3])

    held = {0: packed}
    for m in (12, 8, 4, 2):
        held[m] = exchange(packed, m, devices)
    held[12], weights = lax.optimization_barrier((held[12], weights))
    held[14] = exchange(held[12], 2, devices)
    held[6] = exchange(held[2], 4, devices)
    held[10] = exchange(held[8], 2, devices)
    first = (0, 4, 2, 8, 12)
    last = (14, 6, 10)
    swaps = [swapped(first), swapped(last)]
    ahead = project_early([held[m] for m in first + last] + swaps[:1])
    arrays = [held[m] for m in first + last] + swaps
    sources = [(m,) for m in first + last]
    sources += [tuple(m ^ 1 for m in group) for group in (first, last)]
    early_groups = (first + last + sources[-2],)
    result = pl.pallas_call(
        functools.partial(both_kernel, rows, tokens, sources, early_groups),
        out_shape=jax.ShapeDtypeStruct((size, channels), BF16),
        in_specs=[IN_SMEM] + [IN_VMEM] * (len(arrays) + len(weights) + len(ahead)),
        scratch_shapes=[
            pltpu.VMEM((tiles, devices * (hw + 1), LANES), F32),
            pltpu.VMEM((tiles, devices * (hw + 1), LANES), F32),
            pltpu.VMEM((len(last), tiles, channels, LANES), BF16),
            pltpu.VMEM((hw * (devices * tiles + 1), LANES), F32),
            pltpu.VMEM((2 * tiles, channels, LANES), BF16),
            pltpu.VMEM((devices * tiles * hw, LANES), BF16),
            pltpu.VMEM((devices * tiles * hw, LANES), BF16),
        ],
        compiler_params=pltpu.CompilerParams(vmem_limit_bytes=24 * 1024 * 1024),
        name="both",
    )(me, *arrays, *weights, *ahead)
    return result.reshape(pair.shape)


def layer_norm(values, gain, axis):
    average = jnp.mean(values, axis=axis, keepdims=True)
    centred = values - average
    variance = jnp.mean(centred * centred, axis=axis, keepdims=True)
    return centred * lax.rsqrt(variance + EPS) * gain


def wide_factors(normed, mask, proj):
    hw = proj.shape[1] // 4
    projected = jnp.einsum("ijd,de->eij", normed, proj, preferred_element_type=F32)
    left = mask * jax.nn.sigmoid(projected[hw : 2 * hw]) * projected[:hw]
    right = mask * jax.nn.sigmoid(projected[3 * hw :]) * projected[2 * hw : 3 * hw]
    return left.astype(BF16), right.astype(BF16)


def gathered_update(pair, mask, proj, gate, out, gain, mid, orient):
    rows, tokens, _ = pair.shape
    devices = tokens // rows
    floats = pair.astype(F32)
    normed = layer_norm(floats, gain, -1).astype(BF16)
    left, right = wide_factors(normed, mask, proj)
    everywhere = lax.all_gather(right, "row", axis=1, tiled=True)
    if orient == 1:
        c = left.shape[0]
        blocks = left.reshape(c, rows, devices, rows).transpose(2, 1, 3, 0)
        left = lax.all_to_all(blocks, "row", 0, 0, tiled=True)
        left = left.reshape(tokens, rows, c).transpose(2, 0, 1)
    spec = "cik,cjk->cij" if orient == 0 else "cki,ckj->cij"
    summed = jnp.einsum(spec, left, everywhere, preferred_element_type=F32)
    hidden = layer_norm(summed, mid[:, None, None], 0).astype(BF16)
    gating = jax.nn.sigmoid(jnp.einsum("ijd,de->ije", normed, gate, preferred_element_type=F32))
    update = jnp.einsum("cij,cd->ijd", hidden, out, preferred_element_type=F32)
    return (floats + gating * update).astype(BF16)


def shards(pair, pair_mask, proj, gate, out, gain, mid):
    rows, tokens, _ = pair.shape
    if rows == 4 and 2 * tokens == LANES:
        return small_plan(pair, pair_mask, proj, gate, out, gain, mid)
    mask = pair_mask.astype(F32)[None]
    for o in range(2):
        pair = gathered_update(pair, mask, proj[o], gate[o], out[o], gain[o], mid[o], o)
    return pair


def solution(mesh):
    return jax.shard_map(
        shards,
        mesh=mesh,
        in_specs=(P(("groups", "row")), P(("groups", "row")), P(), P(), P(), P(), P()),
        out_specs=P(("groups", "row")),
        check_vma=False,
    )
```

```python
import functools

import jax
import jax.numpy as jnp
from jax import lax
from jax.experimental import pallas as pl
from jax.experimental.pallas import tpu as pltpu
from jax.sharding import PartitionSpec as P

EPS = 1e-05
F32, BF16 = jnp.float32, jnp.bfloat16
LANES = 128
MASK_ROWS = 16
NT = (((1,), (1,)), ((), ()))
VMEM = pltpu.VMEM
IN_VMEM = pl.BlockSpec(memory_space=pltpu.VMEM)
IN_SMEM = pl.BlockSpec(memory_space=pltpu.SMEM)
SMALL = pltpu.CompilerParams(vmem_limit_bytes=8 * 1024 * 1024)


def dot(a, b):
    return jnp.dot(a, b, preferred_element_type=F32)


def dot_nt(a, b):
    return lax.dot_general(a, b, NT, preferred_element_type=F32)


def twice_sigmoid(half):
    return jnp.tanh(half) + 1.0


def iota(shape, axis):
    return lax.broadcasted_iota(jnp.int32, shape, axis)


def one_hot(condition):
    return condition.astype(F32).astype(BF16)


def token_of(t, rows, tokens):
    devices = tokens // rows
    return (t % devices) * rows + t // devices


def column_norm(values, gain):
    average = jnp.mean(values, axis=0, keepdims=True)
    centred = values - average
    variance = jnp.mean(centred * centred, axis=0, keepdims=True)
    return (centred * lax.rsqrt(variance + EPS) * gain).astype(BF16)


def factors(projected, half_mask):
    hw = projected.shape[0] // 4
    left = half_mask * twice_sigmoid(projected[hw : 2 * hw]) * projected[:hw]
    right = half_mask * twice_sigmoid(projected[3 * hw :]) * projected[2 * hw : 3 * hw]
    return left, right


def side_by_side(chunks):
    return jnp.concatenate(chunks, axis=1)


def tile(values, h):
    return values[:, h * LANES : (h + 1) * LANES]


def pack_kernel(rows, tokens, pair_ref, mask_ref, packed_ref):
    channels = pair_ref.shape[-1]
    square = (tokens, tokens)
    by_lane = one_hot(token_of(iota(square, 0), rows, tokens) == iota(square, 1))
    by_token = one_hot(token_of(iota(square, 1), rows, tokens) == iota(square, 0))
    identity = one_hot(iota((channels, channels), 0) == iota((channels, channels), 1))
    masks = 0.5 * dot(one_hot(mask_ref[...] != 0), by_token)
    tiles = rows * tokens // LANES
    for h in range(tiles):
        pair = [dot(by_lane, pair_ref[i]).astype(BF16) for i in (2 * h, 2 * h + 1)]
        chunk = dot_nt(identity, jnp.concatenate(pair, axis=0))
        packed_ref[0, h * channels : (h + 1) * channels, :] = chunk.astype(BF16)
    lines = [
        jnp.concatenate([masks[2 * h : 2 * h + 1], masks[2 * h + 1 : 2 * h + 2]], axis=1)
        for h in range(tiles)
    ]
    shape = (MASK_ROWS, LANES)
    block = jnp.where(iota(shape, 0) < MASK_ROWS // 2, lines[0], lines[1])
    packed_ref[0, tiles * channels :, :] = block.astype(BF16)


def chunk_of(ref, channels, k, h):
    return ref[k, h * channels : (h + 1) * channels, :].astype(F32)


def mask_of(ref, channels, k, h):
    lines = ref[k, -MASK_ROWS:, :].astype(F32)
    return lines[h * MASK_ROWS // 2 : h * MASK_ROWS // 2 + 1]


def prepare_kernel(
    rows, tokens, me_ref, proj_ref, gate_ref, out_ref, gain_ref, mid_ref,
    proj_t_ref, gate_t_ref, out_t_ref, gain_t_ref, mid_t_ref, restore_ref, spread_ref,
):
    devices = tokens // rows

    def flipped(weight):
        return weight.astype(F32).T

    def column(line):
        return jnp.broadcast_to(line, (LANES, line.shape[1])).T

    hw = mid_ref.shape[1]
    is_gate = iota((4 * hw, proj_ref.shape[1]), 0) // hw % 2 == 1
    for o in range(2):
        proj = flipped(proj_ref[o])
        proj_t_ref[o] = jnp.where(is_gate, 0.5 * proj, proj).astype(BF16)
        gate_t_ref[o] = (0.5 * flipped(gate_ref[o])).astype(BF16)
        out_t_ref[o] = (0.5 * flipped(out_ref[o])).astype(BF16)
        gain_t_ref[o] = column(gain_ref[o : o + 1, :])
        mid_t_ref[o] = column(mid_ref[o : o + 1, :])
    shape = (LANES, LANES)
    lane = iota(shape, 1)
    source = lane // tokens * tokens + token_of(lane % tokens, rows, tokens)
    restore_ref[...] = one_hot(source == iota(shape, 0))
    group, lane = iota(shape, 0) // tokens, iota(shape, 0) % tokens
    same = group == iota(shape, 1) // tokens
    for i in range(rows):
        spread_ref[i] = one_hot(same & (lane == i * devices + me_ref[0]))


def early_kernel(counts, *refs):
    block_refs, (proj_ref, gain_ref, left_ref, right_ref, normed_ref) = refs[:-5], refs[-5:]
    channels, tiles = normed_ref.shape[2], normed_ref.shape[1]
    place = 0
    for block_ref, count in zip(block_refs, counts):
        for k in range(count):
            normed = [
                column_norm(chunk_of(block_ref, channels, k, h), gain_ref[0]) for h in range(tiles)
            ]
            projected = dot(proj_ref[0], side_by_side(normed))
            for h in range(tiles):
                normed_ref[place, h] = normed[h]
                left, right = factors(tile(projected, h), mask_of(block_ref, channels, k, h))
                left_ref[place, h] = left
                right_ref[place, h] = right
            place += 1


def both_kernel(rows, tokens, sources, early_groups, me_ref, *refs):
    devices = tokens // rows
    block_refs, refs = refs[: len(sources)], refs[len(sources) :]
    weight_refs, refs = refs[:7], refs[7:]
    proj_ref, gate_ref, out_ref, gain_ref, mid_ref, restore_ref, spread_ref = weight_refs
    ahead = {}
    for group in early_groups:
        for n, m in enumerate(group):
            ahead[m] = refs[:3] + (n,)
        refs = refs[3:]
    (
        result_ref, left_s, right_s, normed_s, sum_s, now_s, second_left_s, second_right_s,
    ) = refs
    channels = gate_ref.shape[1]
    hw = mid_ref.shape[1]
    tiles = rows * tokens // LANES
    me = me_ref[0]

    where = {m: (ref, k) for ref, held in zip(block_refs, sources) for k, m in enumerate(held)}
    later = [m for m in range(devices) if m not in ahead]

    def place(m, h, left, right):
        here = pl.ds((me ^ m) * (hw + 1), hw)
        left_s[h, here, :] = left
        right_s[h, here, :] = right

    for m in later:
        ref, k = where[m]
        normed = [column_norm(chunk_of(ref, channels, k, h), gain_ref[0]) for h in range(tiles)]
        projected = dot(proj_ref[0], side_by_side(normed))
        for h in range(tiles):
            normed_s[later.index(m), h] = normed[h]
            place(m, h, *factors(tile(projected, h), mask_of(ref, channels, k, h)))
    for m, (left_ref, right_ref, _, n) in ahead.items():
        for h in range(tiles):
            place(m, h, left_ref[n, h], right_ref[n, h])

    def normed_of(m, h):
        if m in ahead:
            return ahead[m][2][ahead[m][3], h]
        return normed_s[later.index(m), h]

    low = iota((devices, LANES), 1) < tokens

    def channel_sum(c):
        here = pl.ds(c, devices, stride=hw + 1)
        left = jnp.concatenate([left_s[h, here, :] for h in range(tiles)], axis=0)
        halves = [[], []]
        for h in range(tiles):
            right = right_s[h, here, :]
            turned = pltpu.roll(right, tokens, 1)
            for q in range(2):
                straight, other = (right, turned) if q == 0 else (turned, right)
                halves[0].append(jnp.where(low, straight, 0.0))
                halves[1].append(jnp.where(low, 0.0, other))
        against = jnp.concatenate(halves[0] + halves[1], axis=0).astype(BF16)
        here = pl.ds(c * (tiles * devices + 1), tiles * devices)
        sum_s[here, :] = dot_nt(left.astype(BF16), against)

    for c in range(hw):
        channel_sum(c)

    for m in range(devices):
        ref, k = where[m]
        hidden, first = [], []
        for h in range(tiles):
            summed = sum_s[pl.ds(h * devices + (me ^ m), hw, stride=tiles * devices + 1), :]
            hidden.append(column_norm(summed, mid_ref[0]))
            first.append(normed_of(m, h))
        update = dot(out_ref[0], side_by_side(hidden))
        logits = dot(gate_ref[0], side_by_side(first))
        normed = []
        for h in range(tiles):
            gated = twice_sigmoid(tile(logits, h)) * tile(update, h)
            now = (chunk_of(ref, channels, k, h) + gated).astype(BF16)
            normed.append(column_norm(now.astype(F32), gain_ref[1]))
            if m == 0:
                now_s[h] = now
                now_s[tiles + h] = normed[h]
        projected = dot(proj_ref[1], side_by_side(normed))
        for h in range(tiles):
            left, right = factors(tile(projected, h), mask_of(ref, channels, k, h))
            here = pl.ds((m * tiles + h) * hw, hw)
            second_left_s[here, :] = left.astype(BF16)
            second_right_s[here, :] = right.astype(BF16)

    depth = 2 * hw
    sums = []
    for i in range(0, rows, 2):
        pair = side_by_side([spread_ref[i], spread_ref[i + 1]])
        totals = [jnp.zeros((hw, LANES), F32)] * 2
        for n in range(devices * tiles // 2):
            here = pl.ds(n * depth, depth)
            spread = dot(second_left_s[here, :], pair)
            right = second_right_s[here, :].astype(F32)
            for o in range(2):
                terms = tile(spread, o) * right
                totals[o] = totals[o] + (terms[:hw] + terms[hw:])
        sums += [total + pltpu.roll(total, tokens, 1) for total in totals]
    low = iota((hw, LANES), 1) < tokens
    for h in range(tiles):
        summed = jnp.where(low, sums[2 * h], sums[2 * h + 1])
        update = dot(out_ref[1], column_norm(summed, mid_ref[1]))
        gating = twice_sigmoid(dot(gate_ref[1], now_s[tiles + h]))
        final = (now_s[h].astype(F32) + gating * update).astype(BF16)
        result_ref[h * LANES : (h + 1) * LANES, :] = dot_nt(restore_ref[...], final).astype(BF16)


def exchange(block, partner_bits, devices):
    pairs = [(d, d ^ partner_bits) for d in range(devices)]
    return lax.ppermute(block, "row", pairs)


def small_plan(pair, mask, proj, gate, out, gain, mid):
    rows, tokens, channels = pair.shape
    devices, size, hw = tokens // rows, rows * tokens, out.shape[1]
    tiles = size // LANES
    packed = pl.pallas_call(
        functools.partial(pack_kernel, rows, tokens),
        out_shape=VMEM((1, tiles * channels + MASK_ROWS, LANES), BF16),
        out_specs=IN_VMEM,
        name="pack",
    )(pair, mask)
    me = lax.axis_index("row").reshape(1).astype(jnp.int32)
    weights = pl.pallas_call(
        functools.partial(prepare_kernel, rows, tokens),
        in_specs=[IN_SMEM] + [pl.BlockSpec()] * 5,
        out_shape=(
            VMEM((2, 4 * hw, channels), BF16),
            VMEM((2, channels, channels), BF16),
            VMEM((2, channels, hw), BF16),
            VMEM((2, channels, LANES), F32),
            VMEM((2, hw, LANES), F32),
            VMEM((LANES, LANES), BF16),
            VMEM((rows, LANES, LANES), BF16),
        ),
        out_specs=(IN_VMEM,) * 7,
        name="prepare",
    )(me, proj, gate, out, gain, mid)

    def swapped(group):
        return exchange(jnp.concatenate([held[m] for m in group]), 1, devices)

    def project_early(blocks):
        count = sum(block.shape[0] for block in blocks)
        return pl.pallas_call(
            functools.partial(early_kernel, [block.shape[0] for block in blocks]),
            in_specs=[IN_VMEM] * (len(blocks) + 2),
            out_shape=(
                VMEM((count, tiles, hw, LANES), F32),
                VMEM((count, tiles, hw, LANES), F32),
                VMEM((count, tiles, channels, LANES), BF16),
            ),
            out_specs=(IN_VMEM,) * 3,
            compiler_params=SMALL,
            name="early",
        )(*blocks, weights[0], weights[3])

    held = {0: packed}
    for m in (12, 8, 4, 2):
        held[m] = exchange(packed, m, devices)
    held[12], weights = lax.optimization_barrier((held[12], weights))
    held[14] = exchange(held[12], 2, devices)
    held[6] = exchange(held[2], 4, devices)
    held[10] = exchange(held[8], 2, devices)
    first = (0, 4, 8, 2, 12)
    last = (14, 6, 10)
    swaps = [swapped(first), swapped(last)]
    ahead = project_early([held[m] for m in first + last] + swaps[:1])
    arrays = [held[m] for m in first + last] + swaps
    sources = [(m,) for m in first + last]
    sources += [tuple(m ^ 1 for m in group) for group in (first, last)]
    early_groups = (first + last + sources[-2],)
    result = pl.pallas_call(
        functools.partial(both_kernel, rows, tokens, sources, early_groups),
        out_shape=jax.ShapeDtypeStruct((size, channels), BF16),
        in_specs=[IN_SMEM] + [IN_VMEM] * (len(arrays) + len(weights) + len(ahead)),
        scratch_shapes=[
            pltpu.VMEM((tiles, devices * (hw + 1), LANES), F32),
            pltpu.VMEM((tiles, devices * (hw + 1), LANES), F32),
            pltpu.VMEM((len(last), tiles, channels, LANES), BF16),
            pltpu.VMEM((hw * (devices * tiles + 1), LANES), F32),
            pltpu.VMEM((2 * tiles, channels, LANES), BF16),
            pltpu.VMEM((devices * tiles * hw, LANES), BF16),
            pltpu.VMEM((devices * tiles * hw, LANES), BF16),
        ],
        compiler_params=pltpu.CompilerParams(vmem_limit_bytes=24 * 1024 * 1024),
        name="both",
    )(me, *arrays, *weights, *ahead)
    return result.reshape(pair.shape)


def layer_norm(values, gain, axis):
    average = jnp.mean(values, axis=axis, keepdims=True)
    centred = values - average
    variance = jnp.mean(centred * centred, axis=axis, keepdims=True)
    return centred * lax.rsqrt(variance + EPS) * gain


def wide_factors(normed, mask, proj):
    hw = proj.shape[1] // 4
    projected = jnp.einsum("ijd,de->eij", normed, proj, preferred_element_type=F32)
    left = mask * jax.nn.sigmoid(projected[hw : 2 * hw]) * projected[:hw]
    right = mask * jax.nn.sigmoid(projected[3 * hw :]) * projected[2 * hw : 3 * hw]
    return left.astype(BF16), right.astype(BF16)


def gathered_update(pair, mask, proj, gate, out, gain, mid, orient):
    rows, tokens, _ = pair.shape
    devices = tokens // rows
    floats = pair.astype(F32)
    normed = layer_norm(floats, gain, -1).astype(BF16)
    left, right = wide_factors(normed, mask, proj)
    everywhere = lax.all_gather(right, "row", axis=1, tiled=True)
    if orient == 1:
        c = left.shape[0]
        blocks = left.reshape(c, rows, devices, rows).transpose(2, 1, 3, 0)
        left = lax.all_to_all(blocks, "row", 0, 0, tiled=True)
        left = left.reshape(tokens, rows, c).transpose(2, 0, 1)
    spec = "cik,cjk->cij" if orient == 0 else "cki,ckj->cij"
    summed = jnp.einsum(spec, left, everywhere, preferred_element_type=F32)
    hidden = layer_norm(summed, mid[:, None, None], 0).astype(BF16)
    gating = jax.nn.sigmoid(jnp.einsum("ijd,de->ije", normed, gate, preferred_element_type=F32))
    update = jnp.einsum("cij,cd->ijd", hidden, out, preferred_element_type=F32)
    return (floats + gating * update).astype(BF16)


def shards(pair, pair_mask, proj, gate, out, gain, mid):
    rows, tokens, _ = pair.shape
    if rows == 4 and 2 * tokens == LANES:
        return small_plan(pair, pair_mask, proj, gate, out, gain, mid)
    mask = pair_mask.astype(F32)[None]
    for o in range(2):
        pair = gathered_update(pair, mask, proj[o], gate[o], out[o], gain[o], mid[o], o)
    return pair


def solution(mesh):
    return jax.shard_map(
        shards,
        mesh=mesh,
        in_specs=(P(("groups", "row")), P(("groups", "row")), P(), P(), P(), P(), P()),
        out_specs=P(("groups", "row")),
        check_vma=False,
    )
```

```python
import functools

import jax
import jax.numpy as jnp
from jax import lax
from jax.experimental import pallas as pl
from jax.experimental.pallas import tpu as pltpu
from jax.sharding import PartitionSpec as P

EPS = 1e-05
F32, BF16 = jnp.float32, jnp.bfloat16
LANES = 128
MASK_ROWS = 16
NT = (((1,), (1,)), ((), ()))
VMEM = pltpu.VMEM
IN_VMEM = pl.BlockSpec(memory_space=pltpu.VMEM)
IN_SMEM = pl.BlockSpec(memory_space=pltpu.SMEM)
SMALL = pltpu.CompilerParams(vmem_limit_bytes=8 * 1024 * 1024)


def dot(a, b):
    return jnp.dot(a, b, preferred_element_type=F32)


def dot_nt(a, b):
    return lax.dot_general(a, b, NT, preferred_element_type=F32)


def twice_sigmoid(half):
    return jnp.tanh(half) + 1.0


def iota(shape, axis):
    return lax.broadcasted_iota(jnp.int32, shape, axis)


def one_hot(condition):
    return condition.astype(F32).astype(BF16)


def token_of(t, rows, tokens):
    devices = tokens // rows
    return (t % devices) * rows + t // devices


def column_norm(values, gain):
    average = jnp.mean(values, axis=0, keepdims=True)
    centred = values - average
    variance = jnp.mean(centred * centred, axis=0, keepdims=True)
    return (centred * lax.rsqrt(variance + EPS) * gain).astype(BF16)


def factors(projected, half_mask):
    hw = projected.shape[0] // 4
    left = half_mask * twice_sigmoid(projected[hw : 2 * hw]) * projected[:hw]
    right = half_mask * twice_sigmoid(projected[3 * hw :]) * projected[2 * hw : 3 * hw]
    return left, right


def side_by_side(chunks):
    return jnp.concatenate(chunks, axis=1)


def tile(values, h):
    return values[:, h * LANES : (h + 1) * LANES]


def pack_kernel(rows, tokens, pair_ref, mask_ref, packed_ref):
    channels = pair_ref.shape[-1]
    square = (tokens, tokens)
    by_lane = one_hot(token_of(iota(square, 0), rows, tokens) == iota(square, 1))
    by_token = one_hot(token_of(iota(square, 1), rows, tokens) == iota(square, 0))
    identity = one_hot(iota((channels, channels), 0) == iota((channels, channels), 1))
    masks = 0.5 * dot(one_hot(mask_ref[...] != 0), by_token)
    tiles = rows * tokens // LANES
    for h in range(tiles):
        pair = [dot(by_lane, pair_ref[i]).astype(BF16) for i in (2 * h, 2 * h + 1)]
        chunk = dot_nt(identity, jnp.concatenate(pair, axis=0))
        packed_ref[0, h * channels : (h + 1) * channels, :] = chunk.astype(BF16)
    lines = [
        jnp.concatenate([masks[2 * h : 2 * h + 1], masks[2 * h + 1 : 2 * h + 2]], axis=1)
        for h in range(tiles)
    ]
    shape = (MASK_ROWS, LANES)
    block = jnp.where(iota(shape, 0) < MASK_ROWS // 2, lines[0], lines[1])
    packed_ref[0, tiles * channels :, :] = block.astype(BF16)


def chunk_of(ref, channels, k, h):
    return ref[k, h * channels : (h + 1) * channels, :].astype(F32)


def mask_of(ref, channels, k, h):
    lines = ref[k, -MASK_ROWS:, :].astype(F32)
    return lines[h * MASK_ROWS // 2 : h * MASK_ROWS // 2 + 1]


def prepare_kernel(
    rows, tokens, me_ref, proj_ref, gate_ref, out_ref, gain_ref, mid_ref,
    proj_t_ref, gate_t_ref, out_t_ref, gain_t_ref, mid_t_ref, restore_ref, spread_ref,
):
    devices = tokens // rows

    def flipped(weight):
        return weight.astype(F32).T

    def column(line):
        return jnp.broadcast_to(line, (LANES, line.shape[1])).T

    hw = mid_ref.shape[1]
    is_gate = iota((4 * hw, proj_ref.shape[1]), 0) // hw % 2 == 1
    for o in range(2):
        proj = flipped(proj_ref[o])
        proj_t_ref[o] = jnp.where(is_gate, 0.5 * proj, proj).astype(BF16)
        gate_t_ref[o] = (0.5 * flipped(gate_ref[o])).astype(BF16)
        out_t_ref[o] = (0.5 * flipped(out_ref[o])).astype(BF16)
        gain_t_ref[o] = column(gain_ref[o : o + 1, :])
        mid_t_ref[o] = column(mid_ref[o : o + 1, :])
    shape = (LANES, LANES)
    lane = iota(shape, 1)
    source = lane // tokens * tokens + token_of(lane % tokens, rows, tokens)
    restore_ref[...] = one_hot(source == iota(shape, 0))
    group, lane = iota(shape, 0) // tokens, iota(shape, 0) % tokens
    same = group == iota(shape, 1) // tokens
    for i in range(rows):
        spread_ref[i] = one_hot(same & (lane == i * devices + me_ref[0]))


def place(me, m, h, left_ref, right_ref, left, right):
    hw = left.shape[0]
    here = pl.ds((me ^ m) * (hw + 1), hw)
    left_ref[h, here, :] = left
    right_ref[h, here, :] = right


def early_kernel(held, me_ref, *refs):
    block_refs, (proj_ref, gain_ref, left_ref, right_ref, normed_ref) = refs[:-5], refs[-5:]
    channels, tiles = normed_ref.shape[2], normed_ref.shape[1]
    n = 0
    for block_ref in block_refs:
        for k in range(block_ref.shape[0]):
            normed = [
                column_norm(chunk_of(block_ref, channels, k, h), gain_ref[0]) for h in range(tiles)
            ]
            projected = dot(proj_ref[0], side_by_side(normed))
            for h in range(tiles):
                normed_ref[n, h] = normed[h]
                both = factors(tile(projected, h), mask_of(block_ref, channels, k, h))
                place(me_ref[0], held[n], h, left_ref, right_ref, *both)
            n += 1


def both_kernel(rows, tokens, sources, early, me_ref, *refs):
    devices = tokens // rows
    block_refs, refs = refs[: len(sources)], refs[len(sources) :]
    weight_refs, refs = refs[:7], refs[7:]
    proj_ref, gate_ref, out_ref, gain_ref, mid_ref, restore_ref, spread_ref = weight_refs
    (
        _, _, early_normed_ref, result_ref, left_s, right_s,
        normed_s, sum_s, now_s, second_left_s, second_right_s,
    ) = refs
    channels = gate_ref.shape[1]
    hw = mid_ref.shape[1]
    tiles = rows * tokens // LANES
    me = me_ref[0]

    where = {m: (ref, k) for ref, held in zip(block_refs, sources) for k, m in enumerate(held)}
    later = [m for m in range(devices) if m not in early]
    for m in later:
        ref, k = where[m]
        normed = [column_norm(chunk_of(ref, channels, k, h), gain_ref[0]) for h in range(tiles)]
        projected = dot(proj_ref[0], side_by_side(normed))
        for h in range(tiles):
            normed_s[later.index(m), h] = normed[h]
            both = factors(tile(projected, h), mask_of(ref, channels, k, h))
            place(me, m, h, left_s, right_s, *both)

    def normed_of(m, h):
        if m in early:
            return early_normed_ref[early.index(m), h]
        return normed_s[later.index(m), h]

    in_low = one_hot(iota((devices, LANES), 1) < tokens)
    in_high = one_hot(iota((devices, LANES), 1) >= tokens)

    def channel_sum(c):
        here = pl.ds(c, devices, stride=hw + 1)
        left = jnp.concatenate([left_s[h, here, :] for h in range(tiles)], axis=0)
        halves = [[], []]
        for h in range(tiles):
            right = right_s[h, here, :]
            turned = pltpu.roll(right, tokens, 1).astype(BF16)
            right = right.astype(BF16)
            halves[0] += [right * in_low, turned * in_low]
            halves[1] += [turned * in_high, right * in_high]
        against = jnp.concatenate(halves[0] + halves[1], axis=0)
        here = pl.ds(c * (tiles * devices + 1), tiles * devices)
        sum_s[here, :] = dot_nt(left.astype(BF16), against)

    for c in range(hw):
        channel_sum(c)

    for m in range(devices):
        ref, k = where[m]
        hidden, first = [], []
        for h in range(tiles):
            summed = sum_s[pl.ds(h * devices + (me ^ m), hw, stride=tiles * devices + 1), :]
            hidden.append(column_norm(summed, mid_ref[0]))
            first.append(normed_of(m, h))
        update = dot(out_ref[0], side_by_side(hidden))
        logits = dot(gate_ref[0], side_by_side(first))
        normed = []
        for h in range(tiles):
            gated = twice_sigmoid(tile(logits, h)) * tile(update, h)
            now = (chunk_of(ref, channels, k, h) + gated).astype(BF16)
            normed.append(column_norm(now.astype(F32), gain_ref[1]))
            if m == 0:
                now_s[h] = now
                now_s[tiles + h] = normed[h]
        projected = dot(proj_ref[1], side_by_side(normed))
        for h in range(tiles):
            left, right = factors(tile(projected, h), mask_of(ref, channels, k, h))
            here = pl.ds((m * tiles + h) * hw, hw)
            second_left_s[here, :] = left.astype(BF16)
            second_right_s[here, :] = right.astype(BF16)

    depth = 2 * hw
    sums = []
    for i in range(0, rows, 2):
        pair = side_by_side([spread_ref[i], spread_ref[i + 1]])
        totals = [jnp.zeros((hw, LANES), F32)] * 2
        for n in range(devices * tiles // 2):
            here = pl.ds(n * depth, depth)
            spread = dot(second_left_s[here, :], pair)
            right = second_right_s[here, :].astype(F32)
            for o in range(2):
                terms = tile(spread, o) * right
                totals[o] = totals[o] + (terms[:hw] + terms[hw:])
        sums += [total + pltpu.roll(total, tokens, 1) for total in totals]
    low = iota((hw, LANES), 1) < tokens
    for h in range(tiles):
        summed = jnp.where(low, sums[2 * h], sums[2 * h + 1])
        update = dot(out_ref[1], column_norm(summed, mid_ref[1]))
        gating = twice_sigmoid(dot(gate_ref[1], now_s[tiles + h]))
        final = (now_s[h].astype(F32) + gating * update).astype(BF16)
        result_ref[h * LANES : (h + 1) * LANES, :] = dot_nt(restore_ref[...], final).astype(BF16)


def exchange(block, partner_bits, devices):
    pairs = [(d, d ^ partner_bits) for d in range(devices)]
    return lax.ppermute(block, "row", pairs)


def small_plan(pair, mask, proj, gate, out, gain, mid):
    rows, tokens, channels = pair.shape
    devices, size, hw = tokens // rows, rows * tokens, out.shape[1]
    tiles = size // LANES
    packed = pl.pallas_call(
        functools.partial(pack_kernel, rows, tokens),
        out_shape=VMEM((1, tiles * channels + MASK_ROWS, LANES), BF16),
        out_specs=IN_VMEM,
        name="pack",
    )(pair, mask)
    me = lax.axis_index("row").reshape(1).astype(jnp.int32)
    weights = pl.pallas_call(
        functools.partial(prepare_kernel, rows, tokens),
        in_specs=[IN_SMEM] + [pl.BlockSpec()] * 5,
        out_shape=(
            VMEM((2, 4 * hw, channels), BF16),
            VMEM((2, channels, channels), BF16),
            VMEM((2, channels, hw), BF16),
            VMEM((2, channels, LANES), F32),
            VMEM((2, hw, LANES), F32),
            VMEM((LANES, LANES), BF16),
            VMEM((rows, LANES, LANES), BF16),
        ),
        out_specs=(IN_VMEM,) * 7,
        name="prepare",
    )(me, proj, gate, out, gain, mid)

    def swapped(group):
        return exchange(jnp.concatenate([held[m] for m in group]), 1, devices)

    factor = VMEM((tiles, devices * (hw + 1), LANES), F32)

    def project_early(blocks, held_there):
        normed = VMEM((len(held_there), tiles, channels, LANES), BF16)
        return pl.pallas_call(
            functools.partial(early_kernel, held_there),
            in_specs=[IN_SMEM] + [IN_VMEM] * (len(blocks) + 2),
            out_shape=(factor, factor, normed),
            out_specs=(IN_VMEM,) * 3,
            compiler_params=SMALL,
            name="early",
        )(me, *blocks, weights[0], weights[3])

    held = {0: packed}
    for m in (12, 8, 4, 2):
        held[m] = exchange(packed, m, devices)
    held[12], weights = lax.optimization_barrier((held[12], weights))
    held[14] = exchange(held[12], 2, devices)
    held[6] = exchange(held[2], 4, devices)
    held[10] = exchange(held[8], 2, devices)
    first = (0, 4, 8, 2, 12)
    last = (14, 6, 10)
    swaps = [swapped(first), swapped(last)]
    early = first + last + tuple(m ^ 1 for m in first)
    ahead = project_early([held[m] for m in first + last] + swaps[:1], early)
    arrays = [held[m] for m in first + last] + swaps
    sources = [(m,) for m in first + last]
    sources += [tuple(m ^ 1 for m in group) for group in (first, last)]
    result, _, _ = pl.pallas_call(
        functools.partial(both_kernel, rows, tokens, sources, early),
        out_shape=(jax.ShapeDtypeStruct((size, channels), BF16), factor, factor),
        in_specs=[IN_SMEM] + [IN_VMEM] * (len(arrays) + len(weights) + len(ahead)),
        out_specs=(pl.BlockSpec(), IN_VMEM, IN_VMEM),
        input_output_aliases={1 + len(arrays) + len(weights) + n: 1 + n for n in range(2)},
        scratch_shapes=[
            pltpu.VMEM((len(last), tiles, channels, LANES), BF16),
            pltpu.VMEM((hw * (devices * tiles + 1), LANES), F32),
            pltpu.VMEM((2 * tiles, channels, LANES), BF16),
            pltpu.VMEM((devices * tiles * hw, LANES), BF16),
            pltpu.VMEM((devices * tiles * hw, LANES), BF16),
        ],
        compiler_params=pltpu.CompilerParams(vmem_limit_bytes=24 * 1024 * 1024),
        name="both",
    )(me, *arrays, *weights, *ahead)
    return result.reshape(pair.shape)


def layer_norm(values, gain, axis):
    average = jnp.mean(values, axis=axis, keepdims=True)
    centred = values - average
    variance = jnp.mean(centred * centred, axis=axis, keepdims=True)
    return centred * lax.rsqrt(variance + EPS) * gain


def wide_factors(normed, mask, proj):
    hw = proj.shape[1] // 4
    projected = jnp.einsum("ijd,de->eij", normed, proj, preferred_element_type=F32)
    left = mask * jax.nn.sigmoid(projected[hw : 2 * hw]) * projected[:hw]
    right = mask * jax.nn.sigmoid(projected[3 * hw :]) * projected[2 * hw : 3 * hw]
    return left.astype(BF16), right.astype(BF16)


def gathered_update(pair, mask, proj, gate, out, gain, mid, orient):
    rows, tokens, _ = pair.shape
    devices = tokens // rows
    floats = pair.astype(F32)
    normed = layer_norm(floats, gain, -1).astype(BF16)
    left, right = wide_factors(normed, mask, proj)
    everywhere = lax.all_gather(right, "row", axis=1, tiled=True)
    if orient == 1:
        c = left.shape[0]
        blocks = left.reshape(c, rows, devices, rows).transpose(2, 1, 3, 0)
        left = lax.all_to_all(blocks, "row", 0, 0, tiled=True)
        left = left.reshape(tokens, rows, c).transpose(2, 0, 1)
    spec = "cik,cjk->cij" if orient == 0 else "cki,ckj->cij"
    summed = jnp.einsum(spec, left, everywhere, preferred_element_type=F32)
    hidden = layer_norm(summed, mid[:, None, None], 0).astype(BF16)
    gating = jax.nn.sigmoid(jnp.einsum("ijd,de->ije", normed, gate, preferred_element_type=F32))
    update = jnp.einsum("cij,cd->ijd", hidden, out, preferred_element_type=F32)
    return (floats + gating * update).astype(BF16)


def shards(pair, pair_mask, proj, gate, out, gain, mid):
    rows, tokens, _ = pair.shape
    if rows == 4 and 2 * tokens == LANES:
        return small_plan(pair, pair_mask, proj, gate, out, gain, mid)
    mask = pair_mask.astype(F32)[None]
    for o in range(2):
        pair = gathered_update(pair, mask, proj[o], gate[o], out[o], gain[o], mid[o], o)
    return pair


def solution(mesh):
    return jax.shard_map(
        shards,
        mesh=mesh,
        in_specs=(P(("groups", "row")), P(("groups", "row")), P(), P(), P(), P(), P()),
        out_specs=P(("groups", "row")),
        check_vma=False,
    )
```

```python
import functools

import jax
import jax.numpy as jnp
from jax import lax
from jax.experimental import pallas as pl
from jax.experimental.pallas import tpu as pltpu
from jax.sharding import PartitionSpec as P

EPS = 1e-05
F32, BF16 = jnp.float32, jnp.bfloat16
LANES = 128
MASK_ROWS = 16
NT = (((1,), (1,)), ((), ()))
VMEM = pltpu.VMEM
IN_VMEM = pl.BlockSpec(memory_space=pltpu.VMEM)
IN_SMEM = pl.BlockSpec(memory_space=pltpu.SMEM)
SMALL = pltpu.CompilerParams(vmem_limit_bytes=8 * 1024 * 1024)


def dot(a, b):
    return jnp.dot(a, b, preferred_element_type=F32)


def dot_nt(a, b):
    return lax.dot_general(a, b, NT, preferred_element_type=F32)


def twice_sigmoid(half):
    return jnp.tanh(half) + 1.0


def iota(shape, axis):
    return lax.broadcasted_iota(jnp.int32, shape, axis)


def one_hot(condition):
    return condition.astype(F32).astype(BF16)


def token_of(t, rows, tokens):
    devices = tokens // rows
    return (t % devices) * rows + t // devices


def column_norm(values, gain):
    average = jnp.mean(values, axis=0, keepdims=True)
    centred = values - average
    variance = jnp.mean(centred * centred, axis=0, keepdims=True)
    return (centred * lax.rsqrt(variance + EPS) * gain).astype(BF16)


def factors(projected, half_mask):
    hw = projected.shape[0] // 4
    left = half_mask * twice_sigmoid(projected[hw : 2 * hw]) * projected[:hw]
    right = half_mask * twice_sigmoid(projected[3 * hw :]) * projected[2 * hw : 3 * hw]
    return left, right


def side_by_side(chunks):
    return jnp.concatenate(chunks, axis=1)


def tile(values, h):
    return values[:, h * LANES : (h + 1) * LANES]


def pack_kernel(rows, tokens, pair_ref, mask_ref, packed_ref):
    channels = pair_ref.shape[-1]
    square = (tokens, tokens)
    by_lane = one_hot(token_of(iota(square, 0), rows, tokens) == iota(square, 1))
    by_token = one_hot(token_of(iota(square, 1), rows, tokens) == iota(square, 0))
    identity = one_hot(iota((channels, channels), 0) == iota((channels, channels), 1))
    masks = 0.5 * dot(one_hot(mask_ref[...] != 0), by_token)
    tiles = rows * tokens // LANES
    for h in range(tiles):
        pair = [dot(by_lane, pair_ref[i]).astype(BF16) for i in (2 * h, 2 * h + 1)]
        chunk = dot_nt(identity, jnp.concatenate(pair, axis=0))
        packed_ref[0, h * channels : (h + 1) * channels, :] = chunk.astype(BF16)
    lines = [
        jnp.concatenate([masks[2 * h : 2 * h + 1], masks[2 * h + 1 : 2 * h + 2]], axis=1)
        for h in range(tiles)
    ]
    shape = (MASK_ROWS, LANES)
    block = jnp.where(iota(shape, 0) < MASK_ROWS // 2, lines[0], lines[1])
    packed_ref[0, tiles * channels :, :] = block.astype(BF16)


def chunk_of(ref, channels, k, h):
    return ref[k, h * channels : (h + 1) * channels, :].astype(F32)


def mask_of(ref, channels, k, h):
    lines = ref[k, -MASK_ROWS:, :].astype(F32)
    return lines[h * MASK_ROWS // 2 : h * MASK_ROWS // 2 + 1]


def prepare_kernel(
    rows, tokens, me_ref, proj_ref, gate_ref, out_ref, gain_ref, mid_ref,
    proj_t_ref, gate_t_ref, out_t_ref, gain_t_ref, mid_t_ref, restore_ref, spread_ref,
):
    devices = tokens // rows

    def flipped(weight):
        return weight.astype(F32).T

    def column(line):
        return jnp.broadcast_to(line, (LANES, line.shape[1])).T

    hw = mid_ref.shape[1]
    is_gate = iota((4 * hw, proj_ref.shape[1]), 0) // hw % 2 == 1
    for o in range(2):
        proj = flipped(proj_ref[o])
        proj_t_ref[o] = jnp.where(is_gate, 0.5 * proj, proj).astype(BF16)
        gate_t_ref[o] = (0.5 * flipped(gate_ref[o])).astype(BF16)
        out_t_ref[o] = (0.5 * flipped(out_ref[o])).astype(BF16)
        gain_t_ref[o] = column(gain_ref[o : o + 1, :])
        mid_t_ref[o] = column(mid_ref[o : o + 1, :])
    shape = (LANES, LANES)
    lane = iota(shape, 1)
    source = lane // tokens * tokens + token_of(lane % tokens, rows, tokens)
    restore_ref[...] = one_hot(source == iota(shape, 0))
    group, lane = iota(shape, 0) // tokens, iota(shape, 0) % tokens
    same = group == iota(shape, 1) // tokens
    for i in range(rows):
        spread_ref[i] = one_hot(same & (lane == i * devices + me_ref[0]))


def early_kernel(counts, *refs):
    block_refs, (proj_ref, gain_ref, left_ref, right_ref, normed_ref) = refs[:-5], refs[-5:]
    channels, tiles = normed_ref.shape[2], normed_ref.shape[1]
    place = 0
    for block_ref, count in zip(block_refs, counts):
        for k in range(count):
            normed = [
                column_norm(chunk_of(block_ref, channels, k, h), gain_ref[0]) for h in range(tiles)
            ]
            projected = dot(proj_ref[0], side_by_side(normed))
            for h in range(tiles):
                normed_ref[place, h] = normed[h]
                left, right = factors(tile(projected, h), mask_of(block_ref, channels, k, h))
                left_ref[place, h] = left
                right_ref[place, h] = right
            place += 1


def both_kernel(rows, tokens, sources, early_groups, me_ref, *refs):
    devices = tokens // rows
    block_refs, refs = refs[: len(sources)], refs[len(sources) :]
    weight_refs, refs = refs[:7], refs[7:]
    proj_ref, gate_ref, out_ref, gain_ref, mid_ref, restore_ref, spread_ref = weight_refs
    ahead = {}
    for group in early_groups:
        for n, m in enumerate(group):
            ahead[m] = refs[:3] + (n,)
        refs = refs[3:]
    (
        result_ref, left_s, right_s, normed_s, sum_s, now_s, second_left_s, second_right_s,
    ) = refs
    channels = gate_ref.shape[1]
    hw = mid_ref.shape[1]
    tiles = rows * tokens // LANES
    me = me_ref[0]

    where = {m: (ref, k) for ref, held in zip(block_refs, sources) for k, m in enumerate(held)}
    later = [m for m in range(devices) if m not in ahead]

    def place(m, h, left, right):
        here = pl.ds((me ^ m) * (hw + 1), hw)
        left_s[h, here, :] = left
        right_s[h, here, :] = right

    for m in later:
        ref, k = where[m]
        normed = [column_norm(chunk_of(ref, channels, k, h), gain_ref[0]) for h in range(tiles)]
        projected = dot(proj_ref[0], side_by_side(normed))
        for h in range(tiles):
            normed_s[later.index(m), h] = normed[h]
            place(m, h, *factors(tile(projected, h), mask_of(ref, channels, k, h)))
    for m, (left_ref, right_ref, _, n) in ahead.items():
        for h in range(tiles):
            place(m, h, left_ref[n, h], right_ref[n, h])

    def normed_of(m, h):
        if m in ahead:
            return ahead[m][2][ahead[m][3], h]
        return normed_s[later.index(m), h]

    in_low = one_hot(iota((devices, LANES), 1) < tokens)
    in_high = one_hot(iota((devices, LANES), 1) >= tokens)

    def channel_sum(c):
        here = pl.ds(c, devices, stride=hw + 1)
        left = jnp.concatenate([left_s[h, here, :] for h in range(tiles)], axis=0)
        halves = [[], []]
        for h in range(tiles):
            right = right_s[h, here, :]
            turned = pltpu.roll(right, tokens, 1).astype(BF16)
            right = right.astype(BF16)
            halves[0] += [right * in_low, turned * in_low]
            halves[1] += [turned * in_high, right * in_high]
        against = jnp.concatenate(halves[0] + halves[1], axis=0)
        here = pl.ds(c * (tiles * devices + 1), tiles * devices)
        sum_s[here, :] = dot_nt(left.astype(BF16), against)

    for c in range(hw):
        channel_sum(c)

    for m in range(devices):
        ref, k = where[m]
        hidden, first = [], []
        for h in range(tiles):
            summed = sum_s[pl.ds(h * devices + (me ^ m), hw, stride=tiles * devices + 1), :]
            hidden.append(column_norm(summed, mid_ref[0]))
            first.append(normed_of(m, h))
        update = dot(out_ref[0], side_by_side(hidden))
        logits = dot(gate_ref[0], side_by_side(first))
        normed = []
        for h in range(tiles):
            gated = twice_sigmoid(tile(logits, h)) * tile(update, h)
            now = (chunk_of(ref, channels, k, h) + gated).astype(BF16)
            normed.append(column_norm(now.astype(F32), gain_ref[1]))
            if m == 0:
                now_s[h] = now
                now_s[tiles + h] = normed[h]
        projected = dot(proj_ref[1], side_by_side(normed))
        for h in range(tiles):
            left, right = factors(tile(projected, h), mask_of(ref, channels, k, h))
            here = pl.ds((m * tiles + h) * hw, hw)
            second_left_s[here, :] = left.astype(BF16)
            second_right_s[here, :] = right.astype(BF16)

    depth = 2 * hw
    sums = []
    for i in range(0, rows, 2):
        pair = side_by_side([spread_ref[i], spread_ref[i + 1]])
        totals = [jnp.zeros((hw, LANES), F32)] * 2
        for n in range(devices * tiles // 2):
            here = pl.ds(n * depth, depth)
            spread = dot(second_left_s[here, :], pair)
            right = second_right_s[here, :].astype(F32)
            for o in range(2):
                terms = tile(spread, o) * right
                totals[o] = totals[o] + (terms[:hw] + terms[hw:])
        sums += [total + pltpu.roll(total, tokens, 1) for total in totals]
    low = iota((hw, LANES), 1) < tokens
    for h in range(tiles):
        summed = jnp.where(low, sums[2 * h], sums[2 * h + 1])
        update = dot(out_ref[1], column_norm(summed, mid_ref[1]))
        gating = twice_sigmoid(dot(gate_ref[1], now_s[tiles + h]))
        final = (now_s[h].astype(F32) + gating * update).astype(BF16)
        result_ref[h * LANES : (h + 1) * LANES, :] = dot_nt(restore_ref[...], final).astype(BF16)


def exchange(block, partner_bits, devices):
    pairs = [(d, d ^ partner_bits) for d in range(devices)]
    return lax.ppermute(block, "row", pairs)


def small_plan(pair, mask, proj, gate, out, gain, mid):
    rows, tokens, channels = pair.shape
    devices, size, hw = tokens // rows, rows * tokens, out.shape[1]
    tiles = size // LANES
    packed = pl.pallas_call(
        functools.partial(pack_kernel, rows, tokens),
        out_shape=VMEM((1, tiles * channels + MASK_ROWS, LANES), BF16),
        out_specs=IN_VMEM,
        name="pack",
    )(pair, mask)
    me = lax.axis_index("row").reshape(1).astype(jnp.int32)
    weights = pl.pallas_call(
        functools.partial(prepare_kernel, rows, tokens),
        in_specs=[IN_SMEM] + [pl.BlockSpec()] * 5,
        out_shape=(
            VMEM((2, 4 * hw, channels), BF16),
            VMEM((2, channels, channels), BF16),
            VMEM((2, channels, hw), BF16),
            VMEM((2, channels, LANES), F32),
            VMEM((2, hw, LANES), F32),
            VMEM((LANES, LANES), BF16),
            VMEM((rows, LANES, LANES), BF16),
        ),
        out_specs=(IN_VMEM,) * 7,
        name="prepare",
    )(me, proj, gate, out, gain, mid)

    def swapped(group):
        return exchange(jnp.concatenate([held[m] for m in group]), 1, devices)

    def project_early(blocks):
        count = sum(block.shape[0] for block in blocks)
        return pl.pallas_call(
            functools.partial(early_kernel, [block.shape[0] for block in blocks]),
            in_specs=[IN_VMEM] * (len(blocks) + 2),
            out_shape=(
                VMEM((count, tiles, hw, LANES), F32),
                VMEM((count, tiles, hw, LANES), F32),
                VMEM((count, tiles, channels, LANES), BF16),
            ),
            out_specs=(IN_VMEM,) * 3,
            compiler_params=SMALL,
            name="early",
        )(*blocks, weights[0], weights[3])

    held = {0: packed}
    for m in (12, 8, 4, 2):
        held[m] = exchange(packed, m, devices)
    held[12], weights = lax.optimization_barrier((held[12], weights))
    held[14] = exchange(held[12], 2, devices)
    held[6] = exchange(held[2], 4, devices)
    held[10] = exchange(held[8], 2, devices)
    first = (0, 4, 8, 2, 12)
    last = (14, 6, 10)
    swaps = [swapped(first), swapped(last)]
    ahead = project_early([held[m] for m in first + last] + swaps[:1])
    arrays = [held[m] for m in first + last] + swaps
    sources = [(m,) for m in first + last]
    sources += [tuple(m ^ 1 for m in group) for group in (first, last)]
    early_groups = (first + last + sources[-2],)
    result = pl.pallas_call(
        functools.partial(both_kernel, rows, tokens, sources, early_groups),
        out_shape=jax.ShapeDtypeStruct((size, channels), BF16),
        in_specs=[IN_SMEM] + [IN_VMEM] * (len(arrays) + len(weights) + len(ahead)),
        scratch_shapes=[
            pltpu.VMEM((tiles, devices * (hw + 1), LANES), F32),
            pltpu.VMEM((tiles, devices * (hw + 1), LANES), F32),
            pltpu.VMEM((len(last), tiles, channels, LANES), BF16),
            pltpu.VMEM((hw * (devices * tiles + 1), LANES), F32),
            pltpu.VMEM((2 * tiles, channels, LANES), BF16),
            pltpu.VMEM((devices * tiles * hw, LANES), BF16),
            pltpu.VMEM((devices * tiles * hw, LANES), BF16),
        ],
        compiler_params=pltpu.CompilerParams(vmem_limit_bytes=24 * 1024 * 1024),
        name="both",
    )(me, *arrays, *weights, *ahead)
    return result.reshape(pair.shape)


def layer_norm(values, gain, axis):
    average = jnp.mean(values, axis=axis, keepdims=True)
    centred = values - average
    variance = jnp.mean(centred * centred, axis=axis, keepdims=True)
    return centred * lax.rsqrt(variance + EPS) * gain


def wide_factors(normed, mask, proj):
    hw = proj.shape[1] // 4
    projected = jnp.einsum("ijd,de->eij", normed, proj, preferred_element_type=F32)
    left = mask * jax.nn.sigmoid(projected[hw : 2 * hw]) * projected[:hw]
    right = mask * jax.nn.sigmoid(projected[3 * hw :]) * projected[2 * hw : 3 * hw]
    return left.astype(BF16), right.astype(BF16)


def gathered_update(pair, mask, proj, gate, out, gain, mid, orient):
    rows, tokens, _ = pair.shape
    devices = tokens // rows
    floats = pair.astype(F32)
    normed = layer_norm(floats, gain, -1).astype(BF16)
    left, right = wide_factors(normed, mask, proj)
    everywhere = lax.all_gather(right, "row", axis=1, tiled=True)
    if orient == 1:
        c = left.shape[0]
        blocks = left.reshape(c, rows, devices, rows).transpose(2, 1, 3, 0)
        left = lax.all_to_all(blocks, "row", 0, 0, tiled=True)
        left = left.reshape(tokens, rows, c).transpose(2, 0, 1)
    spec = "cik,cjk->cij" if orient == 0 else "cki,ckj->cij"
    summed = jnp.einsum(spec, left, everywhere, preferred_element_type=F32)
    hidden = layer_norm(summed, mid[:, None, None], 0).astype(BF16)
    gating = jax.nn.sigmoid(jnp.einsum("ijd,de->ije", normed, gate, preferred_element_type=F32))
    update = jnp.einsum("cij,cd->ijd", hidden, out, preferred_element_type=F32)
    return (floats + gating * update).astype(BF16)


def shards(pair, pair_mask, proj, gate, out, gain, mid):
    rows, tokens, _ = pair.shape
    if rows == 4 and 2 * tokens == LANES:
        return small_plan(pair, pair_mask, proj, gate, out, gain, mid)
    mask = pair_mask.astype(F32)[None]
    for o in range(2):
        pair = gathered_update(pair, mask, proj[o], gate[o], out[o], gain[o], mid[o], o)
    return pair


def solution(mesh):
    return jax.shard_map(
        shards,
        mesh=mesh,
        in_specs=(P(("groups", "row")), P(("groups", "row")), P(), P(), P(), P(), P()),
        out_specs=P(("groups", "row")),
        check_vma=False,
    )
```

```python
import functools

import jax
import jax.numpy as jnp
from jax import lax
from jax.experimental import pallas as pl
from jax.experimental.pallas import tpu as pltpu
from jax.sharding import PartitionSpec as P

EPS = 1e-05
F32, BF16 = jnp.float32, jnp.bfloat16
LANES = 128
MASK_ROWS = 16
NT = (((1,), (1,)), ((), ()))
VMEM = pltpu.VMEM
IN_VMEM = pl.BlockSpec(memory_space=pltpu.VMEM)
IN_SMEM = pl.BlockSpec(memory_space=pltpu.SMEM)
SMALL = pltpu.CompilerParams(vmem_limit_bytes=8 * 1024 * 1024)


def dot(a, b):
    return jnp.dot(a, b, preferred_element_type=F32)


def dot_nt(a, b):
    return lax.dot_general(a, b, NT, preferred_element_type=F32)


def twice_sigmoid(half):
    return jnp.tanh(half) + 1.0


def iota(shape, axis):
    return lax.broadcasted_iota(jnp.int32, shape, axis)


def one_hot(condition):
    return condition.astype(F32).astype(BF16)


def token_of(t, rows, tokens):
    devices = tokens // rows
    return (t % devices) * rows + t // devices


def column_norm(values, gain):
    average = jnp.mean(values, axis=0, keepdims=True)
    centred = values - average
    variance = jnp.mean(centred * centred, axis=0, keepdims=True)
    return (centred * lax.rsqrt(variance + EPS) * gain).astype(BF16)


def factors(projected, half_mask):
    hw = projected.shape[0] // 4
    left = half_mask * twice_sigmoid(projected[hw : 2 * hw]) * projected[:hw]
    right = half_mask * twice_sigmoid(projected[3 * hw :]) * projected[2 * hw : 3 * hw]
    return left, right


def side_by_side(chunks):
    return jnp.concatenate(chunks, axis=1)


def tile(values, h):
    return values[:, h * LANES : (h + 1) * LANES]


def pack_kernel(rows, tokens, pair_ref, mask_ref, packed_ref):
    channels = pair_ref.shape[-1]
    square = (tokens, tokens)
    by_lane = one_hot(token_of(iota(square, 0), rows, tokens) == iota(square, 1))
    by_token = one_hot(token_of(iota(square, 1), rows, tokens) == iota(square, 0))
    identity = one_hot(iota((channels, channels), 0) == iota((channels, channels), 1))
    masks = 0.5 * dot(one_hot(mask_ref[...] != 0), by_token)
    tiles = rows * tokens // LANES
    for h in range(tiles):
        pair = [dot(by_lane, pair_ref[i]).astype(BF16) for i in (2 * h, 2 * h + 1)]
        chunk = dot_nt(identity, jnp.concatenate(pair, axis=0))
        packed_ref[0, h * channels : (h + 1) * channels, :] = chunk.astype(BF16)
    lines = [
        jnp.concatenate([masks[2 * h : 2 * h + 1], masks[2 * h + 1 : 2 * h + 2]], axis=1)
        for h in range(tiles)
    ]
    shape = (MASK_ROWS, LANES)
    block = jnp.where(iota(shape, 0) < MASK_ROWS // 2, lines[0], lines[1])
    packed_ref[0, tiles * channels :, :] = block.astype(BF16)


def chunk_of(ref, channels, k, h):
    return ref[k, h * channels : (h + 1) * channels, :].astype(F32)


def mask_of(ref, channels, k, h):
    lines = ref[k, -MASK_ROWS:, :].astype(F32)
    return lines[h * MASK_ROWS // 2 : h * MASK_ROWS // 2 + 1]


def prepare_kernel(
    rows, tokens, me_ref, proj_ref, gate_ref, out_ref, gain_ref, mid_ref,
    proj_t_ref, gate_t_ref, out_t_ref, gain_t_ref, mid_t_ref, restore_ref, spread_ref,
):
    devices = tokens // rows

    def flipped(weight):
        return weight.astype(F32).T

    def column(line):
        return jnp.broadcast_to(line, (LANES, line.shape[1])).T

    hw = mid_ref.shape[1]
    is_gate = iota((4 * hw, proj_ref.shape[1]), 0) // hw % 2 == 1
    for o in range(2):
        proj = flipped(proj_ref[o])
        proj_t_ref[o] = jnp.where(is_gate, 0.5 * proj, proj).astype(BF16)
        gate_t_ref[o] = (0.5 * flipped(gate_ref[o])).astype(BF16)
        out_t_ref[o] = (0.5 * flipped(out_ref[o])).astype(BF16)
        gain_t_ref[o] = column(gain_ref[o : o + 1, :])
        mid_t_ref[o] = column(mid_ref[o : o + 1, :])
    shape = (LANES, LANES)
    lane = iota(shape, 1)
    source = lane // tokens * tokens + token_of(lane % tokens, rows, tokens)
    restore_ref[...] = one_hot(source == iota(shape, 0))
    group, lane = iota(shape, 0) // tokens, iota(shape, 0) % tokens
    same = group == iota(shape, 1) // tokens
    for i in range(rows):
        spread_ref[i] = one_hot(same & (lane == i * devices + me_ref[0]))


def place(me, m, h, left_ref, right_ref, left, right):
    hw = left.shape[0]
    here = pl.ds((me ^ m) * (hw + 1), hw)
    left_ref[h, here, :] = left
    right_ref[h, here, :] = right


def early_kernel(held, me_ref, *refs):
    block_refs, (proj_ref, gain_ref, left_ref, right_ref, normed_ref) = refs[:-5], refs[-5:]
    channels, tiles = normed_ref.shape[2], normed_ref.shape[1]
    n = 0
    for block_ref in block_refs:
        for k in range(block_ref.shape[0]):
            normed = [
                column_norm(chunk_of(block_ref, channels, k, h), gain_ref[0]) for h in range(tiles)
            ]
            projected = dot(proj_ref[0], side_by_side(normed))
            for h in range(tiles):
                normed_ref[n, h] = normed[h]
                both = factors(tile(projected, h), mask_of(block_ref, channels, k, h))
                place(me_ref[0], held[n], h, left_ref, right_ref, *both)
            n += 1


def both_kernel(rows, tokens, sources, early, me_ref, *refs):
    devices = tokens // rows
    block_refs, refs = refs[: len(sources)], refs[len(sources) :]
    weight_refs, refs = refs[:7], refs[7:]
    proj_ref, gate_ref, out_ref, gain_ref, mid_ref, restore_ref, spread_ref = weight_refs
    (
        _, _, early_normed_ref, result_ref, left_s, right_s,
        normed_s, sum_s, now_s, second_left_s, second_right_s,
    ) = refs
    channels = gate_ref.shape[1]
    hw = mid_ref.shape[1]
    tiles = rows * tokens // LANES
    me = me_ref[0]

    where = {m: (ref, k) for ref, held in zip(block_refs, sources) for k, m in enumerate(held)}
    later = [m for m in range(devices) if m not in early]
    for m in later:
        ref, k = where[m]
        normed = [column_norm(chunk_of(ref, channels, k, h), gain_ref[0]) for h in range(tiles)]
        projected = dot(proj_ref[0], side_by_side(normed))
        for h in range(tiles):
            normed_s[later.index(m), h] = normed[h]
            both = factors(tile(projected, h), mask_of(ref, channels, k, h))
            place(me, m, h, left_s, right_s, *both)

    def normed_of(m, h):
        if m in early:
            return early_normed_ref[early.index(m), h]
        return normed_s[later.index(m), h]

    in_low = one_hot(iota((devices, LANES), 1) < tokens)
    in_high = one_hot(iota((devices, LANES), 1) >= tokens)

    def channel_sum(c):
        here = pl.ds(c, devices, stride=hw + 1)
        left = jnp.concatenate([left_s[h, here, :] for h in range(tiles)], axis=0)
        halves = [[], []]
        for h in range(tiles):
            right = right_s[h, here, :]
            turned = pltpu.roll(right, tokens, 1).astype(BF16)
            right = right.astype(BF16)
            halves[0] += [right * in_low, turned * in_low]
            halves[1] += [turned * in_high, right * in_high]
        against = jnp.concatenate(halves[0] + halves[1], axis=0)
        here = pl.ds(c * (tiles * devices + 1), tiles * devices)
        sum_s[here, :] = dot_nt(left.astype(BF16), against)

    for c in range(hw):
        channel_sum(c)

    for m in range(devices):
        ref, k = where[m]
        hidden, first = [], []
        for h in range(tiles):
            summed = sum_s[pl.ds(h * devices + (me ^ m), hw, stride=tiles * devices + 1), :]
            hidden.append(column_norm(summed, mid_ref[0]))
            first.append(normed_of(m, h))
        update = dot(out_ref[0], side_by_side(hidden))
        logits = dot(gate_ref[0], side_by_side(first))
        normed = []
        for h in range(tiles):
            gated = twice_sigmoid(tile(logits, h)) * tile(update, h)
            now = (chunk_of(ref, channels, k, h) + gated).astype(BF16)
            normed.append(column_norm(now.astype(F32), gain_ref[1]))
            if m == 0:
                now_s[h] = now
                now_s[tiles + h] = normed[h]
        projected = dot(proj_ref[1], side_by_side(normed))
        for h in range(tiles):
            left, right = factors(tile(projected, h), mask_of(ref, channels, k, h))
            here = pl.ds((m * tiles + h) * hw, hw)
            second_left_s[here, :] = left.astype(BF16)
            second_right_s[here, :] = right.astype(BF16)

    depth = 4 * hw
    sums = []
    for i in range(0, rows, 2):
        pair = side_by_side([spread_ref[i], spread_ref[i + 1]])
        totals = [jnp.zeros((hw, LANES), F32)] * 2
        for n in range(devices * tiles // 4):
            here = pl.ds(n * depth, depth)
            spread = dot(second_left_s[here, :], pair)
            right = second_right_s[here, :].astype(F32)
            for o in range(2):
                terms = tile(spread, o) * right
                totals[o] = totals[o] + sum(terms[k * hw : (k + 1) * hw] for k in range(4))
        sums += [total + pltpu.roll(total, tokens, 1) for total in totals]
    low = iota((hw, LANES), 1) < tokens
    for h in range(tiles):
        summed = jnp.where(low, sums[2 * h], sums[2 * h + 1])
        update = dot(out_ref[1], column_norm(summed, mid_ref[1]))
        gating = twice_sigmoid(dot(gate_ref[1], now_s[tiles + h]))
        final = (now_s[h].astype(F32) + gating * update).astype(BF16)
        result_ref[h * LANES : (h + 1) * LANES, :] = dot_nt(restore_ref[...], final).astype(BF16)


def exchange(block, partner_bits, devices):
    pairs = [(d, d ^ partner_bits) for d in range(devices)]
    return lax.ppermute(block, "row", pairs)


def small_plan(pair, mask, proj, gate, out, gain, mid):
    rows, tokens, channels = pair.shape
    devices, size, hw = tokens // rows, rows * tokens, out.shape[1]
    tiles = size // LANES
    packed = pl.pallas_call(
        functools.partial(pack_kernel, rows, tokens),
        out_shape=VMEM((1, tiles * channels + MASK_ROWS, LANES), BF16),
        out_specs=IN_VMEM,
        name="pack",
    )(pair, mask)
    me = lax.axis_index("row").reshape(1).astype(jnp.int32)
    weights = pl.pallas_call(
        functools.partial(prepare_kernel, rows, tokens),
        in_specs=[IN_SMEM] + [pl.BlockSpec()] * 5,
        out_shape=(
            VMEM((2, 4 * hw, channels), BF16),
            VMEM((2, channels, channels), BF16),
            VMEM((2, channels, hw), BF16),
            VMEM((2, channels, LANES), F32),
            VMEM((2, hw, LANES), F32),
            VMEM((LANES, LANES), BF16),
            VMEM((rows, LANES, LANES), BF16),
        ),
        out_specs=(IN_VMEM,) * 7,
        name="prepare",
    )(me, proj, gate, out, gain, mid)

    def swapped(group):
        return exchange(jnp.concatenate([held[m] for m in group]), 1, devices)

    factor = VMEM((tiles, devices * (hw + 1), LANES), F32)

    def project_early(blocks, held_there):
        normed = VMEM((len(held_there), tiles, channels, LANES), BF16)
        return pl.pallas_call(
            functools.partial(early_kernel, held_there),
            in_specs=[IN_SMEM] + [IN_VMEM] * (len(blocks) + 2),
            out_shape=(factor, factor, normed),
            out_specs=(IN_VMEM,) * 3,
            compiler_params=SMALL,
            name="early",
        )(me, *blocks, weights[0], weights[3])

    held = {0: packed}
    for m in (12, 8, 4, 2):
        held[m] = exchange(packed, m, devices)
    held[12], weights = lax.optimization_barrier((held[12], weights))
    held[14] = exchange(held[12], 2, devices)
    held[6] = exchange(held[2], 4, devices)
    held[10] = exchange(held[8], 2, devices)
    first = (0, 4, 8, 2, 12)
    last = (14, 6, 10)
    swaps = [swapped(first), swapped(last)]
    early = first + last + tuple(m ^ 1 for m in first)
    ahead = project_early([held[m] for m in first + last] + swaps[:1], early)
    arrays = [held[m] for m in first + last] + swaps
    sources = [(m,) for m in first + last]
    sources += [tuple(m ^ 1 for m in group) for group in (first, last)]
    result, _, _ = pl.pallas_call(
        functools.partial(both_kernel, rows, tokens, sources, early),
        out_shape=(jax.ShapeDtypeStruct((size, channels), BF16), factor, factor),
        in_specs=[IN_SMEM] + [IN_VMEM] * (len(arrays) + len(weights) + len(ahead)),
        out_specs=(pl.BlockSpec(), IN_VMEM, IN_VMEM),
        input_output_aliases={1 + len(arrays) + len(weights) + n: 1 + n for n in range(2)},
        scratch_shapes=[
            pltpu.VMEM((len(last), tiles, channels, LANES), BF16),
            pltpu.VMEM((hw * (devices * tiles + 1), LANES), F32),
            pltpu.VMEM((2 * tiles, channels, LANES), BF16),
            pltpu.VMEM((devices * tiles * hw, LANES), BF16),
            pltpu.VMEM((devices * tiles * hw, LANES), BF16),
        ],
        compiler_params=pltpu.CompilerParams(vmem_limit_bytes=24 * 1024 * 1024),
        name="both",
    )(me, *arrays, *weights, *ahead)
    return result.reshape(pair.shape)


def layer_norm(values, gain, axis):
    average = jnp.mean(values, axis=axis, keepdims=True)
    centred = values - average
    variance = jnp.mean(centred * centred, axis=axis, keepdims=True)
    return centred * lax.rsqrt(variance + EPS) * gain


def wide_factors(normed, mask, proj):
    hw = proj.shape[1] // 4
    projected = jnp.einsum("ijd,de->eij", normed, proj, preferred_element_type=F32)
    left = mask * jax.nn.sigmoid(projected[hw : 2 * hw]) * projected[:hw]
    right = mask * jax.nn.sigmoid(projected[3 * hw :]) * projected[2 * hw : 3 * hw]
    return left.astype(BF16), right.astype(BF16)


def gathered_update(pair, mask, proj, gate, out, gain, mid, orient):
    rows, tokens, _ = pair.shape
    devices = tokens // rows
    floats = pair.astype(F32)
    normed = layer_norm(floats, gain, -1).astype(BF16)
    left, right = wide_factors(normed, mask, proj)
    everywhere = lax.all_gather(right, "row", axis=1, tiled=True)
    if orient == 1:
        c = left.shape[0]
        blocks = left.reshape(c, rows, devices, rows).transpose(2, 1, 3, 0)
        left = lax.all_to_all(blocks, "row", 0, 0, tiled=True)
        left = left.reshape(tokens, rows, c).transpose(2, 0, 1)
    spec = "cik,cjk->cij" if orient == 0 else "cki,ckj->cij"
    summed = jnp.einsum(spec, left, everywhere, preferred_element_type=F32)
    hidden = layer_norm(summed, mid[:, None, None], 0).astype(BF16)
    gating = jax.nn.sigmoid(jnp.einsum("ijd,de->ije", normed, gate, preferred_element_type=F32))
    update = jnp.einsum("cij,cd->ijd", hidden, out, preferred_element_type=F32)
    return (floats + gating * update).astype(BF16)


def shards(pair, pair_mask, proj, gate, out, gain, mid):
    rows, tokens, _ = pair.shape
    if rows == 4 and 2 * tokens == LANES:
        return small_plan(pair, pair_mask, proj, gate, out, gain, mid)
    mask = pair_mask.astype(F32)[None]
    for o in range(2):
        pair = gathered_update(pair, mask, proj[o], gate[o], out[o], gain[o], mid[o], o)
    return pair


def solution(mesh):
    return jax.shard_map(
        shards,
        mesh=mesh,
        in_specs=(P(("groups", "row")), P(("groups", "row")), P(), P(), P(), P(), P()),
        out_specs=P(("groups", "row")),
        check_vma=False,
    )
```
